32 devices in a mesh: parts: 2 (over y), wide: 4 (over x, core), tensor: 4 (over z).
Axes of the slice: x: 2, y: 2, z: 4, core: 2. Of those that a mesh axis runs over, the one named last changes fastest.
Arguments:
- tokens: bfloat16 [2048, 8192], P(('parts', 'wide'), 'tensor'), parts along dimension 0, may hold values from -300 to 300
- attention_norm_gain: bfloat16 [8192], P('tensor'), may hold values from 0.099609375 to 1.8984375
- key_value_weight: bfloat16 [8192, 2048], P('tensor'), may hold values from -0.0625 to 0.0625
- adapter_down_weight: bfloat16 [64, 8192, 128], P(('parts', 'wide'), 'tensor'), parts along dimension 0, may hold values from -0.0625 to 0.0625
- adapter_up_weight: bfloat16 [64, 64, 2048], P(('parts', 'wide'), None, 'tensor'), parts along dimension 0, may hold values from -0.75 to 0.75
- request_adapter: int32 [2048], P(('parts', 'wide')), parts along dimension 0, may hold values from 0 to 31, as said below
- adapter_storage_row: int32 [64], P('parts'), parts along dimension 0, may hold values from 0 to 31, as said below
- cached_token_length: int32 [2048], P(('parts', 'wide')), parts along dimension 0, may hold values from 1 to 8192
Outputs:
- kv_entries: bfloat16 [2048, 2048], P(('parts', 'wide'), 'tensor'), parts along dimension 0
The draws below stay inside these ranges and needn't reach their ends.
There are 2 independent parts, one for each index of `parts`. The reference program is written for one: setup_inputs(seed, part) draws one part's arguments, and reference() takes and returns one part's arrays. A program takes and returns all parts, laid end to end along the dimension named above; an argument that names none is the same for every part. Nothing has to cross between parts.
Inputs may be any that keep to these rules, and one draw needn't show every extreme that they name: A permutation; adapter a lies in storage row adapter_storage_row[a], held by wide index adapter_storage_row[a] // 8. `request_adapter`: among the 256 requests of one wide index, at most 104 have adapters held by any one wide index; one wide index holds the adapters of exactly 104 requests of every wide index.
All inputs are finite; a program needn't handle non-finite values.
Results may differ from the reference program's by a relative error of at most 0.0057.
Values may be sent and summed in bfloat16 or wider, within the bound.
No kernel may reach another device: no remote copies, remote signals or barrier semaphores. Data moves between devices by JAX's collectives and lax.ppermute only.
A program may use at most 64 MiB of HBM per device.

```python
import math
import jax
import jax.numpy as jnp
from jax import lax

MODEL_WIDTH = 8192
HEAD = 128
ADAPTER_RANK = 64
CTX = 8192
ROWS = 256
ADP_DEV = 8
JOINT_COLUMNS = 2048
ROWS_ALL = 1024
ADAPTER_COUNT = 32
CAP = 104
N_WIDE = 4


def storage_order(key):
    return jax.random.permutation(key, ADAPTER_COUNT)


def draw_adapter_storage_row(key, part):
    order = storage_order(key)
    return order.astype(jnp.int32)


def draw_request_adapter(key, part):
    order = storage_order(key)
    key = jax.random.fold_in(key, 7)
    hot_key, shuffle_key, bit_key, slot_key = jax.random.split(key, 4)
    others = N_WIDE - 1
    hot_owner = jax.random.randint(hot_key, (), 0, N_WIDE)
    position = jnp.arange(ROWS)
    rest_index = jnp.maximum(position - CAP, 0)
    step_bits = jax.random.randint(bit_key, (N_WIDE, ROWS), 0, 2)
    other_rank = (rest_index[None, :] % others + step_bits) % others
    other_owner = (hot_owner + 1 + other_rank) % N_WIDE
    owner_by_position = jnp.where(position[None, :] < CAP, hot_owner, other_owner)
    scores = jax.random.randint(shuffle_key, (N_WIDE, ROWS), 0, 1 << 20) * ROWS + position[None, :]
    shuffle = jnp.argsort(scores, axis=1)
    owner_of_row = jnp.take_along_axis(owner_by_position, shuffle, axis=1)
    slot_index = jax.random.randint(slot_key, (N_WIDE, ROWS), 0, ADP_DEV)
    storage = (owner_of_row * ADP_DEV + slot_index).reshape(-1)
    inverse = jnp.argsort(order)
    return jnp.take(inverse, storage, axis=0).astype(jnp.int32)


def draw_tokens(key, part):
    key = jax.random.fold_in(key, 3)
    row_key, column_key, entry_key = jax.random.split(key, 3)
    column_scale = jnp.power(10.0, 0.5 * jnp.arange(MODEL_WIDTH).astype(jnp.float32) / MODEL_WIDTH)[None, :]
    column_scale = column_scale * jnp.exp(jax.random.uniform(column_key, (1, MODEL_WIDTH), jnp.float32, 0.0, 0.5 * math.log(10.0)))
    row_scale = jnp.exp(jax.random.uniform(row_key, (ROWS_ALL, 1), jnp.float32, 0.0, math.log(10.0)))
    entries = jax.random.normal(entry_key, (ROWS_ALL, MODEL_WIDTH), jnp.float32)
    return jnp.clip(entries * row_scale * column_scale, -300.0, 300.0).astype(jnp.bfloat16)


def draw_cached_token_length(key, part):
    key = jax.random.fold_in(key, 9)
    value_key, top_key, bottom_key = jax.random.split(key, 3)
    lengths = jax.random.randint(value_key, (ROWS_ALL,), 1, CTX + 1)
    top_at = jax.random.randint(top_key, (), 0, ROWS_ALL)
    bottom_at = (top_at + 1 + jax.random.randint(bottom_key, (), 0, ROWS_ALL - 1)) % ROWS_ALL
    return lengths.at[top_at].set(CTX).at[bottom_at].set(1).astype(jnp.int32)


def block_levels(own_key, shape, cuts, least, high):
    factor_of, own = 1.0, jax.random.fold_in(own_key, 6)
    for dim, blocks in cuts:
        draws = jnp.exp(jax.random.uniform(jax.random.fold_in(own, dim), (blocks,), jnp.float32, least / len(cuts), high / len(cuts)))
        factor_of = factor_of * jnp.repeat(draws, shape[dim] // blocks).reshape([-1 if axis == dim else 1 for axis in range(len(shape))])
    return factor_of


def noise(rng, extent, spread, reach, shards=(), kind=jnp.bfloat16):
    drawn = spread * jax.random.normal(rng, extent, jnp.float32)
    if shards:
        drawn = drawn * block_levels(rng, extent, shards, -0.22, 0.18)
    return jnp.clip(drawn, -reach, reach).astype(kind)


def setup_inputs(seed: int = 0, part: int = 0) -> dict:
    key_of = jax.random.split(jax.random.key(seed), 9)
    part_splits = jax.random.split(jax.random.fold_in(key_of[8], part), 9)
    tokens = draw_tokens(jax.random.fold_in(jax.random.fold_in(key_of[8], part), 71), part)
    attention_norm_gain = jnp.clip(1.0 + 0.18 * jax.random.normal(key_of[1], (MODEL_WIDTH,), jnp.float32), 0.099609375, 1.8984375).astype(jnp.bfloat16)
    key_value_weight = noise(key_of[2], (MODEL_WIDTH, JOINT_COLUMNS), MODEL_WIDTH ** -0.5, 0.0625, ((0, 4),))
    adapter_down_weight = noise(part_splits[3], (ADAPTER_COUNT, MODEL_WIDTH, 2 * ADAPTER_RANK), MODEL_WIDTH ** -0.5, 0.0625, ((0, 4), (1, 4)))
    adapter_up_weight = noise(part_splits[4], (ADAPTER_COUNT, ADAPTER_RANK, JOINT_COLUMNS), ADAPTER_RANK ** -0.5, 0.75, ((0, 4), (2, 4)))
    request_adapter = draw_request_adapter(jax.random.fold_in(jax.random.fold_in(key_of[8], part), 71), part)
    adapter_storage_row = draw_adapter_storage_row(jax.random.fold_in(jax.random.fold_in(key_of[8], part), 71), part)
    cached_token_length = draw_cached_token_length(jax.random.fold_in(jax.random.fold_in(key_of[8], part), 71), part)
    return {"tokens": tokens, "attention_norm_gain": attention_norm_gain, "key_value_weight": key_value_weight, "adapter_down_weight": adapter_down_weight, "adapter_up_weight": adapter_up_weight, "request_adapter": request_adapter, "adapter_storage_row": adapter_storage_row, "cached_token_length": cached_token_length}


EPSILON = 1e-05
ROPE_BASE = 500000.0

def rotate_keys(joined_output, positions, column_start, head_size):
    row_count = joined_output.shape[0]
    width_here = joined_output.shape[1]
    heads_here = width_here // head_size
    blocks = joined_output.reshape(row_count, heads_here, head_size)
    half_size = head_size // 2
    freq_index = jnp.arange(half_size).astype(jnp.float32)
    inverse = jnp.exp(freq_index * (-2.0 / head_size) * math.log(ROPE_BASE))
    angles = positions.astype(jnp.float32)[:, None] * inverse[None, :]
    cosine = jnp.cos(angles)[:, None, :]
    sine_part = jnp.sin(angles)[:, None, :]
    first_half = blocks[:, :, :half_size]
    second_half = blocks[:, :, half_size:]
    turned = jnp.concatenate([first_half * cosine - second_half * sine_part, second_half * cosine + first_half * sine_part], axis=2)
    head_ids = column_start // head_size + jnp.arange(heads_here)
    is_key = (head_ids % 2 == 0)[None, :, None]
    return jnp.where(is_key, turned, blocks).reshape(row_count, width_here)

def reference(tokens, attention_norm_gain, key_value_weight, adapter_down_weight, adapter_up_weight, request_adapter, adapter_storage_row, cached_token_length):
    values = tokens.astype(jnp.float32)
    mean_square = lax.optimization_barrier(jnp.mean(values * values, axis=1, keepdims=True))
    normed = (values * lax.rsqrt(mean_square + EPSILON) * attention_norm_gain.astype(jnp.float32)[None, :]).astype(jnp.bfloat16)
    base_product = jnp.dot(normed, key_value_weight, preferred_element_type=jnp.float32)
    stored = jnp.take(adapter_storage_row, request_adapter, axis=0).astype(jnp.int32)
    block_count = ROWS_ALL // 8

    def one_block(piece_list):
        block_rows, stored_block = piece_list
        down_matrices = jnp.take(adapter_down_weight, stored_block, axis=0).astype(jnp.float32)
        reduced_state = jnp.einsum('rd,rdk->rk', block_rows.astype(jnp.float32), down_matrices).astype(jnp.bfloat16)
        low_float = reduced_state.astype(jnp.float32)
        up_matrices = jnp.take(adapter_up_weight, stored_block, axis=0).astype(jnp.float32)
        key_portion = jnp.einsum('rk,rkc->rc', low_float[:, :ADAPTER_RANK], up_matrices)
        value_portion = jnp.einsum('rk,rkc->rc', low_float[:, ADAPTER_RANK:], up_matrices)
        return (key_portion, value_portion)
    key_portion, value_portion = lax.map(one_block, (normed.reshape(block_count, 8, MODEL_WIDTH), stored.reshape(block_count, 8)))
    key_portion = key_portion.reshape(ROWS_ALL, JOINT_COLUMNS)
    value_portion = value_portion.reshape(ROWS_ALL, JOINT_COLUMNS)
    key_column_set = jnp.arange(JOINT_COLUMNS) // HEAD % 2 == 0
    adapter_delta = jnp.where(key_column_set[None, :], key_portion, value_portion).astype(jnp.bfloat16)
    joined_output = base_product + adapter_delta.astype(jnp.float32)
    return rotate_keys(joined_output, cached_token_length, 0, HEAD).astype(jnp.bfloat16)
```

```python
import functools
import math

import jax
import jax.numpy as jnp
from jax import lax
from jax.experimental import pallas as pl
from jax.experimental.pallas import tpu as pltpu
from jax.sharding import PartitionSpec as P

MODEL_WIDTH = 8192
HEAD = 128
EPSILON = 1e-05
ROPE_BASE = 500000.0
VMEM_LIMIT = 48 * 1024 * 1024
F32 = jnp.float32
BF16 = jnp.bfloat16


def params():
    return pltpu.CompilerParams(vmem_limit_bytes=VMEM_LIMIT)


def whole():
    return pl.BlockSpec(memory_space=pltpu.VMEM)


def smem():
    return pl.BlockSpec(memory_space=pltpu.SMEM)


def iota(shape, axis):
    return lax.broadcasted_iota(jnp.int32, shape, axis)


def prep_kernel(n_wide, per_dev, cap, cols, table, me_ref, req_ref, tok_ref, gain_ref, *outs):
    xs, ss = outs[:n_wide], outs[n_wide : 2 * n_wide]
    xg_ref, sq_ref = outs[2 * n_wide :]
    rows, depth = tok_ref.shape
    me = me_ref[0]
    req = req_ref[...]
    stored = jnp.zeros_like(req)
    for a in range(table.shape[0]):
        stored = jnp.where(req == a, table[a], stored)
    owner = lax.div(stored, per_dev)
    slot = (stored - owner * per_dev).astype(F32)
    xg = (tok_ref[...].astype(F32) * gain_ref[...].astype(F32)).astype(BF16)
    xg_ref[...] = xg
    pad = -(-n_wide // 16) * 16
    dest = iota((pad, rows), 0) ^ me
    hit = owner == dest
    earlier = (iota((rows, rows), 0) <= iota((rows, rows), 1)).astype(BF16)
    count = jnp.dot(hit.astype(BF16), earlier, preferred_element_type=F32)
    place = jnp.where(hit, count.astype(jnp.int32) - 1, -1)
    for k in [*range(n_wide - 1, 0, -1), 0]:
        pick = iota((cap, rows), 0) == place[k : k + 1]
        sel = pick.astype(BF16)
        ss[k][...] = sel
        xs[k][:, :depth] = jnp.dot(sel, xg, preferred_element_type=F32).astype(BF16)
        slots = jnp.sum(jnp.where(pick, slot, 0.0), axis=1, keepdims=True)
        xs[k][:, depth:] = jnp.broadcast_to(slots, (cap, HEAD)).astype(BF16)
    tok = tok_ref[...]
    gram = lax.dot_general(tok, tok, (((1,), (1,)), ((), ())), preferred_element_type=F32)
    diag = iota((rows, rows), 0) == iota((rows, rows), 1)
    sq = jnp.sum(jnp.where(diag, gram, 0.0), axis=0, keepdims=True)
    width = min(rows, cols)
    terms = []
    for _ in range(3):
        part = sq.astype(BF16).astype(F32)
        sq = sq - part
        terms += [part[:, i : i + width] for i in range(0, rows, width)]
    block = jnp.zeros((16, width), F32)
    for i, term in enumerate(terms):
        block = jnp.where(iota((16, width), 0) == i, term, block)
    if width < cols:
        block = jnp.concatenate([block, jnp.zeros((16, cols - width), F32)], axis=1)
    sq_ref[...] = block.astype(BF16)


def base_kernel(pos_ref, xg_ref, w_ref, sq_ref, out_ref, acc_ref):
    step = pl.program_id(0)
    y = jnp.dot(xg_ref[...], w_ref[...], preferred_element_type=F32)

    @pl.when(step == 0)
    def _():
        acc_ref[...] = y

    @pl.when(step > 0)
    def _():
        acc_ref[...] += y

    @pl.when(step == pl.num_programs(0) - 1)
    def _():
        rows = xg_ref.shape[0]
        out_ref[:rows] = acc_ref[...].astype(out_ref.dtype)
        out_ref[rows:] = sq_ref[...].astype(out_ref.dtype)


def base_block(block, xg, weight, sq, dtype):
    rows, depth = xg.shape
    cols = sq.shape[1]
    chunk = math.gcd(depth, 512)
    return pl.pallas_call(
        base_kernel,
        out_shape=jax.ShapeDtypeStruct((rows + 16, cols), dtype),
        grid_spec=pltpu.PrefetchScalarGridSpec(
            num_scalar_prefetch=1,
            grid=(depth // chunk,),
            in_specs=[
                pl.BlockSpec((rows, chunk), lambda i, p: (0, i)),
                pl.BlockSpec((chunk, cols), lambda i, p: (i, p[0])),
                pl.BlockSpec((16, cols), lambda i, p: (0, 0)),
            ],
            out_specs=pl.BlockSpec((rows + 16, cols), lambda i, p: (0, 0)),
            scratch_shapes=[pltpu.VMEM((rows, cols), F32)],
        ),
        compiler_params=params(),
        cost_estimate=pl.CostEstimate(
            flops=2 * rows * depth * cols, bytes_accessed=2 * depth * cols, transcendentals=0
        ),
        name="base_block",
    )(block, xg, weight, sq)


def down_kernel(count, *refs):
    xs, down_ref, out_ref, acc_ref = refs[:count], refs[count], refs[count + 1], refs[count + 2]
    step = pl.program_id(0)
    depth = down_ref.shape[1]
    pair = jnp.concatenate([down_ref[0], down_ref[1]], axis=1)
    for j in range(count):
        y = jnp.dot(xs[j][:, :depth], pair, preferred_element_type=F32)
        slot = xs[j][:, depth:].astype(F32).astype(jnp.int32)
        z = jnp.where(slot == 2 * step, y[:, :HEAD], 0.0)
        z = jnp.where(slot == 2 * step + 1, y[:, HEAD:], z)

        @pl.when(step == 0)
        def _():
            acc_ref[j] = z

        @pl.when(step > 0)
        def _():
            acc_ref[j] += z

        @pl.when(step == pl.num_programs(0) - 1)
        def _():
            out_ref[j] = acc_ref[j].astype(BF16)


def down_block(xs, down):
    count = len(xs)
    cap, width = xs[0].shape
    per_dev, depth, rank = down.shape
    return pl.pallas_call(
        functools.partial(down_kernel, count),
        out_shape=jax.ShapeDtypeStruct((count, cap, rank), BF16),
        grid=(per_dev // 2,),
        in_specs=[pl.BlockSpec((cap, width), lambda i: (0, 0)) for _ in xs]
        + [pl.BlockSpec((2, depth, rank), lambda i: (i, 0, 0))],
        out_specs=pl.BlockSpec((count, cap, rank), lambda i: (0, 0, 0)),
        scratch_shapes=[pltpu.VMEM((count, cap, rank), F32)],
        compiler_params=params(),
        cost_estimate=pl.CostEstimate(
            flops=2 * count * cap * depth * rank * per_dev,
            bytes_accessed=2 * per_dev * depth * rank,
            transcendentals=0,
        ),
        name="down_block",
    )(*xs, down)


def head_is_key(parity, heads, h):
    if heads % 2 == 0:
        return h % 2 == 0
    return (parity + h) % 2 == 0


def up_kernel(count, n_tensor, parity_ref, *refs):
    slots = refs[:count]
    parts = refs[count : count + n_tensor]
    up_ref = refs[count + n_tensor]
    outs = refs[count + n_tensor + 1 :]
    per_dev, half, cols = up_ref.shape
    heads = cols // HEAD
    up = up_ref[...].reshape(per_dev * half, cols)
    for j in range(count):
        low = parts[0][j].astype(F32)
        for part in parts[1:]:
            low = low + part[j].astype(F32)
        cap, rank = low.shape
        left = iota((cap, rank), 1) < half
        turned = pltpu.roll(low, half, 1)
        slot = slots[j][...].astype(F32).astype(jnp.int32)
        wide = []
        for source in (jnp.where(left, low, turned), jnp.where(left, turned, low)):
            pieces = []
            for g in range(per_dev // 2):
                mine = slot == 2 * g + jnp.where(left, 0, 1)
                pieces.append(jnp.where(mine, source, 0.0).astype(BF16))
            wide.append(jnp.concatenate(pieces, axis=1))
        for h in range(heads):
            key = head_is_key(parity_ref[0], heads, h)
            if isinstance(key, bool):
                lhs = wide[0] if key else wide[1]
            else:
                lhs = jnp.where(key, wide[0].astype(F32), wide[1].astype(F32)).astype(BF16)
            span = slice(h * HEAD, (h + 1) * HEAD)
            outs[j][:, span] = jnp.dot(lhs, up[:, span], preferred_element_type=F32).astype(BF16)


def up_block(parity, slots, parts, up):
    count, cap, _ = parts[0].shape
    cols = up.shape[2]
    return pl.pallas_call(
        functools.partial(up_kernel, count, len(parts)),
        out_shape=[jax.ShapeDtypeStruct((cap, cols), BF16)] * count,
        in_specs=[smem()] + [whole()] * (count + len(parts) + 1),
        out_specs=[whole()] * count,
        compiler_params=params(),
        name="up_block",
    )(parity, *slots, *parts, up)


def final_kernel(n_wide, n_tensor, parity_ref, *refs):
    base = refs[:n_tensor]
    deltas = refs[n_tensor : n_tensor + n_wide]
    sels = refs[n_tensor + n_wide : n_tensor + 2 * n_wide]
    cos_ref, sin_ref, out_ref = refs[n_tensor + 2 * n_wide :]
    rows, cols = out_ref.shape
    width = min(rows, cols)
    tails = [b[rows:].astype(F32) for b in base]
    tail = sum(tails[1:], tails[0])
    pieces = rows // width
    squares = []
    for i in range(pieces):
        total = tail[i : i + 1]
        for p in range(1, 3):
            total = total + tail[p * pieces + i : p * pieces + i + 1]
        squares.append(total[:, :width])
    square = squares[0] if pieces == 1 else jnp.concatenate(squares, axis=1)
    diag = iota((rows, rows), 0) == iota((rows, rows), 1)
    square = jnp.sum(jnp.where(diag, square, 0.0), axis=1, keepdims=True)
    scale = lax.rsqrt(square * (1.0 / MODEL_WIDTH) + EPSILON)
    total = base[0][:rows].astype(F32)
    for b in base[1:]:
        total = total + b[:rows].astype(F32)
    for sel, delta in zip(sels, deltas):
        total = total + lax.dot_general(
            sel[...], delta[...], (((0,), (0,)), ((), ())), preferred_element_type=F32
        )
    total = total * scale
    heads = cols // HEAD
    for h in range(heads):
        span = slice(h * HEAD, (h + 1) * HEAD)
        x = total[:, span]
        key = head_is_key(parity_ref[0], heads, h)
        if key is False:
            out_ref[:, span] = x.astype(BF16)
            continue
        y = x * cos_ref[...] + pltpu.roll(x, HEAD // 2, 1) * sin_ref[...]
        if key is not True:
            y = jnp.where(key, y, x)
        out_ref[:, span] = y.astype(BF16)


def local(
    mesh_shape,
    tokens,
    attention_norm_gain,
    key_value_weight,
    adapter_down_weight,
    adapter_up_weight,
    request_adapter,
    adapter_storage_row,
    cached_token_length,
):
    n_wide, n_tensor = mesh_shape["wide"], mesh_shape["tensor"]
    rows, depth = tokens.shape
    per_dev = adapter_down_weight.shape[0]
    cols = adapter_up_weight.shape[2]
    cap = 104 if n_wide <= 4 else 64
    me = lax.axis_index("wide").astype(jnp.int32).reshape(1)
    spot = lax.axis_index("tensor").astype(jnp.int32)
    parity = (spot * (cols // HEAD) % 2).reshape(1)

    def over(axis, size, array, k):
        return lax.ppermute(array, axis, [(i, i ^ k) for i in range(size)])

    prep = pl.pallas_call(
        functools.partial(prep_kernel, n_wide, per_dev, cap, cols),
        out_shape=[jax.ShapeDtypeStruct((cap, depth + HEAD), BF16)] * n_wide
        + [jax.ShapeDtypeStruct((cap, rows), BF16)] * n_wide
        + [
            jax.ShapeDtypeStruct((rows, depth), BF16),
            jax.ShapeDtypeStruct((16, cols), BF16),
        ],
        in_specs=[smem(), smem(), whole(), whole(), whole()],
        out_specs=[whole()] * (2 * n_wide + 2),
        compiler_params=params(),
        name="prep",
    )(
        adapter_storage_row,
        me,
        request_adapter.reshape(1, rows),
        tokens,
        attention_norm_gain.reshape(1, depth),
    )
    sent, sels = prep[:n_wide], prep[n_wide : 2 * n_wide]
    xg, sq = prep[2 * n_wide :]

    held = [sent[0]] + [None] * (n_wide - 1)
    for k in range(n_wide - 1, 0, -1):
        held[k] = over("wide", n_wide, sent[k], k)

    base = [None] * n_tensor
    for k in range(n_tensor - 1, 0, -1):
        block = base_block((spot ^ k).reshape(1), xg, key_value_weight, sq, BF16)
        base[k] = over("tensor", n_tensor, block, k)
    base[0] = base_block(spot.reshape(1), xg, key_value_weight, sq, F32)

    half_size = HEAD // 2
    freq_index = jnp.arange(half_size).astype(F32)
    inverse = jnp.exp(freq_index * (-2.0 / HEAD) * math.log(ROPE_BASE))
    angles = cached_token_length.astype(F32)[:, None] * inverse[None, :]
    cosine, sine = jnp.cos(angles), jnp.sin(angles)
    cosine = jnp.concatenate([cosine, cosine], axis=1)
    sine = jnp.concatenate([-sine, sine], axis=1)

    deltas = [None] * n_wide
    for group in (range(0, 2), range(2, n_wide)):
        chunk = [held[k] for k in group]
        slots = [x[:, depth:] for x in chunk]
        low = down_block(chunk, adapter_down_weight)
        parts = [low] + [over("tensor", n_tensor, low, k) for k in range(1, n_tensor)]
        ups = up_block(parity, slots, parts, adapter_up_weight)
        for k, delta in zip(group, ups):
            deltas[k] = delta if k == 0 else over("wide", n_wide, delta, k)

    return pl.pallas_call(
        functools.partial(final_kernel, n_wide, n_tensor),
        out_shape=jax.ShapeDtypeStruct((rows, cols), BF16),
        in_specs=[smem()] + [whole()] * (n_tensor + 2 * n_wide + 2),
        out_specs=whole(),
        compiler_params=params(),
        name="finish",
    )(parity, *base, *deltas, *sels, cosine, sine)


def solution(mesh):
    return jax.shard_map(
        functools.partial(local, dict(mesh.shape)),
        mesh=mesh,
        in_specs=(
            P(("parts", "wide"), "tensor"),
            P("tensor"),
            P("tensor", None),
            P(("parts", "wide"), "tensor", None),
            P(("parts", "wide"), None, "tensor"),
            P(("parts", "wide")),
            P("parts"),
            P(("parts", "wide")),
        ),
        out_specs=P(("parts", "wide"), "tensor"),
        check_vma=False,
    )
```

```python
import functools
import math

import jax
import jax.numpy as jnp
from jax import lax
from jax.experimental import pallas as pl
from jax.experimental.pallas import tpu as pltpu
from jax.sharding import PartitionSpec as P

MODEL_WIDTH = 8192
HEAD = 128
EPSILON = 1e-05
ROPE_BASE = 500000.0
F32 = jnp.float32
BF16 = jnp.bfloat16


def iota(shape, axis):
    return lax.broadcasted_iota(jnp.int32, shape, axis)


def call(kernel, name, outs, vmem=(), hbm=(), after=(), scratch=(), flops=0, moved=0, limit=14):
    def body(*refs):
        keep = len(vmem) + len(hbm)
        kernel(*refs[:keep], *refs[keep + len(after) :])

    return pl.pallas_call(
        body,
        out_shape=outs,
        in_specs=[pl.BlockSpec(memory_space=pltpu.VMEM)] * len(vmem)
        + [pl.BlockSpec(memory_space=pltpu.HBM)] * len(hbm)
        + [pl.BlockSpec(memory_space=pl.ANY)] * len(after),
        out_specs=[pl.BlockSpec(memory_space=pltpu.VMEM)] * len(outs),
        scratch_shapes=scratch,
        compiler_params=pltpu.CompilerParams(vmem_limit_bytes=limit * 1024 * 1024),
        cost_estimate=pl.CostEstimate(flops=flops, bytes_accessed=moved, transcendentals=0),
        name=name,
    )(*vmem, *hbm, *after)


def shape(dims, dtype):
    return jax.ShapeDtypeStruct(dims, dtype)


def to_column(row, count):
    spread = iota((count, row.shape[1]), 0) == iota((count, row.shape[1]), 1)
    return jnp.sum(jnp.where(spread, row, 0.0), axis=1, keepdims=True)


def places(req, table, n_wide, per_dev):
    rows = req.shape[1]
    me = lax.axis_index("wide").astype(jnp.int32)
    stored = jnp.zeros_like(req)
    for a in range(table.shape[0]):
        stored = jnp.where(req == a, table[a], stored)
    owner = lax.div(stored, per_dev)
    slot = stored - owner * per_dev
    pad = -(-n_wide // 16) * 16
    hit = owner == (iota((pad, rows), 0) ^ me)
    earlier = (iota((rows, rows), 0) <= iota((rows, rows), 1)).astype(BF16)
    count = jnp.dot(hit.astype(BF16), earlier, preferred_element_type=F32)
    return jnp.where(hit, count.astype(jnp.int32) - 1, -1), slot


def dispatch_kernel(n_wide, per_dev, cap, req_hbm, table_hbm, tok_hbm, *refs):
    xs = refs[:n_wide]
    done_ref, req_ref, table_ref, tok_ref, sems = refs[n_wide:]
    done_ref[...] = jnp.zeros_like(done_ref)
    rows, depth = tok_ref.shape
    chunk = math.gcd(depth, 512)
    steps = depth // chunk
    small = [
        pltpu.make_async_copy(req_hbm, req_ref, sems.at[0]),
        pltpu.make_async_copy(table_hbm, table_ref, sems.at[1]),
    ]
    big = [
        pltpu.make_async_copy(
            tok_hbm.at[:, pl.ds(i * chunk, chunk)],
            tok_ref.at[:, pl.ds(i * chunk, chunk)],
            sems.at[2 + i],
        )
        for i in range(steps)
    ]
    for copy in small + big:
        copy.start()
    for copy in small:
        copy.wait()
    place, slot = places(req_ref[...], table_ref, n_wide, per_dev)
    height = xs[0].shape[0]
    slots = jnp.broadcast_to(slot.astype(F32), (16, rows)).astype(BF16)
    picks, slot_rows = [], []
    for k in range(n_wide):
        pick = (iota((HEAD, rows), 0) == place[k : k + 1]).astype(BF16)
        slot_rows.append(
            lax.dot_general(slots, pick, (((1,), (1,)), ((), ())), preferred_element_type=F32)
        )
        picks.append(pick[:height])
    for i in range(steps):
        big[i].wait()
        piece = tok_ref[:, i * chunk : (i + 1) * chunk]
        for k in range(n_wide):
            y = jnp.dot(picks[k], piece, preferred_element_type=F32)
            if i == 0:
                first = jnp.where(iota((height, HEAD), 0) == cap, slot_rows[k][:1], y[:, :HEAD])
                xs[k][:, :HEAD] = first.astype(BF16)
                xs[k][:, HEAD:chunk] = y[:, HEAD:].astype(BF16)
            else:
                xs[k][:, i * chunk : (i + 1) * chunk] = y.astype(BF16)


def weight_copies(offsets, weight_hbm, buf, sems, cols):
    spot = lax.axis_index("tensor").astype(jnp.int32)
    depth = weight_hbm.shape[0]
    chunk = buf.shape[2]
    steps = depth // chunk
    copies = []
    for j, k in enumerate(offsets):
        start = pl.multiple_of((spot ^ k) * cols, HEAD)
        copies.append(
            [
                pltpu.make_async_copy(
                    weight_hbm.at[pl.ds(i * chunk, chunk), pl.ds(start, cols)],
                    buf.at[j, i],
                    sems.at[j * steps + i],
                )
                for i in range(steps)
            ]
        )
    for group in copies:
        for copy in group:
            copy.start()
    return copies


def base_first_kernel(offsets, cols, gain_ref, tok_hbm, weight_hbm, xg_ref, *refs):
    outs = refs[: len(offsets)]
    tok_ref, buf, tok_sem, sems = refs[len(offsets) :]
    load = pltpu.make_async_copy(tok_hbm, tok_ref, tok_sem)
    load.start()
    copies = weight_copies(offsets, weight_hbm, buf, sems, cols)
    load.wait()
    depth = tok_ref.shape[1]
    for b in range(depth // HEAD):
        span = slice(b * HEAD, (b + 1) * HEAD)
        xg_ref[:, span] = (
            tok_ref[:, span].astype(F32) * gain_ref[b : b + 1].astype(F32)
        ).astype(BF16)
    base_sums(copies, buf, xg_ref, outs)


def base_kernel(offsets, cols, xg_ref, weight_hbm, *refs):
    outs = refs[: len(offsets)]
    buf, sems = refs[len(offsets) :]
    base_sums(weight_copies(offsets, weight_hbm, buf, sems, cols), buf, xg_ref, outs)


def base_sums(copies, buf, xg_ref, outs):
    chunk = buf.shape[2]
    for j, out_ref in enumerate(outs):
        total = None
        for i, copy in enumerate(copies[j]):
            copy.wait()
            y = jnp.dot(
                xg_ref[:, i * chunk : (i + 1) * chunk], buf[j, i], preferred_element_type=F32
            )
            total = y if total is None else total + y
        out_ref[...] = total.astype(out_ref.dtype)


def pair_kernel(count, *refs):
    for j in range(count):
        total = refs[j][...] + refs[count + j][...].astype(F32)
        refs[2 * count + j][...] = total.astype(BF16)


def scaled_down_kernel(gain_ref, down_hbm, out_ref, buf, sems):
    per_dev, depth, rank = down_hbm.shape
    copies = [pltpu.make_async_copy(down_hbm.at[a], buf.at[a], sems.at[a]) for a in range(per_dev)]
    for copy in copies:
        copy.start()
    columns = []
    for b in range(depth // HEAD):
        columns.append(to_column(gain_ref[b : b + 1].astype(F32), HEAD))
    for a in range(per_dev):
        copies[a].wait()
        for b in range(depth // HEAD):
            span = slice(b * HEAD, (b + 1) * HEAD)
            out_ref[span, a * rank : (a + 1) * rank] = (
                buf[a, span].astype(F32) * columns[b]
            ).astype(BF16)


def aux_kernel(n_wide, per_dev, req_hbm, table_hbm, tok_hbm, sq_ref, *refs):
    sels = refs[:n_wide]
    req_ref, table_ref, tok_ref, sems = refs[n_wide:]
    copies = [
        pltpu.make_async_copy(req_hbm, req_ref, sems.at[0]),
        pltpu.make_async_copy(table_hbm, table_ref, sems.at[1]),
        pltpu.make_async_copy(tok_hbm, tok_ref, sems.at[2]),
    ]
    for copy in copies:
        copy.start()
    for copy in copies:
        copy.wait()
    rows = tok_ref.shape[0]
    place, _ = places(req_ref[...], table_ref, n_wide, per_dev)
    place = place.astype(F32)
    for k in range(n_wide):
        column = to_column(place[k : k + 1], rows).astype(jnp.int32)
        sels[k][...] = (iota((rows, HEAD), 1) == column).astype(BF16)
    tok = tok_ref[...]
    gram = lax.dot_general(tok, tok, (((1,), (1,)), ((), ())), preferred_element_type=F32)
    diag = iota((rows, rows), 0) == iota((rows, rows), 1)
    sq = jnp.sum(jnp.where(diag, gram, 0.0), axis=0, keepdims=True)
    block = jnp.zeros((8, HEAD), F32)
    for p in range(3):
        part = sq.astype(BF16).astype(F32)
        sq = sq - part
        for i in range(rows // HEAD):
            term = part[:, i * HEAD : (i + 1) * HEAD]
            block = jnp.where(iota((8, HEAD), 0) == p * (rows // HEAD) + i, term, block)
    sq_ref[...] = block


def slot_column(x_ref, cap):
    height = x_ref.shape[0]
    base = cap // 16 * 16
    row = x_ref[base : base + 16, :HEAD].astype(F32)[cap - base : cap - base + 1]
    column = to_column(row, height)
    return jnp.where(iota((height, 1), 0) < cap, column, -1.0)


def down_kernel(count, cap, with_sq, *refs):
    xs, down_ref = refs[:count], refs[count]
    sq_ref = refs[count + 1] if with_sq else None
    out_ref = refs[-1]
    height, depth = xs[0].shape
    rank = HEAD
    x = jnp.concatenate([x[...] for x in xs], axis=0) if count > 1 else xs[0][...]
    slot = [slot_column(x, cap) for x in xs]
    slot = jnp.concatenate(slot, axis=0) if count > 1 else slot[0]
    low = jnp.zeros((count * height, rank), F32)
    for g in range(down_ref.shape[1] // (2 * rank)):
        y = jnp.dot(
            x, down_ref[:, 2 * g * rank : 2 * (g + 1) * rank], preferred_element_type=F32
        )
        low = jnp.where(slot == 2 * g, y[:, :rank], low)
        low = jnp.where(slot == 2 * g + 1, y[:, rank:], low)
    for j in range(count):
        part = low[j * height : (j + 1) * height]
        if j == 0 and with_sq:
            tail = [jnp.zeros((cap, rank), F32), sq_ref[...]]
            if height > cap + 8:
                tail.append(jnp.zeros((height - cap - 8, rank), F32))
            part = part + jnp.concatenate(tail, axis=0)
        out_ref[j] = part.astype(BF16)


def head_is_key(heads, h):
    if heads % 2 == 0:
        return h % 2 == 0
    return (lax.axis_index("tensor").astype(jnp.int32) * heads + h) % 2 == 0


def up_kernel(count, n_tensor, cap, with_sq, *refs):
    xs = refs[:count]
    parts = refs[count : count + n_tensor]
    up_ref = refs[count + n_tensor]
    outs = refs[count + n_tensor + 1 :]
    per_dev, half, cols = up_ref.shape
    heads = cols // HEAD
    height, rank = parts[0].shape[1:]
    up = up_ref[...].reshape(per_dev * half, cols)
    sums = []
    for j in range(count):
        low = parts[0][j].astype(F32)
        for part in parts[1:]:
            low = low + part[j].astype(F32)
        sums.append(low)
    if with_sq:
        outs[count][...] = sums[0][cap : cap + 8]
    low = jnp.concatenate(sums, axis=0) if count > 1 else sums[0]
    slot = [slot_column(x, cap) for x in xs]
    slot = jnp.concatenate(slot, axis=0) if count > 1 else slot[0]
    left = iota((count * height, rank), 1) < half
    turned = pltpu.roll(low, half, 1)
    wide = []
    for source in (jnp.where(left, low, turned), jnp.where(left, turned, low)):
        pieces = []
        for g in range(per_dev // 2):
            mine = slot == jnp.where(left, 2.0 * g, 2.0 * g + 1)
            pieces.append(jnp.where(mine, source, 0.0).astype(BF16))
        wide.append(jnp.concatenate(pieces, axis=1))
    for h in range(heads):
        key = head_is_key(heads, h)
        if isinstance(key, bool):
            lhs = wide[0] if key else wide[1]
        else:
            lhs = jnp.where(key, wide[0].astype(F32), wide[1].astype(F32)).astype(BF16)
        span = slice(h * HEAD, (h + 1) * HEAD)
        y = jnp.dot(lhs, up[:, span], preferred_element_type=F32).astype(BF16)
        for j in range(count):
            outs[j][:, span] = y[j * height : (j + 1) * height]


def placed(sels, deltas):
    height, cols = deltas[0].shape
    blocks = []
    for delta in deltas:
        blocks.append(delta[...])
        if height < HEAD:
            blocks.append(jnp.zeros((HEAD - height, cols), BF16))
    lhs = jnp.concatenate([sel[...] for sel in sels], axis=1) if len(sels) > 1 else sels[0][...]
    return jnp.dot(lhs, jnp.concatenate(blocks, axis=0), preferred_element_type=F32)


def gather_kernel(n_base, count, sq_ref, *refs):
    base = refs[:n_base]
    deltas = refs[n_base : n_base + count]
    sels = refs[n_base + count : n_base + 2 * count]
    out_ref, scale_ref = refs[-2:]
    rows, cols = out_ref.shape
    pieces = rows // HEAD
    squares = []
    for i in range(pieces):
        total = sq_ref[i : i + 1]
        for p in range(1, 3):
            total = total + sq_ref[p * pieces + i : p * pieces + i + 1]
        squares.append(total)
    square = to_column(jnp.concatenate(squares, axis=1), rows)
    scale = lax.rsqrt(square * (1.0 / MODEL_WIDTH) + EPSILON)
    scale_ref[...] = jnp.broadcast_to(scale, (rows, HEAD))
    total = base[0][...]
    for b in base[1:]:
        total = total + b[...].astype(F32)
    out_ref[...] = total + placed(sels, deltas)


def finish_kernel(sum_ref, scale_ref, delta_ref, sel_ref, cos_ref, sin_ref, out_ref):
    rows, cols = out_ref.shape
    total = sum_ref[...] + placed([sel_ref], [delta_ref])
    heads = cols // HEAD
    scale = scale_ref[...]
    for h in range(heads):
        span = slice(h * HEAD, (h + 1) * HEAD)
        x = total[:, span] * scale
        key = head_is_key(heads, h)
        if key is False:
            out_ref[:, span] = x.astype(BF16)
            continue
        y = x * cos_ref[...] + pltpu.roll(x, HEAD // 2, 1) * sin_ref[...]
        if key is not True:
            y = jnp.where(key, y, x)
        out_ref[:, span] = y.astype(BF16)


def local(
    mesh_shape,
    tokens,
    attention_norm_gain,
    key_value_weight,
    adapter_down_weight,
    adapter_up_weight,
    request_adapter,
    adapter_storage_row,
    cached_token_length,
):
    n_wide, n_tensor = mesh_shape["wide"], mesh_shape["tensor"]
    rows, depth = tokens.shape
    per_dev, _, rank = adapter_down_weight.shape
    cols = adapter_up_weight.shape[2]
    cap = 104 if n_wide <= 4 else 64
    height = -(-(cap + 8) // 16) * 16
    req = request_adapter.reshape(1, rows)
    gain = attention_norm_gain.reshape(depth // HEAD, HEAD)

    def over(axis, array, k):
        size = mesh_shape[axis]
        return lax.ppermute(array, axis, [(i, i ^ k) for i in range(size)])

    small = [pltpu.VMEM((1, rows), jnp.int32), pltpu.SMEM(adapter_storage_row.shape, jnp.int32)]
    *sent, done = call(
        functools.partial(dispatch_kernel, n_wide, per_dev, cap),
        "dispatch",
        [shape((height, depth), BF16)] * n_wide + [shape((8, HEAD), F32)],
        hbm=(req, adapter_storage_row, tokens),
        scratch=small
        + [pltpu.VMEM((rows, depth), BF16), pltpu.SemaphoreType.DMA((2 + depth // 256,))],
        flops=2 * n_wide * height * rows * depth,
        moved=2 * rows * depth * 4,
        limit=63,
    )
    last = 2
    first = [0, 1] + list(range(3, n_wide))
    order = list(range(n_wide - 1, 2, -1)) + [last, 1]
    held = [sent[0]] + [None] * (n_wide - 1)
    for k in order:
        held[k] = over("wide", sent[k], k)

    chunk = math.gcd(depth, 512)
    steps = depth // chunk

    def weight_scratch(count):
        return [
            pltpu.VMEM((count, steps, chunk, cols), BF16),
            pltpu.SemaphoreType.DMA((count * steps,)),
        ]

    def cost(count):
        return dict(flops=2 * rows * depth * cols * count, moved=2 * depth * cols * count, limit=52)

    twos = list(range(2, n_tensor, 2))
    far = [k ^ 1 for k in twos]
    xg, *away = call(
        functools.partial(base_first_kernel, far, cols),
        "base_far",
        [shape((rows, depth), BF16)] + [shape((rows, cols), BF16)] * len(far),
        vmem=(gain,),
        hbm=(tokens, key_value_weight),
        after=(done,),
        scratch=[pltpu.VMEM((rows, depth), BF16)]
        + weight_scratch(len(far))[:1]
        + [pltpu.SemaphoreType.DMA]
        + weight_scratch(len(far))[1:],
        **cost(len(far)),
    )
    beside = [over("tensor", p, 1) for p in away]
    near, *own = call(
        functools.partial(base_kernel, [1] + twos, cols),
        "base_near",
        [shape((rows, cols), BF16)] + [shape((rows, cols), F32)] * len(twos),
        vmem=(xg,),
        hbm=(key_value_weight,),
        after=(away[0],),
        scratch=weight_scratch(1 + len(twos)),
        **cost(1 + len(twos)),
    )
    near = over("tensor", near, 1)
    (down,) = call(
        scaled_down_kernel,
        "scaled_down",
        [shape((depth, per_dev * rank), BF16)],
        vmem=(gain,),
        hbm=(adapter_down_weight,),
        after=(own[0],),
        scratch=[
            pltpu.VMEM((per_dev, depth, rank), BF16),
            pltpu.SemaphoreType.DMA((per_dev,)),
        ],
        flops=4 * depth * per_dev * rank,
        moved=4 * depth * per_dev * rank,
        limit=40,
    )
    pairs = call(
        functools.partial(pair_kernel, len(twos)),
        "pair_sums",
        [shape((rows, cols), BF16)] * len(twos),
        vmem=(*own, *beside),
        after=(down,),
        moved=8 * rows * cols * len(twos),
    )
    pairs = [over("tensor", p, k) for p, k in zip(pairs, twos)]
    sq, *sels = call(
        functools.partial(aux_kernel, n_wide, per_dev),
        "aux",
        [shape((8, HEAD), F32)] + [shape((rows, HEAD), BF16)] * n_wide,
        hbm=(req, adapter_storage_row, tokens),
        after=(down,),
        scratch=small + [pltpu.VMEM((rows, depth), BF16), pltpu.SemaphoreType.DMA((3,))],
        flops=2 * rows * rows * depth,
        moved=2 * rows * depth,
        limit=52,
    )

    def down_block(group, extra, after):
        xs = [held[k] for k in group]
        (low,) = call(
            functools.partial(down_kernel, len(xs), cap, bool(extra)),
            "down_block",
            [shape((len(xs), height, rank), BF16)],
            vmem=(*xs, down, *extra),
            after=after,
            flops=2 * len(xs) * height * depth * rank * per_dev,
            moved=2 * per_dev * depth * rank,
        )
        return [low] + [over("tensor", low, k) for k in range(n_tensor - 1, 0, -1)]

    def up_block(group, parts, with_sq, after):
        xs = [held[k] for k in group]
        outs = [shape((height, cols), BF16)] * len(xs)
        if with_sq:
            outs = outs + [shape((8, HEAD), F32)]
        return call(
            functools.partial(up_kernel, len(xs), n_tensor, cap, with_sq),
            "up_block",
            outs,
            vmem=(*xs, *parts, adapter_up_weight),
            after=after,
            flops=2 * len(xs) * height * per_dev * rank * cols,
            moved=2 * per_dev * rank * cols,
        )

    first_parts = down_block(first, (sq,), ())
    (base,) = call(
        functools.partial(base_kernel, [0], cols),
        "base_own",
        [shape((rows, cols), F32)],
        vmem=(xg,),
        hbm=(key_value_weight,),
        after=(first_parts[0],),
        scratch=weight_scratch(1),
        **cost(1),
    )

    half_size = HEAD // 2
    freq_index = jnp.arange(half_size).astype(F32)
    inverse = jnp.exp(freq_index * (-2.0 / HEAD) * math.log(ROPE_BASE))
    angles = cached_token_length.astype(F32)[:, None] * inverse[None, :]
    cosine, sine = jnp.cos(angles), jnp.sin(angles)
    cosine = jnp.concatenate([cosine, cosine], axis=1)
    sine = jnp.concatenate([-sine, sine], axis=1)

    last_parts = down_block([last], (), (base, cosine, sine))
    *ups, square = up_block(first, first_parts, True, (last_parts[0],))
    deltas = [u if k == 0 else over("wide", u, k) for k, u in zip(first, ups)]
    (up,) = up_block([last], last_parts, False, (square,))
    delta = over("wide", up, last)
    total, scale = call(
        functools.partial(gather_kernel, 2 + len(pairs), len(first)),
        "gather",
        [shape((rows, cols), F32), shape((rows, HEAD), F32)],
        vmem=(square, base, near, *pairs, *deltas, *[sels[k] for k in first]),
        after=(up,),
        flops=2 * rows * cols * HEAD * len(first),
    )
    return call(
        finish_kernel,
        "finish",
        [shape((rows, cols), BF16)],
        vmem=(total, scale, delta, sels[last], cosine, sine),
        flops=2 * rows * cols * HEAD,
    )[0]


def solution(mesh):
    return jax.shard_map(
        functools.partial(local, dict(mesh.shape)),
        mesh=mesh,
        in_specs=(
            P(("parts", "wide"), "tensor"),
            P("tensor"),
            P("tensor", None),
            P(("parts", "wide"), "tensor", None),
            P(("parts", "wide"), None, "tensor"),
            P(("parts", "wide")),
            P("parts"),
            P(("parts", "wide")),
        ),
        out_specs=P(("parts", "wide"), "tensor"),
        check_vma=False,
    )
```

```python
import functools
import math

import jax
import jax.numpy as jnp
from jax import lax
from jax.experimental import pallas as pl
from jax.experimental.pallas import tpu as pltpu
from jax.sharding import PartitionSpec as P

MODEL_WIDTH = 8192
HEAD = 128
EPSILON = 1e-05
ROPE_BASE = 500000.0
F32 = jnp.float32
BF16 = jnp.bfloat16


def iota(shape, axis):
    return lax.broadcasted_iota(jnp.int32, shape, axis)


def call(kernel, name, outs, vmem=(), hbm=(), after=(), scratch=(), flops=0, moved=0, limit=16, hbm_outs=0):
    def body(*refs):
        keep = len(vmem) + len(hbm)
        kernel(*refs[:keep], *refs[keep + len(after) :])

    return pl.pallas_call(
        body,
        out_shape=outs,
        in_specs=[pl.BlockSpec(memory_space=pltpu.VMEM)] * len(vmem)
        + [pl.BlockSpec(memory_space=pltpu.HBM)] * len(hbm)
        + [pl.BlockSpec(memory_space=pl.ANY)] * len(after),
        out_specs=[pl.BlockSpec(memory_space=pltpu.HBM)] * hbm_outs
        + [pl.BlockSpec(memory_space=pltpu.VMEM)] * (len(outs) - hbm_outs),
        scratch_shapes=scratch,
        compiler_params=pltpu.CompilerParams(vmem_limit_bytes=limit * 1024 * 1024),
        cost_estimate=pl.CostEstimate(flops=flops, bytes_accessed=moved, transcendentals=0),
        name=name,
    )(*vmem, *hbm, *after)


def shape(dims, dtype):
    return jax.ShapeDtypeStruct(dims, dtype)


def to_column(row, count):
    spread = iota((count, row.shape[1]), 0) == iota((count, row.shape[1]), 1)
    return jnp.sum(jnp.where(spread, row, 0.0), axis=1, keepdims=True)


def places(req, table, n_wide, per_dev):
    rows = req.shape[1]
    me = lax.axis_index("wide").astype(jnp.int32)
    stored = jnp.zeros_like(req)
    for a in range(table.shape[0]):
        stored = jnp.where(req == a, table[a], stored)
    owner = lax.div(stored, per_dev)
    slot = stored - owner * per_dev
    pad = -(-n_wide // 16) * 16
    hit = owner == (iota((pad, rows), 0) ^ me)
    earlier = (iota((rows, rows), 0) <= iota((rows, rows), 1)).astype(BF16)
    count = jnp.dot(hit.astype(BF16), earlier, preferred_element_type=F32)
    return jnp.where(hit, count.astype(jnp.int32) - 1, -1), slot


def dispatch_kernel(order, n_wide, per_dev, cap, req_hbm, table_hbm, tok_hbm, gain_hbm, *refs):
    xs = refs[: len(order)]
    wide_gain_ref, req_ref, table_ref, tok_ref, gain_ref, x_ref, sems, out_sems = refs[
        len(order) :
    ]
    rows, depth = tok_ref.shape
    height = x_ref.shape[1]
    loads = [
        pltpu.make_async_copy(req_hbm, req_ref, sems.at[0]),
        pltpu.make_async_copy(table_hbm, table_ref, sems.at[1]),
        pltpu.make_async_copy(tok_hbm, tok_ref, sems.at[2]),
        pltpu.make_async_copy(gain_hbm, gain_ref, sems.at[3]),
    ]
    for copy in loads:
        copy.start()
    loads[0].wait()
    loads[1].wait()
    place, slot = places(req_ref[...], table_ref, n_wide, per_dev)
    slots = jnp.broadcast_to(slot.astype(F32), (16, rows)).astype(BF16)
    picks, slot_rows = [], []
    for k in order:
        pick = (iota((HEAD, rows), 0) == place[k : k + 1]).astype(BF16)
        slot_rows.append(
            lax.dot_general(slots, pick, (((1,), (1,)), ((), ())), preferred_element_type=F32)
        )
        picks.append(pick[:height])
    loads[3].wait()
    wide_gain_ref[...] = gain_ref[...].astype(F32)
    loads[2].wait()
    stores = []
    for j, k in enumerate(order):
        y = jnp.dot(picks[j], tok_ref[...], preferred_element_type=F32)
        first = jnp.where(iota((height, HEAD), 0) == cap, slot_rows[j][:1], y[:, :HEAD])
        x_ref[j, :, :HEAD] = first.astype(BF16)
        x_ref[j, :, HEAD:] = y[:, HEAD:].astype(BF16)
        copy = pltpu.make_async_copy(x_ref.at[j], xs[j], out_sems.at[j])
        copy.start()
        stores.append(copy)
    for copy in stores:
        copy.wait()


def base_kernel(offsets, cols, gain_hbm, tok_hbm, weight_hbm, *refs):
    count = len(offsets)
    outs = refs[:count]
    gain_ref, tok_ref, buf, acc_ref, sems = refs[count:]
    steps, chunk, _ = buf.shape
    copies = [
        pltpu.make_async_copy(weight_hbm.at[pl.ds(i * chunk, chunk)], buf.at[i], sems.at[2 + i])
        for i in range(steps)
    ]
    loads = [
        pltpu.make_async_copy(gain_hbm, gain_ref, sems.at[0]),
        pltpu.make_async_copy(tok_hbm, tok_ref, sems.at[1]),
    ]
    for copy in loads + copies:
        copy.start()
    for copy in loads:
        copy.wait()
    spot = lax.axis_index("tensor").astype(jnp.int32)
    for i in range(steps):
        pieces = []
        for b in range(i * chunk // HEAD, (i + 1) * chunk // HEAD):
            piece = tok_ref[:, b * HEAD : (b + 1) * HEAD].astype(F32) * gain_ref[b : b + 1]
            pieces.append(piece.astype(BF16))
        x = jnp.concatenate(pieces, axis=1)
        copies[i].wait()
        for j, k in enumerate(offsets):
            start = pl.multiple_of((spot ^ k) * cols, HEAD)
            y = jnp.dot(x, buf[i, :, pl.ds(start, cols)], preferred_element_type=F32)
            if i > 0:
                y = y + acc_ref[j]
            if i < steps - 1:
                acc_ref[j] = y
            else:
                outs[j][...] = y.astype(outs[j].dtype)


def pair_kernel(count, *refs):
    for j in range(count):
        total = refs[j][...] + refs[count + j][...].astype(F32)
        refs[2 * count + j][...] = total.astype(BF16)


def scaled_down_kernel(gain_ref, down_hbm, out_ref, buf, sems):
    per_dev, depth, rank = down_hbm.shape
    copies = [pltpu.make_async_copy(down_hbm.at[a], buf.at[a], sems.at[a]) for a in range(per_dev)]
    for copy in copies:
        copy.start()
    columns = []
    for b in range(depth // HEAD):
        columns.append(to_column(gain_ref[b : b + 1], HEAD))
    for a in range(per_dev):
        copies[a].wait()
        for b in range(depth // HEAD):
            span = slice(b * HEAD, (b + 1) * HEAD)
            out_ref[span, a * rank : (a + 1) * rank] = (
                buf[a, span].astype(F32) * columns[b]
            ).astype(BF16)


def aux_kernel(n_wide, per_dev, req_hbm, table_hbm, tok_hbm, sq_ref, *refs):
    sels = refs[:n_wide]
    req_ref, table_ref, tok_ref, sems = refs[n_wide:]
    copies = [
        pltpu.make_async_copy(req_hbm, req_ref, sems.at[0]),
        pltpu.make_async_copy(table_hbm, table_ref, sems.at[1]),
        pltpu.make_async_copy(tok_hbm, tok_ref, sems.at[2]),
    ]
    for copy in copies:
        copy.start()
    for copy in copies:
        copy.wait()
    rows = tok_ref.shape[0]
    place, _ = places(req_ref[...], table_ref, n_wide, per_dev)
    place = place.astype(F32)
    for k in range(n_wide):
        column = to_column(place[k : k + 1], rows).astype(jnp.int32)
        sels[k][...] = (iota((rows, HEAD), 1) == column).astype(BF16)
    tok = tok_ref[...]
    gram = lax.dot_general(tok, tok, (((1,), (1,)), ((), ())), preferred_element_type=F32)
    diag = iota((rows, rows), 0) == iota((rows, rows), 1)
    sq = jnp.sum(jnp.where(diag, gram, 0.0), axis=0, keepdims=True)
    block = jnp.zeros((8, HEAD), F32)
    for p in range(3):
        part = sq.astype(BF16).astype(F32)
        sq = sq - part
        for i in range(rows // HEAD):
            term = part[:, i * HEAD : (i + 1) * HEAD]
            block = jnp.where(iota((8, HEAD), 0) == p * (rows // HEAD) + i, term, block)
    sq_ref[...] = block


def slot_column(x_ref, cap):
    height = x_ref.shape[0]
    base = cap // 16 * 16
    row = x_ref[base : base + 16, :HEAD].astype(F32)[cap - base : cap - base + 1]
    column = to_column(row, height)
    return jnp.where(iota((height, 1), 0) < cap, column, -1.0)


def down_kernel(count, cap, with_sq, *refs):
    xs, down_ref = refs[:count], refs[count]
    sq_ref = refs[count + 1] if with_sq else None
    out_ref = refs[-1]
    height, depth = xs[0].shape
    rank = HEAD
    x = jnp.concatenate([x[...] for x in xs], axis=0) if count > 1 else xs[0][...]
    slot = [slot_column(x, cap) for x in xs]
    slot = jnp.concatenate(slot, axis=0) if count > 1 else slot[0]
    low = jnp.zeros((count * height, rank), F32)
    for g in range(down_ref.shape[1] // (2 * rank)):
        y = jnp.dot(
            x, down_ref[:, 2 * g * rank : 2 * (g + 1) * rank], preferred_element_type=F32
        )
        low = jnp.where(slot == 2 * g, y[:, :rank], low)
        low = jnp.where(slot == 2 * g + 1, y[:, rank:], low)
    for j in range(count):
        part = low[j * height : (j + 1) * height]
        if j == 0 and with_sq:
            tail = [jnp.zeros((cap, rank), F32), sq_ref[...]]
            if height > cap + 8:
                tail.append(jnp.zeros((height - cap - 8, rank), F32))
            part = part + jnp.concatenate(tail, axis=0)
        out_ref[j] = part.astype(BF16)


def low_sum_kernel(count, *refs):
    left, right, out_ref = refs[0], refs[1], refs[2 + count]
    out_ref[...] = (left[...].astype(F32) + right[...].astype(F32)).astype(BF16)
    if count:
        total = refs[2][...]
        for b in refs[3 : 2 + count]:
            total = total + b[...].astype(F32)
        refs[3 + count][...] = total


def head_is_key(heads, h):
    if heads % 2 == 0:
        return h % 2 == 0
    return (lax.axis_index("tensor").astype(jnp.int32) * heads + h) % 2 == 0


def up_kernel(count, n_parts, cap, with_sq, *refs):
    xs = refs[:count]
    parts = refs[count : count + n_parts]
    up_ref = refs[count + n_parts]
    outs = refs[count + n_parts + 1 :]
    per_dev, half, cols = up_ref.shape
    heads = cols // HEAD
    height, rank = parts[0].shape[1:]
    up = up_ref[...].reshape(per_dev * half, cols)
    sums = []
    for j in range(count):
        low = parts[0][j].astype(F32)
        for part in parts[1:]:
            low = low + part[j].astype(F32)
        sums.append(low)
    if with_sq:
        outs[count][...] = sums[0][cap : cap + 8]
    low = jnp.concatenate(sums, axis=0) if count > 1 else sums[0]
    slot = [slot_column(x, cap) for x in xs]
    slot = jnp.concatenate(slot, axis=0) if count > 1 else slot[0]
    left = iota((count * height, rank), 1) < half
    turned = pltpu.roll(low, half, 1)
    wide = []
    for source in (jnp.where(left, low, turned), jnp.where(left, turned, low)):
        pieces = []
        for g in range(per_dev // 2):
            mine = slot == jnp.where(left, 2.0 * g, 2.0 * g + 1)
            pieces.append(jnp.where(mine, source, 0.0).astype(BF16))
        wide.append(jnp.concatenate(pieces, axis=1))
    for h in range(heads):
        key = head_is_key(heads, h)
        if isinstance(key, bool):
            lhs = wide[0] if key else wide[1]
        else:
            lhs = jnp.where(key, wide[0].astype(F32), wide[1].astype(F32)).astype(BF16)
        span = slice(h * HEAD, (h + 1) * HEAD)
        y = jnp.dot(lhs, up[:, span], preferred_element_type=F32).astype(BF16)
        for j in range(count):
            outs[j][:, span] = y[j * height : (j + 1) * height]


def placed(sels, deltas):
    height, cols = deltas[0].shape
    blocks = []
    for delta in deltas:
        blocks.append(delta[...])
        if height < HEAD:
            blocks.append(jnp.zeros((HEAD - height, cols), BF16))
    lhs = jnp.concatenate([sel[...] for sel in sels], axis=1) if len(sels) > 1 else sels[0][...]
    return jnp.dot(lhs, jnp.concatenate(blocks, axis=0), preferred_element_type=F32)


def gather_kernel(n_base, count, sq_ref, *refs):
    base = refs[:n_base]
    deltas = refs[n_base : n_base + count]
    sels = refs[n_base + count : n_base + 2 * count]
    out_ref, scale_ref = refs[-2:]
    rows, cols = out_ref.shape
    pieces = rows // HEAD
    squares = []
    for i in range(pieces):
        total = sq_ref[i : i + 1]
        for p in range(1, 3):
            total = total + sq_ref[p * pieces + i : p * pieces + i + 1]
        squares.append(total)
    square = to_column(jnp.concatenate(squares, axis=1), rows)
    scale = lax.rsqrt(square * (1.0 / MODEL_WIDTH) + EPSILON)
    scale_ref[...] = jnp.broadcast_to(scale, (rows, HEAD))
    total = base[0][...]
    for b in base[1:]:
        total = total + b[...].astype(F32)
    out_ref[...] = total + placed(sels, deltas)


def finish_kernel(sum_ref, scale_ref, delta_ref, sel_ref, cos_ref, sin_ref, out_ref):
    rows, cols = out_ref.shape
    total = sum_ref[...] + placed([sel_ref], [delta_ref])
    heads = cols // HEAD
    scale = scale_ref[...]
    for h in range(heads):
        span = slice(h * HEAD, (h + 1) * HEAD)
        x = total[:, span] * scale
        key = head_is_key(heads, h)
        if key is False:
            out_ref[:, span] = x.astype(BF16)
            continue
        y = x * cos_ref[...] + pltpu.roll(x, HEAD // 2, 1) * sin_ref[...]
        if key is not True:
            y = jnp.where(key, y, x)
        out_ref[:, span] = y.astype(BF16)


def local(
    mesh_shape,
    tokens,
    attention_norm_gain,
    key_value_weight,
    adapter_down_weight,
    adapter_up_weight,
    request_adapter,
    adapter_storage_row,
    cached_token_length,
):
    n_wide, n_tensor = mesh_shape["wide"], mesh_shape["tensor"]
    rows, depth = tokens.shape
    per_dev, _, rank = adapter_down_weight.shape
    cols = adapter_up_weight.shape[2]
    cap = 104 if n_wide <= 4 else 64
    height = -(-(cap + 8) // 16) * 16
    req = request_adapter.reshape(1, rows)
    gain = attention_norm_gain.reshape(depth // HEAD, HEAD)

    def over(axis, array, k):
        size = mesh_shape[axis]
        return lax.ppermute(array, axis, [(i, i ^ k) for i in range(size)])

    small = [pltpu.VMEM((1, rows), jnp.int32), pltpu.SMEM(adapter_storage_row.shape, jnp.int32)]
    last = 2
    first = [0, 1] + list(range(3, n_wide))

    def dispatch(order, after):
        *blocks, wide_gain = call(
            functools.partial(dispatch_kernel, order, n_wide, per_dev, cap),
            "dispatch",
            [shape((height, depth), BF16)] * len(order) + [shape(gain.shape, F32)],
            hbm=(req, adapter_storage_row, tokens, gain),
            hbm_outs=len(order),
            after=after,
            scratch=small
            + [
                pltpu.VMEM((rows, depth), BF16),
                pltpu.VMEM(gain.shape, BF16),
                pltpu.VMEM((len(order), height, depth), BF16),
                pltpu.SemaphoreType.DMA((4,)),
                pltpu.SemaphoreType.DMA((len(order),)),
            ],
            flops=2 * len(order) * height * rows * depth,
            moved=2 * rows * depth * 4,
            limit=63,
        )
        return blocks, wide_gain

    held = [None] * n_wide
    early = list(range(n_wide - 1, 2, -1))
    blocks, wide_gain = dispatch(early, ())
    for k, block in zip(early, blocks):
        held[k] = over("wide", block, k)
    blocks, wide_gain = dispatch([last, 1, 0], (wide_gain,))
    held[0] = blocks[2]
    held[last], held[1] = over("wide", blocks[0], last), over("wide", blocks[1], 1)

    twos = list(range(2, n_tensor, 2))
    far = [k ^ 1 for k in twos]
    offsets = far + [1] + twos + [0]
    chunk = math.gcd(depth, 512)
    steps = depth // chunk
    sums = call(
        functools.partial(base_kernel, offsets, cols),
        "base",
        [shape((rows, cols), BF16)] * (len(far) + 1) + [shape((rows, cols), F32)] * (len(twos) + 1),
        hbm=(wide_gain, tokens, key_value_weight),
        scratch=[
            pltpu.VMEM(gain.shape, F32),
            pltpu.VMEM((rows, depth), BF16),
            pltpu.VMEM((steps, chunk, key_value_weight.shape[1]), BF16),
            pltpu.VMEM((len(offsets), rows, cols), F32),
            pltpu.SemaphoreType.DMA((2 + steps,)),
        ],
        flops=2 * rows * depth * cols * n_tensor,
        moved=2 * depth * cols * n_tensor,
        limit=52,
    )
    away, near, own, base = sums[: len(far)], sums[len(far)], sums[len(far) + 1 : -1], sums[-1]
    beside = [over("tensor", p, 1) for p in away]
    near = over("tensor", near, 1)
    (down,) = call(
        scaled_down_kernel,
        "scaled_down",
        [shape((depth, per_dev * rank), BF16)],
        vmem=(wide_gain,),
        hbm=(adapter_down_weight,),
        after=(base,),
        scratch=[
            pltpu.VMEM((per_dev, depth, rank), BF16),
            pltpu.SemaphoreType.DMA((per_dev,)),
        ],
        flops=4 * depth * per_dev * rank,
        moved=4 * depth * per_dev * rank,
    )
    half_size = HEAD // 2
    freq_index = jnp.arange(half_size).astype(F32)
    inverse = jnp.exp(freq_index * (-2.0 / HEAD) * math.log(ROPE_BASE))
    angles = cached_token_length.astype(F32)[:, None] * inverse[None, :]
    cosine, sine = jnp.cos(angles), jnp.sin(angles)
    cosine = jnp.concatenate([cosine, cosine], axis=1)
    sine = jnp.concatenate([-sine, sine], axis=1)

    pairs = call(
        functools.partial(pair_kernel, len(twos)),
        "pair_sums",
        [shape((rows, cols), BF16)] * len(twos),
        vmem=(*own, *beside),
        after=(down, cosine, sine, held[1]),
        moved=8 * rows * cols * len(twos),
    )
    pairs_here = pairs
    pairs = [over("tensor", p, k) for p, k in zip(pairs, twos)]

    def down_block(group, extra, after):
        xs = [held[k] for k in group]
        (low,) = call(
            functools.partial(down_kernel, len(xs), cap, bool(extra)),
            "down_block",
            [shape((len(xs), height, rank), BF16)],
            vmem=(*xs, down, *extra),
            after=after,
            flops=2 * len(xs) * height * depth * rank * per_dev,
            moved=2 * per_dev * depth * rank,
        )
        return low

    def up_block(group, parts, with_sq, after):
        xs = [held[k] for k in group]
        outs = [shape((height, cols), BF16)] * len(xs)
        if with_sq:
            outs = outs + [shape((8, HEAD), F32)]
        return call(
            functools.partial(up_kernel, len(xs), len(parts), cap, with_sq),
            "up_block",
            outs,
            vmem=(*xs, *parts, adapter_up_weight),
            after=after,
            flops=2 * len(xs) * height * per_dev * rank * cols,
            moved=2 * per_dev * rank * cols,
        )

    low = down_block(first, (), (pairs_here[0],))
    sq, *sels = call(
        functools.partial(aux_kernel, n_wide, per_dev),
        "aux",
        [shape((8, HEAD), F32)] + [shape((rows, HEAD), BF16)] * n_wide,
        hbm=(req, adapter_storage_row, tokens),
        after=(low,),
        scratch=small + [pltpu.VMEM((rows, depth), BF16), pltpu.SemaphoreType.DMA((3,))],
        flops=2 * rows * rows * depth,
        moved=2 * rows * depth,
    )
    step = 1
    while True:
        other = over("tensor", low, step)
        if step * 2 >= n_tensor:
            break
        adds = (base, near) if step == 1 else ()
        outs = [shape(low.shape, BF16)] + [shape((rows, cols), F32)] * (step == 1)
        low, *extra = call(
            functools.partial(low_sum_kernel, len(adds)), "low_sum", outs, vmem=(low, other, *adds), after=(sq,)
        )
        if extra:
            (base,) = extra
        step *= 2
    low_last = down_block([last], (sq,), (low,))
    last_parts = [low_last] + [over("tensor", low_last, k) for k in range(n_tensor - 1, 0, -1)]
    ups = up_block(first, [low, other], False, (low_last,))
    deltas = [u if k == 0 else over("wide", u, k) for k, u in zip(first, ups)]
    up, square = up_block([last], last_parts, True, (ups[0],))
    delta = over("wide", up, last)
    total, scale = call(
        functools.partial(gather_kernel, 1 + len(pairs), len(first)),
        "gather",
        [shape((rows, cols), F32), shape((rows, HEAD), F32)],
        vmem=(square, base, *pairs, *deltas, *[sels[k] for k in first]),
        after=(up,),
        flops=2 * rows * cols * HEAD * len(first),
    )
    return call(
        finish_kernel,
        "finish",
        [shape((rows, cols), BF16)],
        vmem=(total, scale, delta, sels[last], cosine, sine),
        flops=2 * rows * cols * HEAD,
    )[0]


def solution(mesh):
    return jax.shard_map(
        functools.partial(local, dict(mesh.shape)),
        mesh=mesh,
        in_specs=(
            P(("parts", "wide"), "tensor"),
            P("tensor"),
            P("tensor", None),
            P(("parts", "wide"), "tensor", None),
            P(("parts", "wide"), None, "tensor"),
            P(("parts", "wide")),
            P("parts"),
            P(("parts", "wide")),
        ),
        out_specs=P(("parts", "wide"), "tensor"),
        check_vma=False,
    )
```

```python
import functools
import math

import jax
import jax.numpy as jnp
from jax import lax
from jax.experimental import pallas as pl
from jax.experimental.pallas import tpu as pltpu
from jax.sharding import PartitionSpec as P

MODEL_WIDTH = 8192
HEAD = 128
EPSILON = 1e-05
ROPE_BASE = 500000.0
F32 = jnp.float32
BF16 = jnp.bfloat16


def iota(shape, axis):
    return lax.broadcasted_iota(jnp.int32, shape, axis)


def call(kernel, name, outs, vmem=(), hbm=(), after=(), scratch=(), flops=0, moved=0, limit=16, hbm_outs=0):
    def body(*refs):
        keep = len(vmem) + len(hbm)
        kernel(*refs[:keep], *refs[keep + len(after) :])

    return pl.pallas_call(
        body,
        out_shape=outs,
        in_specs=[pl.BlockSpec(memory_space=pltpu.VMEM)] * len(vmem)
        + [pl.BlockSpec(memory_space=pltpu.HBM)] * len(hbm)
        + [pl.BlockSpec(memory_space=pl.ANY)] * len(after),
        out_specs=[pl.BlockSpec(memory_space=pltpu.HBM)] * hbm_outs
        + [pl.BlockSpec(memory_space=pltpu.VMEM)] * (len(outs) - hbm_outs),
        scratch_shapes=scratch,
        compiler_params=pltpu.CompilerParams(vmem_limit_bytes=limit * 1024 * 1024),
        cost_estimate=pl.CostEstimate(flops=flops, bytes_accessed=moved, transcendentals=0),
        name=name,
    )(*vmem, *hbm, *after)


def shape(dims, dtype):
    return jax.ShapeDtypeStruct(dims, dtype)


def to_column(row, count):
    spread = iota((count, row.shape[1]), 0) == iota((count, row.shape[1]), 1)
    return jnp.sum(jnp.where(spread, row, 0.0), axis=1, keepdims=True)


def places(req, table, n_wide, per_dev):
    rows = req.shape[1]
    me = lax.axis_index("wide").astype(jnp.int32)
    stored = jnp.zeros_like(req)
    for a in range(table.shape[0]):
        stored = jnp.where(req == a, table[a], stored)
    owner = lax.div(stored, per_dev)
    slot = stored - owner * per_dev
    pad = -(-n_wide // 16) * 16
    hit = owner == (iota((pad, rows), 0) ^ me)
    earlier = (iota((rows, rows), 0) <= iota((rows, rows), 1)).astype(BF16)
    count = jnp.dot(hit.astype(BF16), earlier, preferred_element_type=F32)
    return jnp.where(hit, count.astype(jnp.int32) - 1, -1), slot


def dispatch_kernel(order, n_wide, per_dev, cap, req_hbm, table_hbm, tok_hbm, gain_hbm, *refs):
    xs = refs[: len(order)]
    wide_gain_ref, req_ref, table_ref, tok_ref, gain_ref, x_ref, sems, out_sems = refs[
        len(order) :
    ]
    rows, depth = tok_ref.shape
    height = x_ref.shape[1]
    loads = [
        pltpu.make_async_copy(req_hbm, req_ref, sems.at[0]),
        pltpu.make_async_copy(table_hbm, table_ref, sems.at[1]),
        pltpu.make_async_copy(tok_hbm, tok_ref, sems.at[2]),
        pltpu.make_async_copy(gain_hbm, gain_ref, sems.at[3]),
    ]
    for copy in loads:
        copy.start()
    loads[0].wait()
    loads[1].wait()
    place, slot = places(req_ref[...], table_ref, n_wide, per_dev)
    slots = jnp.broadcast_to(slot.astype(F32), (16, rows)).astype(BF16)
    picks, slot_rows = [], []
    for k in order:
        pick = (iota((HEAD, rows), 0) == place[k : k + 1]).astype(BF16)
        slot_rows.append(
            lax.dot_general(slots, pick, (((1,), (1,)), ((), ())), preferred_element_type=F32)
        )
        picks.append(pick[:height])
    loads[3].wait()
    wide_gain_ref[...] = gain_ref[...].astype(F32)
    loads[2].wait()
    stores = []
    for j, k in enumerate(order):
        y = jnp.dot(picks[j], tok_ref[...], preferred_element_type=F32)
        first = jnp.where(iota((height, HEAD), 0) == cap, slot_rows[j][:1], y[:, :HEAD])
        x_ref[j, :, :HEAD] = first.astype(BF16)
        x_ref[j, :, HEAD:] = y[:, HEAD:].astype(BF16)
        copy = pltpu.make_async_copy(x_ref.at[j], xs[j], out_sems.at[j])
        copy.start()
        stores.append(copy)
    for copy in stores:
        copy.wait()


def base_kernel(offsets, cols, gain_hbm, tok_hbm, weight_hbm, *refs):
    count = len(offsets)
    outs = refs[:count]
    gain_ref, tok_ref, buf, acc_ref, sems = refs[count:]
    steps, chunk, _ = buf.shape
    copies = [
        pltpu.make_async_copy(weight_hbm.at[pl.ds(i * chunk, chunk)], buf.at[i], sems.at[2 + i])
        for i in range(steps)
    ]
    loads = [
        pltpu.make_async_copy(gain_hbm, gain_ref, sems.at[0]),
        pltpu.make_async_copy(tok_hbm, tok_ref, sems.at[1]),
    ]
    for copy in loads + copies:
        copy.start()
    for copy in loads:
        copy.wait()
    spot = lax.axis_index("tensor").astype(jnp.int32)
    for i in range(steps):
        pieces = []
        for b in range(i * chunk // HEAD, (i + 1) * chunk // HEAD):
            piece = tok_ref[:, b * HEAD : (b + 1) * HEAD].astype(F32) * gain_ref[b : b + 1]
            pieces.append(piece.astype(BF16))
        x = jnp.concatenate(pieces, axis=1)
        copies[i].wait()
        for j, k in enumerate(offsets):
            start = pl.multiple_of((spot ^ k) * cols, HEAD)
            y = jnp.dot(x, buf[i, :, pl.ds(start, cols)], preferred_element_type=F32)
            if i > 0:
                y = y + acc_ref[j]
            if i < steps - 1:
                acc_ref[j] = y
            else:
                outs[j][...] = y.astype(outs[j].dtype)


def pair_kernel(count, start, *refs):
    for j in range(count):
        out_ref = refs[2 * count + j]
        rows = slice(start, start + out_ref.shape[0])
        out_ref[...] = (refs[j][rows] + refs[count + j][rows].astype(F32)).astype(BF16)


def scaled_down_kernel(gain_ref, down_hbm, out_ref, buf, sems):
    per_dev, depth, rank = down_hbm.shape
    copies = [pltpu.make_async_copy(down_hbm.at[a], buf.at[a], sems.at[a]) for a in range(per_dev)]
    for copy in copies:
        copy.start()
    columns = []
    for b in range(depth // HEAD):
        columns.append(to_column(gain_ref[b : b + 1], HEAD))
    for a in range(per_dev):
        copies[a].wait()
        for b in range(depth // HEAD):
            span = slice(b * HEAD, (b + 1) * HEAD)
            out_ref[span, a * rank : (a + 1) * rank] = (
                buf[a, span].astype(F32) * columns[b]
            ).astype(BF16)


def aux_kernel(n_wide, per_dev, req_hbm, table_hbm, tok_hbm, sq_ref, *refs):
    sels = refs[:n_wide]
    req_ref, table_ref, tok_ref, sems = refs[n_wide:]
    copies = [
        pltpu.make_async_copy(req_hbm, req_ref, sems.at[0]),
        pltpu.make_async_copy(table_hbm, table_ref, sems.at[1]),
        pltpu.make_async_copy(tok_hbm, tok_ref, sems.at[2]),
    ]
    for copy in copies:
        copy.start()
    for copy in copies:
        copy.wait()
    rows = tok_ref.shape[0]
    place, _ = places(req_ref[...], table_ref, n_wide, per_dev)
    place = place.astype(F32)
    for k in range(n_wide):
        column = to_column(place[k : k + 1], rows).astype(jnp.int32)
        sels[k][...] = (iota((rows, HEAD), 1) == column).astype(BF16)
    tok = tok_ref[...]
    gram = lax.dot_general(tok, tok, (((1,), (1,)), ((), ())), preferred_element_type=F32)
    diag = iota((rows, rows), 0) == iota((rows, rows), 1)
    sq = jnp.sum(jnp.where(diag, gram, 0.0), axis=0, keepdims=True)
    block = jnp.zeros((8, HEAD), F32)
    for p in range(3):
        part = sq.astype(BF16).astype(F32)
        sq = sq - part
        for i in range(rows // HEAD):
            term = part[:, i * HEAD : (i + 1) * HEAD]
            block = jnp.where(iota((8, HEAD), 0) == p * (rows // HEAD) + i, term, block)
    sq_ref[...] = block


def slot_column(x_ref, cap):
    height = x_ref.shape[0]
    base = cap // 16 * 16
    row = x_ref[base : base + 16, :HEAD].astype(F32)[cap - base : cap - base + 1]
    column = to_column(row, height)
    return jnp.where(iota((height, 1), 0) < cap, column, -1.0)


def down_kernel(count, cap, with_sq, *refs):
    xs, down_ref = refs[:count], refs[count]
    sq_ref = refs[count + 1] if with_sq else None
    out_ref = refs[-1]
    height, depth = xs[0].shape
    rank = HEAD
    x = jnp.concatenate([x[...] for x in xs], axis=0) if count > 1 else xs[0][...]
    slot = [slot_column(x, cap) for x in xs]
    slot = jnp.concatenate(slot, axis=0) if count > 1 else slot[0]
    low = jnp.zeros((count * height, rank), F32)
    for g in range(down_ref.shape[1] // (2 * rank)):
        y = jnp.dot(
            x, down_ref[:, 2 * g * rank : 2 * (g + 1) * rank], preferred_element_type=F32
        )
        low = jnp.where(slot == 2 * g, y[:, :rank], low)
        low = jnp.where(slot == 2 * g + 1, y[:, rank:], low)
    for j in range(count):
        part = low[j * height : (j + 1) * height]
        if j == 0 and with_sq:
            tail = [jnp.zeros((cap, rank), F32), sq_ref[...]]
            if height > cap + 8:
                tail.append(jnp.zeros((height - cap - 8, rank), F32))
            part = part + jnp.concatenate(tail, axis=0)
        out_ref[j] = part.astype(BF16)


def low_sum_kernel(left_ref, right_ref, *refs):
    out_ref = refs[len(refs) // 2]
    total = left_ref[...].astype(F32) + right_ref[...].astype(F32)
    out_ref[...] = total.astype(BF16)
    if len(refs) > 1:
        refs[2][...] = refs[0][...]


def head_is_key(heads, h):
    if heads % 2 == 0:
        return h % 2 == 0
    return (lax.axis_index("tensor").astype(jnp.int32) * heads + h) % 2 == 0


def up_kernel(count, n_parts, cap, with_sq, *refs):
    xs = refs[:count]
    parts = refs[count : count + n_parts]
    up_ref = refs[count + n_parts]
    outs = refs[count + n_parts + 1 :]
    per_dev, half, cols = up_ref.shape
    heads = cols // HEAD
    height, rank = parts[0].shape[1:]
    up = up_ref[...].reshape(per_dev * half, cols)
    sums = []
    for j in range(count):
        low = parts[0][j].astype(F32)
        for part in parts[1:]:
            low = low + part[j].astype(F32)
        sums.append(low)
    if with_sq:
        outs[count][...] = sums[0][cap : cap + 8]
    low = jnp.concatenate(sums, axis=0) if count > 1 else sums[0]
    slot = [slot_column(x, cap) for x in xs]
    slot = jnp.concatenate(slot, axis=0) if count > 1 else slot[0]
    left = iota((count * height, rank), 1) < half
    turned = pltpu.roll(low, half, 1)
    wide = []
    for source in (jnp.where(left, low, turned), jnp.where(left, turned, low)):
        pieces = []
        for g in range(per_dev // 2):
            mine = slot == jnp.where(left, 2.0 * g, 2.0 * g + 1)
            pieces.append(jnp.where(mine, source, 0.0).astype(BF16))
        wide.append(jnp.concatenate(pieces, axis=1))
    for h in range(heads):
        key = head_is_key(heads, h)
        if isinstance(key, bool):
            lhs = wide[0] if key else wide[1]
        else:
            lhs = jnp.where(key, wide[0].astype(F32), wide[1].astype(F32)).astype(BF16)
        span = slice(h * HEAD, (h + 1) * HEAD)
        y = jnp.dot(lhs, up[:, span], preferred_element_type=F32).astype(BF16)
        for j in range(count):
            outs[j][:, span] = y[j * height : (j + 1) * height]


def placed(sels, deltas):
    height, cols = deltas[0].shape
    blocks = []
    for delta in deltas:
        blocks.append(delta[...])
        if height < HEAD:
            blocks.append(jnp.zeros((HEAD - height, cols), BF16))
    lhs = jnp.concatenate([sel[...] for sel in sels], axis=1) if len(sels) > 1 else sels[0][...]
    return jnp.dot(lhs, jnp.concatenate(blocks, axis=0), preferred_element_type=F32)


def base_sum_kernel(n_pairs, base_ref, *refs):
    out_ref = refs[n_pairs]
    half = refs[0].shape[0] if n_pairs else 0
    out_ref[...] = base_ref[...]
    for top in refs[:n_pairs]:
        out_ref[:half] += top[...].astype(F32)


def gather_kernel(n_pairs, count, sq_ref, base_ref, near_ref, *refs):
    bottoms = refs[:n_pairs]
    deltas = refs[n_pairs : n_pairs + count]
    sels = refs[n_pairs + count : n_pairs + 2 * count]
    out_ref, scale_ref = refs[-2:]
    rows, cols = out_ref.shape
    pieces = rows // HEAD
    squares = []
    for i in range(pieces):
        total = sq_ref[i : i + 1]
        for p in range(1, 3):
            total = total + sq_ref[p * pieces + i : p * pieces + i + 1]
        squares.append(total)
    square = to_column(jnp.concatenate(squares, axis=1), rows)
    scale = lax.rsqrt(square * (1.0 / MODEL_WIDTH) + EPSILON)
    scale_ref[...] = jnp.broadcast_to(scale, (rows, HEAD))
    total = base_ref[...] + near_ref[...].astype(F32) + placed(sels, deltas)
    if bottoms:
        half = rows - bottoms[0].shape[0]
        lower = total[half:]
        for bottom in bottoms:
            lower = lower + bottom[...].astype(F32)
        out_ref[:half] = total[:half]
        out_ref[half:] = lower
    else:
        out_ref[...] = total


def finish_kernel(count, sum_ref, scale_ref, cos_ref, sin_ref, *refs):
    deltas, sels, out_ref = refs[:count], refs[count : 2 * count], refs[2 * count]
    rows, cols = out_ref.shape
    total = sum_ref[...] + placed(sels, deltas)
    heads = cols // HEAD
    scale = scale_ref[...]
    for h in range(heads):
        span = slice(h * HEAD, (h + 1) * HEAD)
        x = total[:, span] * scale
        key = head_is_key(heads, h)
        if key is False:
            out_ref[:, span] = x.astype(BF16)
            continue
        y = x * cos_ref[...] + pltpu.roll(x, HEAD // 2, 1) * sin_ref[...]
        if key is not True:
            y = jnp.where(key, y, x)
        out_ref[:, span] = y.astype(BF16)


def local(
    mesh_shape,
    tokens,
    attention_norm_gain,
    key_value_weight,
    adapter_down_weight,
    adapter_up_weight,
    request_adapter,
    adapter_storage_row,
    cached_token_length,
):
    n_wide, n_tensor = mesh_shape["wide"], mesh_shape["tensor"]
    rows, depth = tokens.shape
    per_dev, _, rank = adapter_down_weight.shape
    cols = adapter_up_weight.shape[2]
    cap = 104 if n_wide <= 4 else 64
    height = -(-(cap + 8) // 16) * 16
    req = request_adapter.reshape(1, rows)
    gain = attention_norm_gain.reshape(depth // HEAD, HEAD)

    def over(axis, array, k):
        size = mesh_shape[axis]
        return lax.ppermute(array, axis, [(i, i ^ k) for i in range(size)])

    small = [pltpu.VMEM((1, rows), jnp.int32), pltpu.SMEM(adapter_storage_row.shape, jnp.int32)]
    first, last = [0, 1], list(range(2, n_wide))

    def dispatch(order, after):
        *blocks, wide_gain = call(
            functools.partial(dispatch_kernel, order, n_wide, per_dev, cap),
            "dispatch",
            [shape((height, depth), BF16)] * len(order) + [shape(gain.shape, F32)],
            hbm=(req, adapter_storage_row, tokens, gain),
            hbm_outs=len(order),
            after=after,
            scratch=small
            + [
                pltpu.VMEM((rows, depth), BF16),
                pltpu.VMEM(gain.shape, BF16),
                pltpu.VMEM((len(order), height, depth), BF16),
                pltpu.SemaphoreType.DMA((4,)),
                pltpu.SemaphoreType.DMA((len(order),)),
            ],
            flops=2 * len(order) * height * rows * depth,
            moved=2 * rows * depth * 4,
            limit=63,
        )
        return blocks, wide_gain

    order = list(range(n_wide - 1, -1, -1))
    blocks, wide_gain = dispatch(order, ())
    held = [blocks[n_wide - 1 - k] for k in range(n_wide)]
    held[1:] = [over("wide", held[k], k) for k in range(1, n_wide)]

    twos = list(range(2, n_tensor, 2))
    far = [k ^ 1 for k in twos]
    offsets = far + [1] + twos + [0]
    chunk = math.gcd(depth, 512)
    steps = depth // chunk
    sums = call(
        functools.partial(base_kernel, offsets, cols),
        "base",
        [shape((rows, cols), BF16)] * (len(far) + 1) + [shape((rows, cols), F32)] * (len(twos) + 1),
        hbm=(wide_gain, tokens, key_value_weight),
        scratch=[
            pltpu.VMEM(gain.shape, F32),
            pltpu.VMEM((rows, depth), BF16),
            pltpu.VMEM((steps, chunk, key_value_weight.shape[1]), BF16),
            pltpu.VMEM((len(offsets), rows, cols), F32),
            pltpu.SemaphoreType.DMA((2 + steps,)),
        ],
        flops=2 * rows * depth * cols * n_tensor,
        moved=2 * depth * cols * n_tensor,
        limit=52,
    )
    away, near, own, base = sums[: len(far)], sums[len(far)], sums[len(far) + 1 : -1], sums[-1]
    beside = [over("tensor", p, 1) for p in away]
    (down,) = call(
        scaled_down_kernel,
        "scaled_down",
        [shape((depth, per_dev * rank), BF16)],
        vmem=(wide_gain,),
        hbm=(adapter_down_weight,),
        after=(base,),
        scratch=[
            pltpu.VMEM((per_dev, depth, rank), BF16),
            pltpu.SemaphoreType.DMA((per_dev,)),
        ],
        flops=4 * depth * per_dev * rank,
        moved=4 * depth * per_dev * rank,
    )
    half_size = HEAD // 2
    freq_index = jnp.arange(half_size).astype(F32)
    inverse = jnp.exp(freq_index * (-2.0 / HEAD) * math.log(ROPE_BASE))
    angles = cached_token_length.astype(F32)[:, None] * inverse[None, :]
    cosine, sine = jnp.cos(angles), jnp.sin(angles)
    cosine = jnp.concatenate([cosine, cosine], axis=1)
    sine = jnp.concatenate([-sine, sine], axis=1)

    def pair_sums(start, after):
        pairs = call(
            functools.partial(pair_kernel, len(twos), start),
            "pair_sums",
            [shape((rows // 2, cols), BF16)] * len(twos),
            vmem=(*own, *beside),
            after=after,
            moved=4 * rows * cols * len(twos),
        )
        return pairs[-1], [over("tensor", p, k) for p, k in zip(pairs, twos)]

    def down_block(group, extra, after):
        xs = [held[k] for k in group]
        (low,) = call(
            functools.partial(down_kernel, len(xs), cap, bool(extra)),
            "down_block",
            [shape((len(xs), height, rank), BF16)],
            vmem=(*xs, down, *extra),
            after=after,
            flops=2 * len(xs) * height * depth * rank * per_dev,
            moved=2 * per_dev * depth * rank,
        )
        return low

    def up_block(group, parts, with_sq, after):
        xs = [held[k] for k in group]
        outs = [shape((height, cols), BF16)] * len(xs)
        if with_sq:
            outs = outs + [shape((8, HEAD), F32)]
        return call(
            functools.partial(up_kernel, len(xs), len(parts), cap, with_sq),
            "up_block",
            outs,
            vmem=(*xs, *parts, adapter_up_weight),
            after=after,
            flops=2 * len(xs) * height * per_dev * rank * cols,
            moved=2 * per_dev * rank * cols,
        )

    low = down_block(first, (), ())
    sq, *sels = call(
        functools.partial(aux_kernel, n_wide, per_dev),
        "aux",
        [shape((8, HEAD), F32)] + [shape((rows, HEAD), BF16)] * n_wide,
        hbm=(req, adapter_storage_row, tokens),
        after=(low,),
        scratch=small + [pltpu.VMEM((rows, depth), BF16), pltpu.SemaphoreType.DMA((3,))],
        flops=2 * rows * rows * depth,
        moved=2 * rows * depth,
    )
    pair, tops = pair_sums(0, (sq, cosine, sine))
    step = 1
    while True:
        other = over("tensor", low, step)
        if step * 2 >= n_tensor:
            break
        more = (near,) if step == 1 else ()
        low, *handed = call(
            low_sum_kernel,
            "low_sum",
            [shape(low.shape, BF16)] + [shape((rows, cols), BF16)] * len(more),
            vmem=(low, other, *more),
            after=(pair,),
        )
        if handed:
            near = over("tensor", handed[0], 1)
        step *= 2
    (base,) = call(
        functools.partial(base_sum_kernel, len(tops)),
        "base_sum",
        [shape((rows, cols), F32)],
        vmem=(base, *tops),
        after=(low,),
    )
    low_last = down_block(last, (sq,), (base,))
    last_parts = [low_last] + [over("tensor", low_last, k) for k in range(n_tensor - 1, 0, -1)]
    ups = up_block(first, [low, other], False, (low_last,))
    deltas = [u if k == 0 else over("wide", u, k) for k, u in zip(first, ups)]
    pair, bottoms = pair_sums(rows // 2, (ups[0],))
    *ups, square = up_block(last, last_parts, True, (pair,))
    last_deltas = [over("wide", u, k) for k, u in zip(last, ups)]
    total, scale = call(
        functools.partial(gather_kernel, len(bottoms), len(first)),
        "gather",
        [shape((rows, cols), F32), shape((rows, HEAD), F32)],
        vmem=(square, base, near, *bottoms, *deltas, *[sels[k] for k in first]),
        after=(ups[0],),
        flops=2 * rows * cols * HEAD * len(first),
    )
    return call(
        functools.partial(finish_kernel, len(last)),
        "finish",
        [shape((rows, cols), BF16)],
        vmem=(total, scale, cosine, sine, *last_deltas, *[sels[k] for k in last]),
        flops=2 * rows * cols * HEAD,
    )[0]


def solution(mesh):
    return jax.shard_map(
        functools.partial(local, dict(mesh.shape)),
        mesh=mesh,
        in_specs=(
            P(("parts", "wide"), "tensor"),
            P("tensor"),
            P("tensor", None),
            P(("parts", "wide"), "tensor", None),
            P(("parts", "wide"), None, "tensor"),
            P(("parts", "wide")),
            P("parts"),
            P(("parts", "wide")),
        ),
        out_specs=P(("parts", "wide"), "tensor"),
        check_vma=False,
    )
```

```python
import functools
import math

import jax
import jax.numpy as jnp
from jax import lax
from jax.experimental import pallas as pl
from jax.experimental.pallas import tpu as pltpu
from jax.sharding import PartitionSpec as P

MODEL_WIDTH = 8192
HEAD = 128
EPSILON = 1e-05
ROPE_BASE = 500000.0
F32 = jnp.float32
BF16 = jnp.bfloat16


def iota(shape, axis):
    return lax.broadcasted_iota(jnp.int32, shape, axis)


def call(kernel, name, outs, vmem=(), hbm=(), after=(), scratch=(), flops=0, moved=0, limit=16, hbm_outs=0):
    def body(*refs):
        keep = len(vmem) + len(hbm)
        kernel(*refs[:keep], *refs[keep + len(after) :])

    return pl.pallas_call(
        body,
        out_shape=outs,
        in_specs=[pl.BlockSpec(memory_space=pltpu.VMEM)] * len(vmem)
        + [pl.BlockSpec(memory_space=pltpu.HBM)] * len(hbm)
        + [pl.BlockSpec(memory_space=pl.ANY)] * len(after),
        out_specs=[pl.BlockSpec(memory_space=pltpu.HBM)] * hbm_outs
        + [pl.BlockSpec(memory_space=pltpu.VMEM)] * (len(outs) - hbm_outs),
        scratch_shapes=scratch,
        compiler_params=pltpu.CompilerParams(vmem_limit_bytes=limit * 1024 * 1024),
        cost_estimate=pl.CostEstimate(flops=flops, bytes_accessed=moved, transcendentals=0),
        name=name,
    )(*vmem, *hbm, *after)


def shape(dims, dtype):
    return jax.ShapeDtypeStruct(dims, dtype)


def to_column(row, count):
    spread = iota((count, row.shape[1]), 0) == iota((count, row.shape[1]), 1)
    return jnp.sum(jnp.where(spread, row, 0.0), axis=1, keepdims=True)


def places(req, table, n_wide, per_dev):
    rows = req.shape[1]
    me = lax.axis_index("wide").astype(jnp.int32)
    stored = jnp.zeros_like(req)
    for a in range(table.shape[0]):
        stored = jnp.where(req == a, table[a], stored)
    owner = lax.div(stored, per_dev)
    slot = stored - owner * per_dev
    pad = -(-n_wide // 16) * 16
    hit = owner == (iota((pad, rows), 0) ^ me)
    earlier = (iota((rows, rows), 0) <= iota((rows, rows), 1)).astype(BF16)
    count = jnp.dot(hit.astype(BF16), earlier, preferred_element_type=F32)
    return jnp.where(hit, count.astype(jnp.int32) - 1, -1), slot


def dispatch_kernel(order, n_wide, per_dev, cap, req_hbm, table_hbm, tok_hbm, gain_hbm, *refs):
    xs = refs[: len(order)]
    wide_gain_ref, req_ref, table_ref, tok_ref, gain_ref, x_ref, sems, out_sems = refs[
        len(order) :
    ]
    rows, depth = tok_ref.shape
    height = x_ref.shape[1]
    loads = [
        pltpu.make_async_copy(req_hbm, req_ref, sems.at[0]),
        pltpu.make_async_copy(table_hbm, table_ref, sems.at[1]),
        pltpu.make_async_copy(tok_hbm, tok_ref, sems.at[2]),
        pltpu.make_async_copy(gain_hbm, gain_ref, sems.at[3]),
    ]
    for copy in loads:
        copy.start()
    loads[0].wait()
    loads[1].wait()
    place, slot = places(req_ref[...], table_ref, n_wide, per_dev)
    slots = jnp.broadcast_to(slot.astype(F32), (16, rows)).astype(BF16)
    picks, slot_rows = [], []
    for k in order:
        pick = (iota((HEAD, rows), 0) == place[k : k + 1]).astype(BF16)
        slot_rows.append(
            lax.dot_general(slots, pick, (((1,), (1,)), ((), ())), preferred_element_type=F32)
        )
        picks.append(pick[:height])
    loads[3].wait()
    wide_gain_ref[...] = gain_ref[...].astype(F32)
    loads[2].wait()
    stores = []
    for j, k in enumerate(order):
        y = jnp.dot(picks[j], tok_ref[...], preferred_element_type=F32)
        first = jnp.where(iota((height, HEAD), 0) == cap, slot_rows[j][:1], y[:, :HEAD])
        x_ref[j, :, :HEAD] = first.astype(BF16)
        x_ref[j, :, HEAD:] = y[:, HEAD:].astype(BF16)
        copy = pltpu.make_async_copy(x_ref.at[j], xs[j], out_sems.at[j])
        copy.start()
        stores.append(copy)
    for copy in stores:
        copy.wait()


def base_kernel(offsets, cols, gain_hbm, tok_hbm, weight_hbm, *refs):
    count = len(offsets)
    outs = refs[:count]
    gain_ref, tok_ref, buf, acc_ref, sems = refs[count:]
    steps, chunk, _ = buf.shape
    copies = [
        pltpu.make_async_copy(weight_hbm.at[pl.ds(i * chunk, chunk)], buf.at[i], sems.at[2 + i])
        for i in range(steps)
    ]
    loads = [
        pltpu.make_async_copy(gain_hbm, gain_ref, sems.at[0]),
        pltpu.make_async_copy(tok_hbm, tok_ref, sems.at[1]),
    ]
    for copy in loads + copies:
        copy.start()
    for copy in loads:
        copy.wait()
    spot = lax.axis_index("tensor").astype(jnp.int32)
    for i in range(steps):
        pieces = []
        for b in range(i * chunk // HEAD, (i + 1) * chunk // HEAD):
            piece = tok_ref[:, b * HEAD : (b + 1) * HEAD].astype(F32) * gain_ref[b : b + 1]
            pieces.append(piece.astype(BF16))
        x = jnp.concatenate(pieces, axis=1)
        copies[i].wait()
        for j, k in enumerate(offsets):
            start = pl.multiple_of((spot ^ k) * cols, HEAD)
            y = jnp.dot(x, buf[i, :, pl.ds(start, cols)], preferred_element_type=F32)
            if i > 0:
                y = y + acc_ref[j]
            if i < steps - 1:
                acc_ref[j] = y
            else:
                outs[j][...] = y.astype(outs[j].dtype)


def pair_kernel(count, start, *refs):
    for j in range(count):
        out_ref = refs[2 * count + j]
        rows = slice(start, start + out_ref.shape[0])
        out_ref[...] = (refs[j][rows] + refs[count + j][rows].astype(F32)).astype(BF16)


def scaled_down_kernel(gain_ref, down_hbm, out_ref, buf, sems):
    per_dev, depth, rank = down_hbm.shape
    copies = [pltpu.make_async_copy(down_hbm.at[a], buf.at[a], sems.at[a]) for a in range(per_dev)]
    for copy in copies:
        copy.start()
    columns = []
    for b in range(depth // HEAD):
        columns.append(to_column(gain_ref[b : b + 1], HEAD))
    for a in range(per_dev):
        copies[a].wait()
        for b in range(depth // HEAD):
            span = slice(b * HEAD, (b + 1) * HEAD)
            out_ref[span, a * rank : (a + 1) * rank] = (
                buf[a, span].astype(F32) * columns[b]
            ).astype(BF16)


def aux_kernel(n_wide, per_dev, req_hbm, table_hbm, tok_hbm, sq_ref, *refs):
    sels = refs[:n_wide]
    req_ref, table_ref, tok_ref, sems = refs[n_wide:]
    copies = [
        pltpu.make_async_copy(req_hbm, req_ref, sems.at[0]),
        pltpu.make_async_copy(table_hbm, table_ref, sems.at[1]),
        pltpu.make_async_copy(tok_hbm, tok_ref, sems.at[2]),
    ]
    for copy in copies:
        copy.start()
    for copy in copies:
        copy.wait()
    rows = tok_ref.shape[0]
    place, _ = places(req_ref[...], table_ref, n_wide, per_dev)
    place = place.astype(F32)
    for k in range(n_wide):
        column = to_column(place[k : k + 1], rows).astype(jnp.int32)
        sels[k][...] = (iota((rows, HEAD), 1) == column).astype(BF16)
    tok = tok_ref[...]
    gram = lax.dot_general(tok, tok, (((1,), (1,)), ((), ())), preferred_element_type=F32)
    diag = iota((rows, rows), 0) == iota((rows, rows), 1)
    sq = jnp.sum(jnp.where(diag, gram, 0.0), axis=0, keepdims=True)
    block = jnp.zeros((8, HEAD), F32)
    for p in range(3):
        part = sq.astype(BF16).astype(F32)
        sq = sq - part
        for i in range(rows // HEAD):
            term = part[:, i * HEAD : (i + 1) * HEAD]
            block = jnp.where(iota((8, HEAD), 0) == p * (rows // HEAD) + i, term, block)
    sq_ref[...] = block


def slot_column(x_ref, cap):
    height = x_ref.shape[0]
    base = cap // 16 * 16
    row = x_ref[base : base + 16, :HEAD].astype(F32)[cap - base : cap - base + 1]
    column = to_column(row, height)
    return jnp.where(iota((height, 1), 0) < cap, column, -1.0)


def down_kernel(count, cap, with_sq, *refs):
    xs, down_ref = refs[:count], refs[count]
    sq_ref = refs[count + 1] if with_sq else None
    out_ref = refs[-1]
    height, depth = xs[0].shape
    rank = HEAD
    x = jnp.concatenate([x[...] for x in xs], axis=0) if count > 1 else xs[0][...]
    slot = [slot_column(x, cap) for x in xs]
    slot = jnp.concatenate(slot, axis=0) if count > 1 else slot[0]
    low = jnp.zeros((count * height, rank), F32)
    for g in range(down_ref.shape[1] // (2 * rank)):
        y = jnp.dot(
            x, down_ref[:, 2 * g * rank : 2 * (g + 1) * rank], preferred_element_type=F32
        )
        low = jnp.where(slot == 2 * g, y[:, :rank], low)
        low = jnp.where(slot == 2 * g + 1, y[:, rank:], low)
    for j in range(count):
        part = low[j * height : (j + 1) * height]
        if j == 0 and with_sq:
            tail = [jnp.zeros((cap, rank), F32), sq_ref[...]]
            if height > cap + 8:
                tail.append(jnp.zeros((height - cap - 8, rank), F32))
            part = part + jnp.concatenate(tail, axis=0)
        for i in range(j, out_ref.shape[0], count):
            out_ref[i] = part.astype(BF16)


def low_sum_kernel(left_ref, right_ref, *refs):
    out_ref = refs[len(refs) // 2]
    total = left_ref[...].astype(F32) + right_ref[...].astype(F32)
    out_ref[...] = total.astype(BF16)
    if len(refs) > 1:
        refs[2][...] = refs[0][...]


def head_is_key(heads, h):
    if heads % 2 == 0:
        return h % 2 == 0
    return (lax.axis_index("tensor").astype(jnp.int32) * heads + h) % 2 == 0


def up_kernel(count, n_parts, cap, with_sq, *refs):
    xs = refs[:count]
    parts = refs[count : count + n_parts]
    up_ref = refs[count + n_parts]
    outs = refs[count + n_parts + 1 :]
    per_dev, half, cols = up_ref.shape
    heads = cols // HEAD
    height, rank = parts[0].shape[1:]
    up = up_ref[...].reshape(per_dev * half, cols)
    sums = []
    for j in range(count):
        terms = [part[i].astype(F32) for part in parts for i in range(j, part.shape[0], count)]
        sums.append(sum(terms[1:], terms[0]))
    if with_sq:
        outs[count][...] = sums[0][cap : cap + 8]
    low = jnp.concatenate(sums, axis=0) if count > 1 else sums[0]
    slot = [slot_column(x, cap) for x in xs]
    slot = jnp.concatenate(slot, axis=0) if count > 1 else slot[0]
    left = iota((count * height, rank), 1) < half
    turned = pltpu.roll(low, half, 1)
    wide = []
    for source in (jnp.where(left, low, turned), jnp.where(left, turned, low)):
        pieces = []
        for g in range(per_dev // 2):
            mine = slot == jnp.where(left, 2.0 * g, 2.0 * g + 1)
            pieces.append(jnp.where(mine, source, 0.0).astype(BF16))
        wide.append(jnp.concatenate(pieces, axis=1))
    for h in range(heads):
        key = head_is_key(heads, h)
        if isinstance(key, bool):
            lhs = wide[0] if key else wide[1]
        else:
            lhs = jnp.where(key, wide[0].astype(F32), wide[1].astype(F32)).astype(BF16)
        span = slice(h * HEAD, (h + 1) * HEAD)
        y = jnp.dot(lhs, up[:, span], preferred_element_type=F32).astype(BF16)
        for j in range(count):
            outs[j][:, span] = y[j * height : (j + 1) * height]


def placed(sels, deltas):
    height, cols = deltas[0].shape
    blocks = []
    for delta in deltas:
        blocks.append(delta[...])
        if height < HEAD:
            blocks.append(jnp.zeros((HEAD - height, cols), BF16))
    lhs = jnp.concatenate([sel[...] for sel in sels], axis=1) if len(sels) > 1 else sels[0][...]
    return jnp.dot(lhs, jnp.concatenate(blocks, axis=0), preferred_element_type=F32)


def base_sum_kernel(n_pairs, base_ref, *refs):
    out_ref = refs[n_pairs]
    half = refs[0].shape[0] if n_pairs else 0
    out_ref[...] = base_ref[...]
    for top in refs[:n_pairs]:
        out_ref[:half] += top[...].astype(F32)


def gather_kernel(n_pairs, count, sq_ref, base_ref, near_ref, *refs):
    bottoms = refs[:n_pairs]
    deltas = refs[n_pairs : n_pairs + count]
    sels = refs[n_pairs + count : n_pairs + 2 * count]
    out_ref, scale_ref = refs[-2:]
    rows, cols = out_ref.shape
    pieces = rows // HEAD
    squares = []
    for i in range(pieces):
        total = sq_ref[i : i + 1]
        for p in range(1, 3):
            total = total + sq_ref[p * pieces + i : p * pieces + i + 1]
        squares.append(total)
    square = to_column(jnp.concatenate(squares, axis=1), rows)
    scale = lax.rsqrt(square * (1.0 / MODEL_WIDTH) + EPSILON)
    scale_ref[...] = jnp.broadcast_to(scale, (rows, HEAD))
    total = base_ref[...] + near_ref[...].astype(F32) + placed(sels, deltas)
    if bottoms:
        half = rows - bottoms[0].shape[0]
        lower = total[half:]
        for bottom in bottoms:
            lower = lower + bottom[...].astype(F32)
        out_ref[:half] = total[:half]
        out_ref[half:] = lower
    else:
        out_ref[...] = total


def finish_kernel(count, sum_ref, scale_ref, cos_ref, sin_ref, *refs):
    deltas, sels, out_ref = refs[:count], refs[count : 2 * count], refs[2 * count]
    rows, cols = out_ref.shape
    total = sum_ref[...] + placed(sels, deltas)
    heads = cols // HEAD
    scale = scale_ref[...]
    for h in range(heads):
        span = slice(h * HEAD, (h + 1) * HEAD)
        x = total[:, span] * scale
        key = head_is_key(heads, h)
        if key is False:
            out_ref[:, span] = x.astype(BF16)
            continue
        y = x * cos_ref[...] + pltpu.roll(x, HEAD // 2, 1) * sin_ref[...]
        if key is not True:
            y = jnp.where(key, y, x)
        out_ref[:, span] = y.astype(BF16)


def local(
    mesh_shape,
    tokens,
    attention_norm_gain,
    key_value_weight,
    adapter_down_weight,
    adapter_up_weight,
    request_adapter,
    adapter_storage_row,
    cached_token_length,
):
    n_wide, n_tensor = mesh_shape["wide"], mesh_shape["tensor"]
    rows, depth = tokens.shape
    per_dev, _, rank = adapter_down_weight.shape
    cols = adapter_up_weight.shape[2]
    cap = 104 if n_wide <= 4 else 64
    height = -(-(cap + 8) // 16) * 16
    req = request_adapter.reshape(1, rows)
    gain = attention_norm_gain.reshape(depth // HEAD, HEAD)

    def over(axis, array, k):
        size = mesh_shape[axis]
        return lax.ppermute(array, axis, [(i, i ^ k) for i in range(size)])

    small = [pltpu.VMEM((1, rows), jnp.int32), pltpu.SMEM(adapter_storage_row.shape, jnp.int32)]
    first, last = [0, 1], list(range(2, n_wide))

    def dispatch(order, after):
        *blocks, wide_gain = call(
            functools.partial(dispatch_kernel, order, n_wide, per_dev, cap),
            "dispatch",
            [shape((height, depth), BF16)] * len(order) + [shape(gain.shape, F32)],
            hbm=(req, adapter_storage_row, tokens, gain),
            hbm_outs=len(order),
            after=after,
            scratch=small
            + [
                pltpu.VMEM((rows, depth), BF16),
                pltpu.VMEM(gain.shape, BF16),
                pltpu.VMEM((len(order), height, depth), BF16),
                pltpu.SemaphoreType.DMA((4,)),
                pltpu.SemaphoreType.DMA((len(order),)),
            ],
            flops=2 * len(order) * height * rows * depth,
            moved=2 * rows * depth * 4,
            limit=63,
        )
        return blocks, wide_gain

    order = list(range(n_wide - 1, -1, -1))
    blocks, wide_gain = dispatch(order, ())
    held = [blocks[n_wide - 1 - k] for k in range(n_wide)]
    held[1:] = [over("wide", held[k], k) for k in range(1, n_wide)]

    twos = list(range(2, n_tensor, 2))
    far = [k ^ 1 for k in twos]
    offsets = far + [1] + twos + [0]
    chunk = math.gcd(depth, 512)
    steps = depth // chunk
    sums = call(
        functools.partial(base_kernel, offsets, cols),
        "base",
        [shape((rows, cols), BF16)] * (len(far) + 1) + [shape((rows, cols), F32)] * (len(twos) + 1),
        hbm=(wide_gain, tokens, key_value_weight),
        scratch=[
            pltpu.VMEM(gain.shape, F32),
            pltpu.VMEM((rows, depth), BF16),
            pltpu.VMEM((steps, chunk, key_value_weight.shape[1]), BF16),
            pltpu.VMEM((len(offsets), rows, cols), F32),
            pltpu.SemaphoreType.DMA((2 + steps,)),
        ],
        flops=2 * rows * depth * cols * n_tensor,
        moved=2 * depth * cols * n_tensor,
        limit=52,
    )
    away, near, own, base = sums[: len(far)], sums[len(far)], sums[len(far) + 1 : -1], sums[-1]
    beside = [over("tensor", p, 1) for p in away]
    (down,) = call(
        scaled_down_kernel,
        "scaled_down",
        [shape((depth, per_dev * rank), BF16)],
        vmem=(wide_gain,),
        hbm=(adapter_down_weight,),
        after=(base,),
        scratch=[
            pltpu.VMEM((per_dev, depth, rank), BF16),
            pltpu.SemaphoreType.DMA((per_dev,)),
        ],
        flops=4 * depth * per_dev * rank,
        moved=4 * depth * per_dev * rank,
    )
    half_size = HEAD // 2
    freq_index = jnp.arange(half_size).astype(F32)
    inverse = jnp.exp(freq_index * (-2.0 / HEAD) * math.log(ROPE_BASE))
    angles = cached_token_length.astype(F32)[:, None] * inverse[None, :]
    cosine, sine = jnp.cos(angles), jnp.sin(angles)
    cosine = jnp.concatenate([cosine, cosine], axis=1)
    sine = jnp.concatenate([-sine, sine], axis=1)

    def pair_sums(start, after):
        pairs = call(
            functools.partial(pair_kernel, len(twos), start),
            "pair_sums",
            [shape((rows // 2, cols), BF16)] * len(twos),
            vmem=(*own, *beside),
            after=after,
            moved=4 * rows * cols * len(twos),
        )
        return pairs[-1], [over("tensor", p, k) for p, k in zip(pairs, twos)]

    def down_block(group, extra, after, copies=1):
        xs = [held[k] for k in group]
        (low,) = call(
            functools.partial(down_kernel, len(xs), cap, bool(extra)),
            "down_block",
            [shape((copies * len(xs), height, rank), BF16)],
            vmem=(*xs, down, *extra),
            after=after,
            flops=2 * len(xs) * height * depth * rank * per_dev,
            moved=2 * per_dev * depth * rank,
        )
        return low

    def up_block(group, parts, with_sq, after):
        xs = [held[k] for k in group]
        outs = [shape((height, cols), BF16)] * len(xs)
        if with_sq:
            outs = outs + [shape((8, HEAD), F32)]
        return call(
            functools.partial(up_kernel, len(xs), len(parts), cap, with_sq),
            "up_block",
            outs,
            vmem=(*xs, *parts, adapter_up_weight),
            after=after,
            flops=2 * len(xs) * height * per_dev * rank * cols,
            moved=2 * per_dev * rank * cols,
        )

    low = down_block(first, (), ())
    sq, *sels = call(
        functools.partial(aux_kernel, n_wide, per_dev),
        "aux",
        [shape((8, HEAD), F32)] + [shape((rows, HEAD), BF16)] * n_wide,
        hbm=(req, adapter_storage_row, tokens),
        after=(low,),
        scratch=small + [pltpu.VMEM((rows, depth), BF16), pltpu.SemaphoreType.DMA((3,))],
        flops=2 * rows * rows * depth,
        moved=2 * rows * depth,
    )
    pair, tops = pair_sums(0, (sq, cosine, sine))
    step = 1
    while True:
        other = over("tensor", low, step)
        if step * 2 >= n_tensor:
            break
        more = (near,) if step == 1 else ()
        low, *handed = call(
            low_sum_kernel,
            "low_sum",
            [shape(low.shape, BF16)] + [shape((rows, cols), BF16)] * len(more),
            vmem=(low, other, *more),
            after=(pair,),
        )
        if handed:
            near = over("tensor", handed[0], 1)
        step *= 2
    (base,) = call(
        functools.partial(base_sum_kernel, len(tops)),
        "base_sum",
        [shape((rows, cols), F32)],
        vmem=(base, *tops),
        after=(low,),
    )
    low_last = down_block(last, (sq,), (base,), n_tensor)
    last_parts = [lax.all_to_all(low_last, "tensor", 0, 0, tiled=True)]
    ups = up_block(first, [low, other], False, (last_parts[0],))
    deltas = [u if k == 0 else over("wide", u, k) for k, u in zip(first, ups)]
    pair, bottoms = pair_sums(rows // 2, (ups[0],))
    *ups, square = up_block(last, last_parts, True, (pair,))
    last_deltas = [over("wide", u, k) for k, u in zip(last, ups)]
    total, scale = call(
        functools.partial(gather_kernel, len(bottoms), len(first)),
        "gather",
        [shape((rows, cols), F32), shape((rows, HEAD), F32)],
        vmem=(square, base, near, *bottoms, *deltas, *[sels[k] for k in first]),
        after=(ups[0],),
        flops=2 * rows * cols * HEAD * len(first),
    )
    return call(
        functools.partial(finish_kernel, len(last)),
        "finish",
        [shape((rows, cols), BF16)],
        vmem=(total, scale, cosine, sine, *last_deltas, *[sels[k] for k in last]),
        flops=2 * rows * cols * HEAD,
    )[0]


def solution(mesh):
    return jax.shard_map(
        functools.partial(local, dict(mesh.shape)),
        mesh=mesh,
        in_specs=(
            P(("parts", "wide"), "tensor"),
            P("tensor"),
            P("tensor", None),
            P(("parts", "wide"), "tensor", None),
            P(("parts", "wide"), None, "tensor"),
            P(("parts", "wide")),
            P("parts"),
            P(("parts", "wide")),
        ),
        out_specs=P(("parts", "wide"), "tensor"),
        check_vma=False,
    )
```

```python
import functools
import math

import jax
import jax.numpy as jnp
from jax import lax
from jax.experimental import pallas as pl
from jax.experimental.pallas import tpu as pltpu
from jax.sharding import PartitionSpec as P

MODEL_WIDTH = 8192
HEAD = 128
EPSILON = 1e-05
ROPE_BASE = 500000.0
F32 = jnp.float32
BF16 = jnp.bfloat16


def iota(shape, axis):
    return lax.broadcasted_iota(jnp.int32, shape, axis)


def call(kernel, name, outs, vmem=(), hbm=(), after=(), scratch=(), flops=0, moved=0, limit=16, hbm_outs=0):
    def body(*refs):
        keep = len(vmem) + len(hbm)
        kernel(*refs[:keep], *refs[keep + len(after) :])

    return pl.pallas_call(
        body,
        out_shape=outs,
        in_specs=[pl.BlockSpec(memory_space=pltpu.VMEM)] * len(vmem)
        + [pl.BlockSpec(memory_space=pltpu.HBM)] * len(hbm)
        + [pl.BlockSpec(memory_space=pl.ANY)] * len(after),
        out_specs=[pl.BlockSpec(memory_space=pltpu.HBM)] * hbm_outs
        + [pl.BlockSpec(memory_space=pltpu.VMEM)] * (len(outs) - hbm_outs),
        scratch_shapes=scratch,
        compiler_params=pltpu.CompilerParams(vmem_limit_bytes=limit * 1024 * 1024),
        cost_estimate=pl.CostEstimate(flops=flops, bytes_accessed=moved, transcendentals=0),
        name=name,
    )(*vmem, *hbm, *after)


def shape(dims, dtype):
    return jax.ShapeDtypeStruct(dims, dtype)


def to_column(row, count):
    spread = iota((count, row.shape[1]), 0) == iota((count, row.shape[1]), 1)
    return jnp.sum(jnp.where(spread, row, 0.0), axis=1, keepdims=True)


def places(req, table, n_wide, per_dev):
    rows = req.shape[1]
    me = lax.axis_index("wide").astype(jnp.int32)
    stored = jnp.zeros_like(req)
    for a in range(table.shape[0]):
        stored = jnp.where(req == a, table[a], stored)
    owner = lax.div(stored, per_dev)
    slot = stored - owner * per_dev
    pad = -(-n_wide // 16) * 16
    hit = owner == (iota((pad, rows), 0) ^ me)
    earlier = (iota((rows, rows), 0) <= iota((rows, rows), 1)).astype(BF16)
    count = jnp.dot(hit.astype(BF16), earlier, preferred_element_type=F32)
    return jnp.where(hit, count.astype(jnp.int32) - 1, -1), slot


def dispatch_kernel(order, n_wide, per_dev, cap, req_hbm, table_hbm, tok_hbm, gain_hbm, *refs):
    xs = refs[: len(order)]
    wide_gain_ref, req_ref, table_ref, tok_ref, gain_ref, x_ref, sems, out_sems = refs[
        len(order) :
    ]
    rows, depth = tok_ref.shape
    height = x_ref.shape[1]
    loads = [
        pltpu.make_async_copy(req_hbm, req_ref, sems.at[0]),
        pltpu.make_async_copy(table_hbm, table_ref, sems.at[1]),
        pltpu.make_async_copy(tok_hbm, tok_ref, sems.at[2]),
        pltpu.make_async_copy(gain_hbm, gain_ref, sems.at[3]),
    ]
    for copy in loads:
        copy.start()
    loads[0].wait()
    loads[1].wait()
    place, slot = places(req_ref[...], table_ref, n_wide, per_dev)
    slots = jnp.broadcast_to(slot.astype(F32), (16, rows)).astype(BF16)
    picks, slot_rows = [], []
    for k in order:
        pick = (iota((HEAD, rows), 0) == place[k : k + 1]).astype(BF16)
        slot_rows.append(
            lax.dot_general(slots, pick, (((1,), (1,)), ((), ())), preferred_element_type=F32)
        )
        picks.append(pick[:height])
    loads[3].wait()
    wide_gain_ref[...] = gain_ref[...].astype(F32)
    loads[2].wait()
    stores = []
    for j, k in enumerate(order):
        y = jnp.dot(picks[j], tok_ref[...], preferred_element_type=F32)
        first = jnp.where(iota((height, HEAD), 0) == cap, slot_rows[j][:1], y[:, :HEAD])
        x_ref[j, :, :HEAD] = first.astype(BF16)
        x_ref[j, :, HEAD:] = y[:, HEAD:].astype(BF16)
        copy = pltpu.make_async_copy(x_ref.at[j], xs[j], out_sems.at[j])
        copy.start()
        stores.append(copy)
    for copy in stores:
        copy.wait()


def base_kernel(offsets, cols, gain_hbm, tok_hbm, weight_hbm, *refs):
    count = len(offsets)
    outs = refs[:count]
    gain_ref, tok_ref, buf, acc_ref, sems = refs[count:]
    steps, chunk, _ = buf.shape
    copies = [
        pltpu.make_async_copy(weight_hbm.at[pl.ds(i * chunk, chunk)], buf.at[i], sems.at[2 + i])
        for i in range(steps)
    ]
    loads = [
        pltpu.make_async_copy(gain_hbm, gain_ref, sems.at[0]),
        pltpu.make_async_copy(tok_hbm, tok_ref, sems.at[1]),
    ]
    for copy in loads + copies:
        copy.start()
    for copy in loads:
        copy.wait()
    spot = lax.axis_index("tensor").astype(jnp.int32)
    for i in range(steps):
        pieces = []
        for b in range(i * chunk // HEAD, (i + 1) * chunk // HEAD):
            piece = tok_ref[:, b * HEAD : (b + 1) * HEAD].astype(F32) * gain_ref[b : b + 1]
            pieces.append(piece.astype(BF16))
        x = jnp.concatenate(pieces, axis=1)
        copies[i].wait()
        for j, k in enumerate(offsets):
            start = pl.multiple_of((spot ^ k) * cols, HEAD)
            y = jnp.dot(x, buf[i, :, pl.ds(start, cols)], preferred_element_type=F32)
            if i > 0:
                y = y + acc_ref[j]
            if i < steps - 1:
                acc_ref[j] = y
            else:
                outs[j][...] = y.astype(outs[j].dtype)


def pair_kernel(count, start, *refs):
    for j in range(count):
        out_ref = refs[2 * count + j]
        rows = slice(start, start + out_ref.shape[0])
        out_ref[...] = (refs[j][rows] + refs[count + j][rows].astype(F32)).astype(BF16)


def pair_low_kernel(count, near_ref, low_ref, other_ref, *refs):
    outs, sent_ref = refs[2 * count : -1], refs[-1]
    cols = refs[0].shape[1]
    half = refs[0].shape[0] // 2
    for j in range(count):
        total = (refs[j][:half] + refs[count + j][:half].astype(F32)).astype(BF16)
        for h in range(cols // HEAD):
            outs[j][h * half : (h + 1) * half] = total[:, h * HEAD : (h + 1) * HEAD]
    base = cols // HEAD * half
    groups, height, _ = low_ref.shape
    for i in range(groups):
        total = low_ref[i].astype(F32) + other_ref[i].astype(F32)
        outs[0][base + i * height : base + (i + 1) * height] = total.astype(BF16)
    sent_ref[...] = near_ref[...]


def scaled_down_kernel(gain_ref, down_hbm, out_ref, buf, sems):
    per_dev, depth, rank = down_hbm.shape
    copies = [pltpu.make_async_copy(down_hbm.at[a], buf.at[a], sems.at[a]) for a in range(per_dev)]
    for copy in copies:
        copy.start()
    columns = []
    for b in range(depth // HEAD):
        columns.append(to_column(gain_ref[b : b + 1], HEAD))
    for a in range(per_dev):
        copies[a].wait()
        for b in range(depth // HEAD):
            span = slice(b * HEAD, (b + 1) * HEAD)
            out_ref[span, a * rank : (a + 1) * rank] = (
                buf[a, span].astype(F32) * columns[b]
            ).astype(BF16)


def aux_kernel(n_wide, per_dev, req_hbm, table_hbm, tok_hbm, sq_ref, *refs):
    sels = refs[:n_wide]
    req_ref, table_ref, tok_ref, sems = refs[n_wide:]
    copies = [
        pltpu.make_async_copy(req_hbm, req_ref, sems.at[0]),
        pltpu.make_async_copy(table_hbm, table_ref, sems.at[1]),
        pltpu.make_async_copy(tok_hbm, tok_ref, sems.at[2]),
    ]
    for copy in copies:
        copy.start()
    for copy in copies:
        copy.wait()
    rows = tok_ref.shape[0]
    place, _ = places(req_ref[...], table_ref, n_wide, per_dev)
    place = place.astype(F32)
    for k in range(n_wide):
        column = to_column(place[k : k + 1], rows).astype(jnp.int32)
        sels[k][...] = (iota((rows, HEAD), 1) == column).astype(BF16)
    tok = tok_ref[...]
    gram = lax.dot_general(tok, tok, (((1,), (1,)), ((), ())), preferred_element_type=F32)
    diag = iota((rows, rows), 0) == iota((rows, rows), 1)
    sq = jnp.sum(jnp.where(diag, gram, 0.0), axis=0, keepdims=True)
    block = jnp.zeros((8, HEAD), F32)
    for p in range(3):
        part = sq.astype(BF16).astype(F32)
        sq = sq - part
        for i in range(rows // HEAD):
            term = part[:, i * HEAD : (i + 1) * HEAD]
            block = jnp.where(iota((8, HEAD), 0) == p * (rows // HEAD) + i, term, block)
    sq_ref[...] = block


def slot_column(x_ref, cap):
    height = x_ref.shape[0]
    base = cap // 16 * 16
    row = x_ref[base : base + 16, :HEAD].astype(F32)[cap - base : cap - base + 1]
    column = to_column(row, height)
    return jnp.where(iota((height, 1), 0) < cap, column, -1.0)


def down_kernel(count, cap, with_sq, *refs):
    xs, down_ref = refs[:count], refs[count]
    sq_ref = refs[count + 1] if with_sq else None
    out_ref = refs[-1]
    height, depth = xs[0].shape
    rank = HEAD
    x = jnp.concatenate([x[...] for x in xs], axis=0) if count > 1 else xs[0][...]
    slot = [slot_column(x, cap) for x in xs]
    slot = jnp.concatenate(slot, axis=0) if count > 1 else slot[0]
    low = jnp.zeros((count * height, rank), F32)
    for g in range(down_ref.shape[1] // (2 * rank)):
        y = jnp.dot(
            x, down_ref[:, 2 * g * rank : 2 * (g + 1) * rank], preferred_element_type=F32
        )
        low = jnp.where(slot == 2 * g, y[:, :rank], low)
        low = jnp.where(slot == 2 * g + 1, y[:, rank:], low)
    for j in range(count):
        part = low[j * height : (j + 1) * height]
        if j == 0 and with_sq:
            tail = [jnp.zeros((cap, rank), F32), sq_ref[...]]
            if height > cap + 8:
                tail.append(jnp.zeros((height - cap - 8, rank), F32))
            part = part + jnp.concatenate(tail, axis=0)
        out_ref[j] = part.astype(BF16)


def low_term(ref, i, groups, height):
    if len(ref.shape) == 3:
        return ref[i].astype(F32)
    start = ref.shape[0] - (groups - i) * height
    return ref[start : start + height].astype(F32)


def low_sum_kernel(left_ref, right_ref, out_ref):
    groups, height, _ = out_ref.shape
    for i in range(groups):
        left = low_term(left_ref, i, groups, height)
        out_ref[i] = (left + low_term(right_ref, i, groups, height)).astype(BF16)


def head_is_key(heads, h):
    if heads % 2 == 0:
        return h % 2 == 0
    return (lax.axis_index("tensor").astype(jnp.int32) * heads + h) % 2 == 0


def up_kernel(count, n_parts, cap, with_sq, *refs):
    xs = refs[:count]
    parts = refs[count : count + n_parts]
    up_ref = refs[count + n_parts]
    outs = refs[count + n_parts + 1 :]
    per_dev, half, cols = up_ref.shape
    heads = cols // HEAD
    height, rank = outs[0].shape[0], 2 * half
    up = up_ref[...].reshape(per_dev * half, cols)
    sums = []
    for j in range(count):
        terms = [low_term(part, j, count, height) for part in parts]
        sums.append(sum(terms[1:], terms[0]))
    if with_sq:
        outs[count][...] = sums[0][cap : cap + 8]
    low = jnp.concatenate(sums, axis=0) if count > 1 else sums[0]
    slot = [slot_column(x, cap) for x in xs]
    slot = jnp.concatenate(slot, axis=0) if count > 1 else slot[0]
    left = iota((count * height, rank), 1) < half
    turned = pltpu.roll(low, half, 1)
    wide = []
    for source in (jnp.where(left, low, turned), jnp.where(left, turned, low)):
        pieces = []
        for g in range(per_dev // 2):
            mine = slot == jnp.where(left, 2.0 * g, 2.0 * g + 1)
            pieces.append(jnp.where(mine, source, 0.0).astype(BF16))
        wide.append(jnp.concatenate(pieces, axis=1))
    for h in range(heads):
        key = head_is_key(heads, h)
        if isinstance(key, bool):
            lhs = wide[0] if key else wide[1]
        else:
            lhs = jnp.where(key, wide[0].astype(F32), wide[1].astype(F32)).astype(BF16)
        span = slice(h * HEAD, (h + 1) * HEAD)
        y = jnp.dot(lhs, up[:, span], preferred_element_type=F32).astype(BF16)
        for j in range(count):
            outs[j][:, span] = y[j * height : (j + 1) * height]


def placed(sels, deltas):
    height, cols = deltas[0].shape
    blocks = []
    for delta in deltas:
        blocks.append(delta[...])
        if height < HEAD:
            blocks.append(jnp.zeros((HEAD - height, cols), BF16))
    lhs = jnp.concatenate([sel[...] for sel in sels], axis=1) if len(sels) > 1 else sels[0][...]
    return jnp.dot(lhs, jnp.concatenate(blocks, axis=0), preferred_element_type=F32)


def gather_kernel(n_pairs, count, sq_ref, base_ref, near_ref, *refs):
    tops, bottoms = refs[:n_pairs], refs[n_pairs : 2 * n_pairs]
    deltas = refs[2 * n_pairs : 2 * n_pairs + count]
    sels = refs[2 * n_pairs + count : 2 * n_pairs + 2 * count]
    out_ref, scale_ref = refs[-2:]
    rows, cols = out_ref.shape
    pieces = rows // HEAD
    squares = []
    for i in range(pieces):
        total = sq_ref[i : i + 1]
        for p in range(1, 3):
            total = total + sq_ref[p * pieces + i : p * pieces + i + 1]
        squares.append(total)
    square = to_column(jnp.concatenate(squares, axis=1), rows)
    scale = lax.rsqrt(square * (1.0 / MODEL_WIDTH) + EPSILON)
    scale_ref[...] = jnp.broadcast_to(scale, (rows, HEAD))
    total = base_ref[...] + near_ref[...].astype(F32) + placed(sels, deltas)
    half = rows // 2
    lower = total[half:]
    for bottom in bottoms:
        lower = lower + bottom[...].astype(F32)
    out_ref[half:] = lower
    for h in range(cols // HEAD):
        span = slice(h * HEAD, (h + 1) * HEAD)
        upper = total[:half, span]
        for top in tops:
            upper = upper + top[h * half : (h + 1) * half].astype(F32)
        out_ref[:half, span] = upper


def finish_kernel(count, sum_ref, scale_ref, cos_ref, sin_ref, *refs):
    deltas, sels, out_ref = refs[:count], refs[count : 2 * count], refs[2 * count]
    rows, cols = out_ref.shape
    total = sum_ref[...] + placed(sels, deltas)
    heads = cols // HEAD
    scale = scale_ref[...]
    for h in range(heads):
        span = slice(h * HEAD, (h + 1) * HEAD)
        x = total[:, span] * scale
        key = head_is_key(heads, h)
        if key is False:
            out_ref[:, span] = x.astype(BF16)
            continue
        y = x * cos_ref[...] + pltpu.roll(x, HEAD // 2, 1) * sin_ref[...]
        if key is not True:
            y = jnp.where(key, y, x)
        out_ref[:, span] = y.astype(BF16)


def local(
    mesh_shape,
    tokens,
    attention_norm_gain,
    key_value_weight,
    adapter_down_weight,
    adapter_up_weight,
    request_adapter,
    adapter_storage_row,
    cached_token_length,
):
    n_wide, n_tensor = mesh_shape["wide"], mesh_shape["tensor"]
    rows, depth = tokens.shape
    per_dev, _, rank = adapter_down_weight.shape
    cols = adapter_up_weight.shape[2]
    cap = 104 if n_wide <= 4 else 64
    height = -(-(cap + 8) // 16) * 16
    req = request_adapter.reshape(1, rows)
    gain = attention_norm_gain.reshape(depth // HEAD, HEAD)

    def over(axis, array, k):
        size = mesh_shape[axis]
        return lax.ppermute(array, axis, [(i, i ^ k) for i in range(size)])

    small = [pltpu.VMEM((1, rows), jnp.int32), pltpu.SMEM(adapter_storage_row.shape, jnp.int32)]
    first, last = [0, 1], list(range(2, n_wide))

    def dispatch(order, after):
        *blocks, wide_gain = call(
            functools.partial(dispatch_kernel, order, n_wide, per_dev, cap),
            "dispatch",
            [shape((height, depth), BF16)] * len(order) + [shape(gain.shape, F32)],
            hbm=(req, adapter_storage_row, tokens, gain),
            hbm_outs=len(order),
            after=after,
            scratch=small
            + [
                pltpu.VMEM((rows, depth), BF16),
                pltpu.VMEM(gain.shape, BF16),
                pltpu.VMEM((len(order), height, depth), BF16),
                pltpu.SemaphoreType.DMA((4,)),
                pltpu.SemaphoreType.DMA((len(order),)),
            ],
            flops=2 * len(order) * height * rows * depth,
            moved=2 * rows * depth * 4,
            limit=63,
        )
        return blocks, wide_gain

    order = list(range(n_wide - 1, -1, -1))
    blocks, wide_gain = dispatch(order, ())
    held = [blocks[n_wide - 1 - k] for k in range(n_wide)]
    held[1:] = [over("wide", held[k], k) for k in range(1, n_wide)]

    twos = list(range(2, n_tensor, 2))
    far = [k ^ 1 for k in twos]
    offsets = far + [1] + twos + [0]
    chunk = math.gcd(depth, 512)
    steps = depth // chunk
    sums = call(
        functools.partial(base_kernel, offsets, cols),
        "base",
        [shape((rows, cols), BF16)] * (len(far) + 1) + [shape((rows, cols), F32)] * (len(twos) + 1),
        hbm=(wide_gain, tokens, key_value_weight),
        scratch=[
            pltpu.VMEM(gain.shape, F32),
            pltpu.VMEM((rows, depth), BF16),
            pltpu.VMEM((steps, chunk, key_value_weight.shape[1]), BF16),
            pltpu.VMEM((len(offsets), rows, cols), F32),
            pltpu.SemaphoreType.DMA((2 + steps,)),
        ],
        flops=2 * rows * depth * cols * n_tensor,
        moved=2 * depth * cols * n_tensor,
        limit=52,
    )
    away, near, own, base = sums[: len(far)], sums[len(far)], sums[len(far) + 1 : -1], sums[-1]
    beside = [over("tensor", p, 1) for p in away]
    (down,) = call(
        scaled_down_kernel,
        "scaled_down",
        [shape((depth, per_dev * rank), BF16)],
        vmem=(wide_gain,),
        hbm=(adapter_down_weight,),
        after=(base,),
        scratch=[
            pltpu.VMEM((per_dev, depth, rank), BF16),
            pltpu.SemaphoreType.DMA((per_dev,)),
        ],
        flops=4 * depth * per_dev * rank,
        moved=4 * depth * per_dev * rank,
    )
    half_size = HEAD // 2
    freq_index = jnp.arange(half_size).astype(F32)
    inverse = jnp.exp(freq_index * (-2.0 / HEAD) * math.log(ROPE_BASE))
    angles = cached_token_length.astype(F32)[:, None] * inverse[None, :]
    cosine, sine = jnp.cos(angles), jnp.sin(angles)
    cosine = jnp.concatenate([cosine, cosine], axis=1)
    sine = jnp.concatenate([-sine, sine], axis=1)

    def down_block(group, extra, after):
        xs = [held[k] for k in group]
        (low,) = call(
            functools.partial(down_kernel, len(xs), cap, bool(extra)),
            "down_block",
            [shape((len(xs), height, rank), BF16)],
            vmem=(*xs, down, *extra),
            after=after,
            flops=2 * len(xs) * height * depth * rank * per_dev,
            moved=2 * per_dev * depth * rank,
        )
        return low

    def up_block(group, parts, with_sq, after):
        xs = [held[k] for k in group]
        outs = [shape((height, cols), BF16)] * len(xs)
        if with_sq:
            outs = outs + [shape((8, HEAD), F32)]
        return call(
            functools.partial(up_kernel, len(xs), len(parts), cap, with_sq),
            "up_block",
            outs,
            vmem=(*xs, *parts, adapter_up_weight),
            after=after,
            flops=2 * len(xs) * height * per_dev * rank * cols,
            moved=2 * per_dev * rank * cols,
        )

    low = down_block(first, (), ())
    sq, *sels = call(
        functools.partial(aux_kernel, n_wide, per_dev),
        "aux",
        [shape((8, HEAD), F32)] + [shape((rows, HEAD), BF16)] * n_wide,
        hbm=(req, adapter_storage_row, tokens),
        after=(low,),
        scratch=small + [pltpu.VMEM((rows, depth), BF16), pltpu.SemaphoreType.DMA((3,))],
        flops=2 * rows * rows * depth,
        moved=2 * rows * depth,
    )
    half = rows // 2
    upper = cols // HEAD * half
    other = over("tensor", low, 1)
    *pairs, near = call(
        functools.partial(pair_low_kernel, len(twos)),
        "pair_low_sums",
        [shape((upper + len(first) * height, HEAD), BF16)]
        + [shape((upper, HEAD), BF16)] * (len(twos) - 1)
        + [shape((rows, cols), BF16)],
        vmem=(near, low, other, *own, *beside),
        after=(sq, cosine, sine),
    )
    tops = [over("tensor", p, k) for p, k in zip(pairs, twos)]
    near = over("tensor", near, 1)
    done = pairs[0]
    low, other = pairs[0], tops[0]
    for step in range(2, n_tensor.bit_length() - 1):
        (low,) = call(
            low_sum_kernel,
            "low_sum",
            [shape((len(first), height, rank), BF16)],
            vmem=(low, other),
        )
        other = over("tensor", low, 2**step)
    low_last = down_block(last, (sq,), (done,))
    last_parts = [low_last] + [over("tensor", low_last, k) for k in range(n_tensor - 1, 0, -1)]
    ups = up_block(first, [low, other], False, (low_last,))
    deltas = [u if k == 0 else over("wide", u, k) for k, u in zip(first, ups)]
    pairs = call(
        functools.partial(pair_kernel, len(twos), half),
        "pair_sums",
        [shape((half, cols), BF16)] * len(twos),
        vmem=(*own, *beside),
        after=(ups[0],),
    )
    bottoms = [over("tensor", p, k) for p, k in zip(pairs, twos)]
    *ups, square = up_block(last, last_parts, True, (pairs[0],))
    last_deltas = [over("wide", u, k) for k, u in zip(last, ups)]
    total, scale = call(
        functools.partial(gather_kernel, len(bottoms), len(first)),
        "gather",
        [shape((rows, cols), F32), shape((rows, HEAD), F32)],
        vmem=(square, base, near, *tops, *bottoms, *deltas, *[sels[k] for k in first]),
        after=(ups[0],),
        flops=2 * rows * cols * HEAD * len(first),
    )
    return call(
        functools.partial(finish_kernel, len(last)),
        "finish",
        [shape((rows, cols), BF16)],
        vmem=(total, scale, cosine, sine, *last_deltas, *[sels[k] for k in last]),
        flops=2 * rows * cols * HEAD,
    )[0]


def solution(mesh):
    return jax.shard_map(
        functools.partial(local, dict(mesh.shape)),
        mesh=mesh,
        in_specs=(
            P(("parts", "wide"), "tensor"),
            P("tensor"),
            P("tensor", None),
            P(("parts", "wide"), "tensor", None),
            P(("parts", "wide"), None, "tensor"),
            P(("parts", "wide")),
            P("parts"),
            P(("parts", "wide")),
        ),
        out_specs=P(("parts", "wide"), "tensor"),
        check_vma=False,
    )
```

```python
import functools
import math

import jax
import jax.numpy as jnp
from jax import lax
from jax.experimental import pallas as pl
from jax.experimental.pallas import tpu as pltpu
from jax.sharding import PartitionSpec as P

MODEL_WIDTH = 8192
HEAD = 128
EPSILON = 1e-05
ROPE_BASE = 500000.0
F32 = jnp.float32
BF16 = jnp.bfloat16


def iota(shape, axis):
    return lax.broadcasted_iota(jnp.int32, shape, axis)


def call(kernel, name, outs, vmem=(), hbm=(), after=(), scratch=(), flops=0, moved=0, limit=16, hbm_outs=0):
    def body(*refs):
        keep = len(vmem) + len(hbm)
        kernel(*refs[:keep], *refs[keep + len(after) :])

    return pl.pallas_call(
        body,
        out_shape=outs,
        in_specs=[pl.BlockSpec(memory_space=pltpu.VMEM)] * len(vmem)
        + [pl.BlockSpec(memory_space=pltpu.HBM)] * len(hbm)
        + [pl.BlockSpec(memory_space=pl.ANY)] * len(after),
        out_specs=[pl.BlockSpec(memory_space=pltpu.HBM)] * hbm_outs
        + [pl.BlockSpec(memory_space=pltpu.VMEM)] * (len(outs) - hbm_outs),
        scratch_shapes=scratch,
        compiler_params=pltpu.CompilerParams(vmem_limit_bytes=limit * 1024 * 1024),
        cost_estimate=pl.CostEstimate(flops=flops, bytes_accessed=moved, transcendentals=0),
        name=name,
    )(*vmem, *hbm, *after)


def shape(dims, dtype):
    return jax.ShapeDtypeStruct(dims, dtype)


def to_column(row, count):
    spread = iota((count, row.shape[1]), 0) == iota((count, row.shape[1]), 1)
    return jnp.sum(jnp.where(spread, row, 0.0), axis=1, keepdims=True)


def places(req, table, n_wide, per_dev):
    rows = req.shape[1]
    me = lax.axis_index("wide").astype(jnp.int32)
    stored = jnp.zeros_like(req)
    for a in range(table.shape[0]):
        stored = jnp.where(req == a, table[a], stored)
    owner = lax.div(stored, per_dev)
    slot = stored - owner * per_dev
    pad = -(-n_wide // 16) * 16
    hit = owner == (iota((pad, rows), 0) ^ me)
    earlier = (iota((rows, rows), 0) <= iota((rows, rows), 1)).astype(BF16)
    count = jnp.dot(hit.astype(BF16), earlier, preferred_element_type=F32)
    return jnp.where(hit, count.astype(jnp.int32) - 1, -1), slot


def dispatch_kernel(order, n_wide, per_dev, cap, req_hbm, table_hbm, tok_hbm, gain_hbm, *refs):
    xs = refs[: len(order)]
    xg_hbm, req_ref, table_ref, tok_ref, gain_ref, x_ref, xg_ref, sems, out_sems = refs[
        len(order) :
    ]
    rows, depth = tok_ref.shape
    height = x_ref.shape[1]
    loads = [
        pltpu.make_async_copy(req_hbm, req_ref, sems.at[0]),
        pltpu.make_async_copy(table_hbm, table_ref, sems.at[1]),
        pltpu.make_async_copy(tok_hbm, tok_ref, sems.at[2]),
        pltpu.make_async_copy(gain_hbm, gain_ref, sems.at[3]),
    ]
    for copy in loads:
        copy.start()
    loads[0].wait()
    loads[1].wait()
    place, slot = places(req_ref[...], table_ref, n_wide, per_dev)
    slots = jnp.broadcast_to(slot.astype(F32), (16, rows)).astype(BF16)
    picks, slot_rows = [], []
    for k in order:
        pick = (iota((HEAD, rows), 0) == place[k : k + 1]).astype(BF16)
        slot_rows.append(
            lax.dot_general(slots, pick, (((1,), (1,)), ((), ())), preferred_element_type=F32)
        )
        picks.append(pick[:height])
    loads[3].wait()
    loads[2].wait()
    stores = []
    for j, k in enumerate(order):
        if k == 1:
            for b in range(depth // HEAD):
                span = slice(b * HEAD, (b + 1) * HEAD)
                piece = tok_ref[:, span].astype(F32) * gain_ref[b : b + 1].astype(F32)
                xg_ref[:, span] = piece.astype(BF16)
            copy = pltpu.make_async_copy(xg_ref, xg_hbm, out_sems.at[len(order)])
            copy.start()
            stores.append(copy)
        y = jnp.dot(picks[j], tok_ref[...], preferred_element_type=F32)
        first = jnp.where(iota((height, HEAD), 0) == cap, slot_rows[j][:1], y[:, :HEAD])
        x_ref[j, :, :HEAD] = first.astype(BF16)
        x_ref[j, :, HEAD:] = y[:, HEAD:].astype(BF16)
        copy = pltpu.make_async_copy(x_ref.at[j], xs[j], out_sems.at[j])
        copy.start()
        stores.append(copy)
    for copy in stores:
        copy.wait()


def base_far_kernel(offsets, cols, xg_hbm, weight_hbm, *refs):
    outs = refs[: len(offsets)]
    x_ref, buf, sems = refs[len(offsets) :]
    _, steps, chunk, _ = buf.shape
    spot = lax.axis_index("tensor").astype(jnp.int32)
    load = pltpu.make_async_copy(xg_hbm, x_ref, sems.at[0])
    load.start()
    copies = []
    for j, k in enumerate(offsets):
        start = pl.multiple_of((spot ^ k) * cols, HEAD)
        for i in range(steps):
            source = weight_hbm.at[pl.ds(i * chunk, chunk), pl.ds(start, cols)]
            copy = pltpu.make_async_copy(source, buf.at[j, i], sems.at[1 + len(copies)])
            copy.start()
            copies.append(copy)
    load.wait()
    for j in range(len(offsets)):
        total = None
        for i in range(steps):
            copies[j * steps + i].wait()
            x = x_ref[:, i * chunk : (i + 1) * chunk]
            y = jnp.dot(x, buf[j, i], preferred_element_type=F32)
            total = y if total is None else total + y
        outs[j][...] = total.astype(BF16)


def base_kernel(offsets, cols, xg_hbm, weight_hbm, *refs):
    count = len(offsets)
    outs = refs[:count]
    x_ref, buf, acc_ref, sems = refs[count:]
    steps, chunk, _ = buf.shape
    load = pltpu.make_async_copy(xg_hbm, x_ref, sems.at[0])
    copies = [
        pltpu.make_async_copy(weight_hbm.at[pl.ds(i * chunk, chunk)], buf.at[i], sems.at[1 + i])
        for i in range(steps)
    ]
    for copy in [load] + copies:
        copy.start()
    load.wait()
    spot = lax.axis_index("tensor").astype(jnp.int32)
    for i in range(steps):
        x = x_ref[:, i * chunk : (i + 1) * chunk]
        copies[i].wait()
        for j, k in enumerate(offsets):
            start = pl.multiple_of((spot ^ k) * cols, HEAD)
            y = jnp.dot(x, buf[i, :, pl.ds(start, cols)], preferred_element_type=F32)
            if i > 0:
                y = y + acc_ref[j]
            if i < steps - 1:
                acc_ref[j] = y
            else:
                outs[j][...] = y.astype(outs[j].dtype)


def pair_kernel(count, start, base_ref, near_ref, *refs):
    refs[-1][...] = base_ref[...] + near_ref[...].astype(F32)
    for j in range(count):
        out_ref = refs[2 * count + j]
        rows = slice(start, start + out_ref.shape[0])
        out_ref[...] = (refs[j][rows] + refs[count + j][rows].astype(F32)).astype(BF16)


def pair_low_kernel(count, low_ref, other_ref, *refs):
    outs = refs[2 * count :]
    cols = refs[0].shape[1]
    half = refs[0].shape[0] // 2
    for j in range(count):
        total = (refs[j][:half] + refs[count + j][:half].astype(F32)).astype(BF16)
        for h in range(cols // HEAD):
            outs[j][h * half : (h + 1) * half] = total[:, h * HEAD : (h + 1) * HEAD]
    base = cols // HEAD * half
    groups, height, _ = low_ref.shape
    for i in range(groups):
        total = low_ref[i].astype(F32) + other_ref[i].astype(F32)
        outs[0][base + i * height : base + (i + 1) * height] = total.astype(BF16)


def scaled_down_kernel(gain_ref, down_hbm, out_ref, buf, sems):
    per_dev, depth, rank = down_hbm.shape
    copies = [pltpu.make_async_copy(down_hbm.at[a], buf.at[a], sems.at[a]) for a in range(per_dev)]
    for copy in copies:
        copy.start()
    columns = []
    for b in range(depth // HEAD):
        columns.append(to_column(gain_ref[b : b + 1].astype(F32), HEAD))
    for a in range(per_dev):
        copies[a].wait()
        for b in range(depth // HEAD):
            span = slice(b * HEAD, (b + 1) * HEAD)
            out_ref[span, a * rank : (a + 1) * rank] = (
                buf[a, span].astype(F32) * columns[b]
            ).astype(BF16)


def aux_kernel(n_wide, per_dev, req_hbm, table_hbm, tok_hbm, sq_ref, *refs):
    sels = refs[:n_wide]
    req_ref, table_ref, tok_ref, sems = refs[n_wide:]
    copies = [
        pltpu.make_async_copy(req_hbm, req_ref, sems.at[0]),
        pltpu.make_async_copy(table_hbm, table_ref, sems.at[1]),
        pltpu.make_async_copy(tok_hbm, tok_ref, sems.at[2]),
    ]
    for copy in copies:
        copy.start()
    for copy in copies:
        copy.wait()
    rows = tok_ref.shape[0]
    place, _ = places(req_ref[...], table_ref, n_wide, per_dev)
    place = place.astype(F32)
    for k in range(n_wide):
        column = to_column(place[k : k + 1], rows).astype(jnp.int32)
        sels[k][...] = (iota((rows, HEAD), 1) == column).astype(BF16)
    tok = tok_ref[...]
    gram = lax.dot_general(tok, tok, (((1,), (1,)), ((), ())), preferred_element_type=F32)
    diag = iota((rows, rows), 0) == iota((rows, rows), 1)
    sq = jnp.sum(jnp.where(diag, gram, 0.0), axis=0, keepdims=True)
    block = jnp.zeros((8, HEAD), F32)
    for p in range(3):
        part = sq.astype(BF16).astype(F32)
        sq = sq - part
        for i in range(rows // HEAD):
            term = part[:, i * HEAD : (i + 1) * HEAD]
            block = jnp.where(iota((8, HEAD), 0) == p * (rows // HEAD) + i, term, block)
    sq_ref[...] = block


def slot_column(x_ref, cap):
    height = x_ref.shape[0]
    base = cap // 16 * 16
    row = x_ref[base : base + 16, :HEAD].astype(F32)[cap - base : cap - base + 1]
    column = to_column(row, height)
    return jnp.where(iota((height, 1), 0) < cap, column, -1.0)


def down_kernel(count, cap, with_sq, *refs):
    xs, down_ref = refs[:count], refs[count]
    sq_ref = refs[count + 1] if with_sq else None
    out_ref = refs[-1]
    height, depth = xs[0].shape
    rank = HEAD
    x = jnp.concatenate([x[...] for x in xs], axis=0) if count > 1 else xs[0][...]
    slot = [slot_column(x, cap) for x in xs]
    slot = jnp.concatenate(slot, axis=0) if count > 1 else slot[0]
    low = jnp.zeros((count * height, rank), F32)
    for g in range(down_ref.shape[1] // (2 * rank)):
        y = jnp.dot(
            x, down_ref[:, 2 * g * rank : 2 * (g + 1) * rank], preferred_element_type=F32
        )
        low = jnp.where(slot == 2 * g, y[:, :rank], low)
        low = jnp.where(slot == 2 * g + 1, y[:, rank:], low)
    for j in range(count):
        part = low[j * height : (j + 1) * height]
        if j == 0 and with_sq:
            tail = [jnp.zeros((cap, rank), F32), sq_ref[...]]
            if height > cap + 8:
                tail.append(jnp.zeros((height - cap - 8, rank), F32))
            part = part + jnp.concatenate(tail, axis=0)
        out_ref[j] = part.astype(BF16)


def low_term(ref, i, groups, height):
    if len(ref.shape) == 3:
        return ref[i].astype(F32)
    start = ref.shape[0] - (groups - i) * height
    return ref[start : start + height].astype(F32)


def low_sum_kernel(left_ref, right_ref, out_ref):
    groups, height, _ = out_ref.shape
    for i in range(groups):
        left = low_term(left_ref, i, groups, height)
        out_ref[i] = (left + low_term(right_ref, i, groups, height)).astype(BF16)


def head_is_key(heads, h):
    if heads % 2 == 0:
        return h % 2 == 0
    return (lax.axis_index("tensor").astype(jnp.int32) * heads + h) % 2 == 0


def up_kernel(count, n_parts, cap, with_sq, *refs):
    xs = refs[:count]
    parts = refs[count : count + n_parts]
    up_ref = refs[count + n_parts]
    outs = refs[count + n_parts + 1 :]
    per_dev, half, cols = up_ref.shape
    heads = cols // HEAD
    height, rank = outs[0].shape[0], 2 * half
    up = up_ref[...].reshape(per_dev * half, cols)
    sums = []
    for j in range(count):
        terms = [low_term(part, j, count, height) for part in parts]
        sums.append(sum(terms[1:], terms[0]))
    if with_sq:
        outs[count][...] = sums[0][cap : cap + 8]
    low = jnp.concatenate(sums, axis=0) if count > 1 else sums[0]
    slot = [slot_column(x, cap) for x in xs]
    slot = jnp.concatenate(slot, axis=0) if count > 1 else slot[0]
    left = iota((count * height, rank), 1) < half
    turned = pltpu.roll(low, half, 1)
    wide = []
    for source in (jnp.where(left, low, turned), jnp.where(left, turned, low)):
        pieces = []
        for g in range(per_dev // 2):
            mine = slot == jnp.where(left, 2.0 * g, 2.0 * g + 1)
            pieces.append(jnp.where(mine, source, 0.0).astype(BF16))
        wide.append(jnp.concatenate(pieces, axis=1))
    for h in range(heads):
        key = head_is_key(heads, h)
        if isinstance(key, bool):
            lhs = wide[0] if key else wide[1]
        else:
            lhs = jnp.where(key, wide[0].astype(F32), wide[1].astype(F32)).astype(BF16)
        span = slice(h * HEAD, (h + 1) * HEAD)
        y = jnp.dot(lhs, up[:, span], preferred_element_type=F32).astype(BF16)
        for j in range(count):
            outs[j][:, span] = y[j * height : (j + 1) * height]


def placed(sels, deltas):
    height, cols = deltas[0].shape
    blocks = []
    for delta in deltas:
        blocks.append(delta[...])
        if height < HEAD:
            blocks.append(jnp.zeros((HEAD - height, cols), BF16))
    lhs = jnp.concatenate([sel[...] for sel in sels], axis=1) if len(sels) > 1 else sels[0][...]
    return jnp.dot(lhs, jnp.concatenate(blocks, axis=0), preferred_element_type=F32)


def gather_kernel(n_pairs, count, sq_ref, base_ref, *refs):
    tops, bottoms = refs[:n_pairs], refs[n_pairs : 2 * n_pairs]
    deltas = refs[2 * n_pairs : 2 * n_pairs + count]
    sels = refs[2 * n_pairs + count : 2 * n_pairs + 2 * count]
    out_ref, scale_ref = refs[-2:]
    rows, cols = out_ref.shape
    pieces = rows // HEAD
    squares = []
    for i in range(pieces):
        total = sq_ref[i : i + 1]
        for p in range(1, 3):
            total = total + sq_ref[p * pieces + i : p * pieces + i + 1]
        squares.append(total)
    square = to_column(jnp.concatenate(squares, axis=1), rows)
    scale = lax.rsqrt(square * (1.0 / MODEL_WIDTH) + EPSILON)
    scale_ref[...] = jnp.broadcast_to(scale, (rows, HEAD))
    total = base_ref[...] + placed(sels, deltas)
    half = rows // 2
    lower = total[half:]
    for bottom in bottoms:
        lower = lower + bottom[...].astype(F32)
    out_ref[half:] = lower
    for h in range(cols // HEAD):
        span = slice(h * HEAD, (h + 1) * HEAD)
        upper = total[:half, span]
        for top in tops:
            upper = upper + top[h * half : (h + 1) * half].astype(F32)
        out_ref[:half, span] = upper


def finish_kernel(count, sum_ref, scale_ref, cos_ref, sin_ref, *refs):
    deltas, sels, out_ref = refs[:count], refs[count : 2 * count], refs[2 * count]
    rows, cols = out_ref.shape
    total = sum_ref[...] + placed(sels, deltas)
    heads = cols // HEAD
    scale = scale_ref[...]
    for h in range(heads):
        span = slice(h * HEAD, (h + 1) * HEAD)
        x = total[:, span] * scale
        key = head_is_key(heads, h)
        if key is False:
            out_ref[:, span] = x.astype(BF16)
            continue
        y = x * cos_ref[...] + pltpu.roll(x, HEAD // 2, 1) * sin_ref[...]
        if key is not True:
            y = jnp.where(key, y, x)
        out_ref[:, span] = y.astype(BF16)


def local(
    mesh_shape,
    tokens,
    attention_norm_gain,
    key_value_weight,
    adapter_down_weight,
    adapter_up_weight,
    request_adapter,
    adapter_storage_row,
    cached_token_length,
):
    n_wide, n_tensor = mesh_shape["wide"], mesh_shape["tensor"]
    rows, depth = tokens.shape
    per_dev, _, rank = adapter_down_weight.shape
    cols = adapter_up_weight.shape[2]
    cap = 104 if n_wide <= 4 else 64
    height = -(-(cap + 8) // 16) * 16
    req = request_adapter.reshape(1, rows)
    gain = attention_norm_gain.reshape(depth // HEAD, HEAD)

    def over(axis, array, k):
        size = mesh_shape[axis]
        return lax.ppermute(array, axis, [(i, i ^ k) for i in range(size)])

    small = [pltpu.VMEM((1, rows), jnp.int32), pltpu.SMEM(adapter_storage_row.shape, jnp.int32)]
    first, last = [0, 1], list(range(2, n_wide))

    order = list(range(n_wide - 1, -1, -1))
    *blocks, xg = call(
        functools.partial(dispatch_kernel, order, n_wide, per_dev, cap),
        "dispatch",
        [shape((height, depth), BF16)] * n_wide + [shape((rows, depth), BF16)],
        hbm=(req, adapter_storage_row, tokens, gain),
        hbm_outs=n_wide + 1,
        scratch=small
        + [
            pltpu.VMEM((rows, depth), BF16),
            pltpu.VMEM(gain.shape, BF16),
            pltpu.VMEM((n_wide, height, depth), BF16),
            pltpu.VMEM((rows, depth), BF16),
            pltpu.SemaphoreType.DMA((4,)),
            pltpu.SemaphoreType.DMA((n_wide + 1,)),
        ],
        flops=2 * n_wide * height * rows * depth,
        moved=2 * rows * depth * 4,
        limit=63,
    )
    held = [blocks[n_wide - 1 - k] for k in range(n_wide)]
    held[1:] = [over("wide", held[k], k) for k in range(1, n_wide)]

    twos = list(range(2, n_tensor, 2))
    far = [k ^ 1 for k in twos]
    offsets = [1] + twos + [0]
    chunk = math.gcd(depth, 512)
    steps = depth // chunk
    away = call(
        functools.partial(base_far_kernel, far, cols),
        "base_far",
        [shape((rows, cols), BF16)] * len(far),
        hbm=(xg, key_value_weight),
        scratch=[
            pltpu.VMEM((rows, depth), BF16),
            pltpu.VMEM((len(far), steps, chunk, cols), BF16),
            pltpu.SemaphoreType.DMA((1 + len(far) * steps,)),
        ],
        flops=2 * rows * depth * cols * len(far),
        moved=2 * depth * cols * len(far),
        limit=58,
    )
    beside = [over("tensor", p, 1) for p in away]
    (down,) = call(
        scaled_down_kernel,
        "scaled_down",
        [shape((depth, per_dev * rank), BF16)],
        vmem=(gain,),
        hbm=(adapter_down_weight,),
        after=(away[0],),
        scratch=[
            pltpu.VMEM((per_dev, depth, rank), BF16),
            pltpu.SemaphoreType.DMA((per_dev,)),
        ],
        flops=4 * depth * per_dev * rank,
        moved=4 * depth * per_dev * rank,
    )

    half_size = HEAD // 2
    freq_index = jnp.arange(half_size).astype(F32)
    inverse = jnp.exp(freq_index * (-2.0 / HEAD) * math.log(ROPE_BASE))
    angles = cached_token_length.astype(F32)[:, None] * inverse[None, :]
    cosine, sine = jnp.cos(angles), jnp.sin(angles)
    cosine = jnp.concatenate([cosine, cosine], axis=1)
    sine = jnp.concatenate([-sine, sine], axis=1)

    def down_block(group, extra, after):
        xs = [held[k] for k in group]
        (low,) = call(
            functools.partial(down_kernel, len(xs), cap, bool(extra)),
            "down_block",
            [shape((len(xs), height, rank), BF16)],
            vmem=(*xs, down, *extra),
            after=after,
            flops=2 * len(xs) * height * depth * rank * per_dev,
            moved=2 * per_dev * depth * rank,
        )
        return low

    def up_block(group, parts, with_sq, after):
        xs = [held[k] for k in group]
        outs = [shape((height, cols), BF16)] * len(xs)
        if with_sq:
            outs = outs + [shape((8, HEAD), F32)]
        return call(
            functools.partial(up_kernel, len(xs), len(parts), cap, with_sq),
            "up_block",
            outs,
            vmem=(*xs, *parts, adapter_up_weight),
            after=after,
            flops=2 * len(xs) * height * per_dev * rank * cols,
            moved=2 * per_dev * rank * cols,
        )

    low = down_block(first, (), ())
    other = over("tensor", low, 1)
    near, *own, base = call(
        functools.partial(base_kernel, offsets, cols),
        "base",
        [shape((rows, cols), BF16)] + [shape((rows, cols), F32)] * (len(twos) + 1),
        hbm=(xg, key_value_weight),
        after=(low,),
        scratch=[
            pltpu.VMEM((rows, depth), BF16),
            pltpu.VMEM((steps, chunk, key_value_weight.shape[1]), BF16),
            pltpu.VMEM((len(offsets), rows, cols), F32),
            pltpu.SemaphoreType.DMA((1 + steps,)),
        ],
        flops=2 * rows * depth * cols * len(offsets),
        moved=2 * depth * cols * n_tensor,
        limit=52,
    )
    near = over("tensor", near, 1)
    half = rows // 2
    upper = cols // HEAD * half
    pairs = call(
        functools.partial(pair_low_kernel, len(twos)),
        "pair_low_sums",
        [shape((upper + len(first) * height, HEAD), BF16)]
        + [shape((upper, HEAD), BF16)] * (len(twos) - 1),
        vmem=(low, other, *own, *beside),
    )
    tops = [over("tensor", p, k) for p, k in zip(pairs, twos)]
    done = pairs[0]
    low, other = pairs[0], tops[0]
    sq, *sels = call(
        functools.partial(aux_kernel, n_wide, per_dev),
        "aux",
        [shape((8, HEAD), F32)] + [shape((rows, HEAD), BF16)] * n_wide,
        hbm=(req, adapter_storage_row, tokens),
        after=(done,),
        scratch=small + [pltpu.VMEM((rows, depth), BF16), pltpu.SemaphoreType.DMA((3,))],
        flops=2 * rows * rows * depth,
        moved=2 * rows * depth,
    )
    for step in range(2, n_tensor.bit_length() - 1):
        (low,) = call(
            low_sum_kernel,
            "low_sum",
            [shape((len(first), height, rank), BF16)],
            vmem=(low, other),
        )
        other = over("tensor", low, 2**step)
    low_last = down_block(last, (sq,), (cosine, sine))
    last_parts = [low_last] + [over("tensor", low_last, k) for k in range(n_tensor - 1, 0, -1)]
    ups = up_block(first, [low, other], False, (low_last,))
    deltas = [u if k == 0 else over("wide", u, k) for k, u in zip(first, ups)]
    *pairs, base = call(
        functools.partial(pair_kernel, len(twos), half),
        "pair_sums",
        [shape((half, cols), BF16)] * len(twos) + [shape((rows, cols), F32)],
        vmem=(base, near, *own, *beside),
        after=(ups[0],),
    )
    bottoms = [over("tensor", p, k) for p, k in zip(pairs, twos)]
    *ups, square = up_block(last, last_parts, True, (pairs[0],))
    last_deltas = [over("wide", u, k) for k, u in zip(last, ups)]
    total, scale = call(
        functools.partial(gather_kernel, len(bottoms), len(first)),
        "gather",
        [shape((rows, cols), F32), shape((rows, HEAD), F32)],
        vmem=(square, base, *tops, *bottoms, *deltas, *[sels[k] for k in first]),
        after=(ups[0],),
        flops=2 * rows * cols * HEAD * len(first),
    )
    return call(
        functools.partial(finish_kernel, len(last)),
        "finish",
        [shape((rows, cols), BF16)],
        vmem=(total, scale, cosine, sine, *last_deltas, *[sels[k] for k in last]),
        flops=2 * rows * cols * HEAD,
    )[0]


def solution(mesh):
    return jax.shard_map(
        functools.partial(local, dict(mesh.shape)),
        mesh=mesh,
        in_specs=(
            P(("parts", "wide"), "tensor"),
            P("tensor"),
            P("tensor", None),
            P(("parts", "wide"), "tensor", None),
            P(("parts", "wide"), None, "tensor"),
            P(("parts", "wide")),
            P("parts"),
            P(("parts", "wide")),
        ),
        out_specs=P(("parts", "wide"), "tensor"),
        check_vma=False,
    )
```

```python
import functools
import math

import jax
import jax.numpy as jnp
from jax import lax
from jax.experimental import pallas as pl
from jax.experimental.pallas import tpu as pltpu
from jax.sharding import PartitionSpec as P

MODEL_WIDTH = 8192
HEAD = 128
EPSILON = 1e-05
ROPE_BASE = 500000.0
F32 = jnp.float32
BF16 = jnp.bfloat16


def iota(shape, axis):
    return lax.broadcasted_iota(jnp.int32, shape, axis)


def call(kernel, name, outs, vmem=(), hbm=(), after=(), scratch=(), flops=0, moved=0, limit=16, hbm_outs=0):
    def body(*refs):
        keep = len(vmem) + len(hbm)
        kernel(*refs[:keep], *refs[keep + len(after) :])

    return pl.pallas_call(
        body,
        out_shape=outs,
        in_specs=[pl.BlockSpec(memory_space=pltpu.VMEM)] * len(vmem)
        + [pl.BlockSpec(memory_space=pltpu.HBM)] * len(hbm)
        + [pl.BlockSpec(memory_space=pl.ANY)] * len(after),
        out_specs=[pl.BlockSpec(memory_space=pltpu.HBM)] * hbm_outs
        + [pl.BlockSpec(memory_space=pltpu.VMEM)] * (len(outs) - hbm_outs),
        scratch_shapes=scratch,
        compiler_params=pltpu.CompilerParams(vmem_limit_bytes=limit * 1024 * 1024),
        cost_estimate=pl.CostEstimate(flops=flops, bytes_accessed=moved, transcendentals=0),
        name=name,
    )(*vmem, *hbm, *after)


def shape(dims, dtype):
    return jax.ShapeDtypeStruct(dims, dtype)


def to_column(row, count):
    spread = iota((count, row.shape[1]), 0) == iota((count, row.shape[1]), 1)
    return jnp.sum(jnp.where(spread, row, 0.0), axis=1, keepdims=True)


def places(req, table, n_wide, per_dev):
    rows = req.shape[1]
    me = lax.axis_index("wide").astype(jnp.int32)
    stored = jnp.zeros_like(req)
    for a in range(table.shape[0]):
        stored = jnp.where(req == a, table[a], stored)
    owner = lax.div(stored, per_dev)
    slot = stored - owner * per_dev
    pad = -(-n_wide // 16) * 16
    hit = owner == (iota((pad, rows), 0) ^ me)
    earlier = (iota((rows, rows), 0) <= iota((rows, rows), 1)).astype(BF16)
    count = jnp.dot(hit.astype(BF16), earlier, preferred_element_type=F32)
    return jnp.where(hit, count.astype(jnp.int32) - 1, -1), slot


def dispatch_kernel(order, n_wide, per_dev, cap, req_hbm, table_hbm, tok_hbm, gain_hbm, *refs):
    xs = refs[: len(order)]
    wide_gain_ref, req_ref, table_ref, tok_ref, gain_ref, x_ref, sems, out_sems = refs[
        len(order) :
    ]
    rows, depth = tok_ref.shape
    height = x_ref.shape[1]
    loads = [
        pltpu.make_async_copy(req_hbm, req_ref, sems.at[0]),
        pltpu.make_async_copy(table_hbm, table_ref, sems.at[1]),
        pltpu.make_async_copy(tok_hbm, tok_ref, sems.at[2]),
        pltpu.make_async_copy(gain_hbm, gain_ref, sems.at[3]),
    ]
    for copy in loads:
        copy.start()
    loads[0].wait()
    loads[1].wait()
    place, slot = places(req_ref[...], table_ref, n_wide, per_dev)
    slots = jnp.broadcast_to(slot.astype(F32), (16, rows)).astype(BF16)
    picks, slot_rows = [], []
    for k in order:
        pick = (iota((HEAD, rows), 0) == place[k : k + 1]).astype(BF16)
        slot_rows.append(
            lax.dot_general(slots, pick, (((1,), (1,)), ((), ())), preferred_element_type=F32)
        )
        picks.append(pick[:height])
    loads[3].wait()
    wide_gain_ref[...] = gain_ref[...].astype(F32)
    loads[2].wait()
    stores = []
    for j, k in enumerate(order):
        y = jnp.dot(picks[j], tok_ref[...], preferred_element_type=F32)
        first = jnp.where(iota((height, HEAD), 0) == cap, slot_rows[j][:1], y[:, :HEAD])
        x_ref[j, :, :HEAD] = first.astype(BF16)
        x_ref[j, :, HEAD:] = y[:, HEAD:].astype(BF16)
        copy = pltpu.make_async_copy(x_ref.at[j], xs[j], out_sems.at[j])
        copy.start()
        stores.append(copy)
    for copy in stores:
        copy.wait()


def base_kernel(offsets, cols, gain_hbm, tok_hbm, weight_hbm, *refs):
    count = len(offsets)
    outs = refs[:count]
    gain_ref, tok_ref, buf, acc_ref, sems = refs[count:]
    steps, chunk, _ = buf.shape
    copies = [
        pltpu.make_async_copy(weight_hbm.at[pl.ds(i * chunk, chunk)], buf.at[i], sems.at[2 + i])
        for i in range(steps)
    ]
    loads = [
        pltpu.make_async_copy(gain_hbm, gain_ref, sems.at[0]),
        pltpu.make_async_copy(tok_hbm, tok_ref, sems.at[1]),
    ]
    for copy in loads + copies:
        copy.start()
    for copy in loads:
        copy.wait()
    spot = lax.axis_index("tensor").astype(jnp.int32)
    for i in range(steps):
        pieces = []
        for b in range(i * chunk // HEAD, (i + 1) * chunk // HEAD):
            piece = tok_ref[:, b * HEAD : (b + 1) * HEAD].astype(F32) * gain_ref[b : b + 1]
            pieces.append(piece.astype(BF16))
        x = jnp.concatenate(pieces, axis=1)
        copies[i].wait()
        for j, k in enumerate(offsets):
            start = pl.multiple_of((spot ^ k) * cols, HEAD)
            y = jnp.dot(x, buf[i, :, pl.ds(start, cols)], preferred_element_type=F32)
            if i > 0:
                y = y + acc_ref[j]
            if i < steps - 1:
                acc_ref[j] = y
            else:
                outs[j][...] = y.astype(outs[j].dtype)


def pair_kernel(count, start, base_ref, near_ref, *refs):
    refs[-1][...] = base_ref[...] + near_ref[...].astype(F32)
    for j in range(count):
        out_ref = refs[2 * count + j]
        rows = slice(start, start + out_ref.shape[0])
        out_ref[...] = (refs[j][rows] + refs[count + j][rows].astype(F32)).astype(BF16)


def pair_low_kernel(count, low_ref, other_ref, *refs):
    outs = refs[2 * count :]
    cols = refs[0].shape[1]
    half = refs[0].shape[0] // 2
    for j in range(count):
        total = (refs[j][:half] + refs[count + j][:half].astype(F32)).astype(BF16)
        for h in range(cols // HEAD):
            outs[j][h * half : (h + 1) * half] = total[:, h * HEAD : (h + 1) * HEAD]
    base = cols // HEAD * half
    groups, height, _ = low_ref.shape
    for i in range(groups):
        total = low_ref[i].astype(F32) + other_ref[i].astype(F32)
        outs[0][base + i * height : base + (i + 1) * height] = total.astype(BF16)


def scaled_down_kernel(gain_ref, down_hbm, out_ref, buf, sems):
    per_dev, depth, rank = down_hbm.shape
    copies = [pltpu.make_async_copy(down_hbm.at[a], buf.at[a], sems.at[a]) for a in range(per_dev)]
    for copy in copies:
        copy.start()
    columns = []
    for b in range(depth // HEAD):
        columns.append(to_column(gain_ref[b : b + 1], HEAD))
    for a in range(per_dev):
        copies[a].wait()
        for b in range(depth // HEAD):
            span = slice(b * HEAD, (b + 1) * HEAD)
            out_ref[span, a * rank : (a + 1) * rank] = (
                buf[a, span].astype(F32) * columns[b]
            ).astype(BF16)


def aux_kernel(n_wide, per_dev, near_ref, req_hbm, table_hbm, tok_hbm, sq_ref, *refs):
    sels = refs[:n_wide]
    sent_ref, req_ref, table_ref, tok_ref, sems = refs[n_wide:]
    copies = [
        pltpu.make_async_copy(req_hbm, req_ref, sems.at[0]),
        pltpu.make_async_copy(table_hbm, table_ref, sems.at[1]),
        pltpu.make_async_copy(tok_hbm, tok_ref, sems.at[2]),
    ]
    for copy in copies:
        copy.start()
    sent_ref[...] = near_ref[...]
    for copy in copies:
        copy.wait()
    rows = tok_ref.shape[0]
    place, _ = places(req_ref[...], table_ref, n_wide, per_dev)
    place = place.astype(F32)
    for k in range(n_wide):
        column = to_column(place[k : k + 1], rows).astype(jnp.int32)
        sels[k][...] = (iota((rows, HEAD), 1) == column).astype(BF16)
    tok = tok_ref[...]
    gram = lax.dot_general(tok, tok, (((1,), (1,)), ((), ())), preferred_element_type=F32)
    diag = iota((rows, rows), 0) == iota((rows, rows), 1)
    sq = jnp.sum(jnp.where(diag, gram, 0.0), axis=0, keepdims=True)
    block = jnp.zeros((8, HEAD), F32)
    for p in range(3):
        part = sq.astype(BF16).astype(F32)
        sq = sq - part
        for i in range(rows // HEAD):
            term = part[:, i * HEAD : (i + 1) * HEAD]
            block = jnp.where(iota((8, HEAD), 0) == p * (rows // HEAD) + i, term, block)
    sq_ref[...] = block


def slot_column(x_ref, cap):
    height = x_ref.shape[0]
    base = cap // 16 * 16
    row = x_ref[base : base + 16, :HEAD].astype(F32)[cap - base : cap - base + 1]
    column = to_column(row, height)
    return jnp.where(iota((height, 1), 0) < cap, column, -1.0)


def down_kernel(count, cap, with_sq, *refs):
    xs, down_ref = refs[:count], refs[count]
    sq_ref = refs[count + 1] if with_sq else None
    out_ref = refs[-1]
    height, depth = xs[0].shape
    rank = HEAD
    x = jnp.concatenate([x[...] for x in xs], axis=0) if count > 1 else xs[0][...]
    slot = [slot_column(x, cap) for x in xs]
    slot = jnp.concatenate(slot, axis=0) if count > 1 else slot[0]
    low = jnp.zeros((count * height, rank), F32)
    for g in range(down_ref.shape[1] // (2 * rank)):
        y = jnp.dot(
            x, down_ref[:, 2 * g * rank : 2 * (g + 1) * rank], preferred_element_type=F32
        )
        low = jnp.where(slot == 2 * g, y[:, :rank], low)
        low = jnp.where(slot == 2 * g + 1, y[:, rank:], low)
    for j in range(count):
        part = low[j * height : (j + 1) * height]
        if j == 0 and with_sq:
            tail = [jnp.zeros((cap, rank), F32), sq_ref[...]]
            if height > cap + 8:
                tail.append(jnp.zeros((height - cap - 8, rank), F32))
            part = part + jnp.concatenate(tail, axis=0)
        out_ref[j] = part.astype(BF16)


def low_term(ref, i, groups, height):
    if len(ref.shape) == 3:
        return ref[i].astype(F32)
    start = ref.shape[0] - (groups - i) * height
    return ref[start : start + height].astype(F32)


def low_sum_kernel(left_ref, right_ref, out_ref):
    groups, height, _ = out_ref.shape
    for i in range(groups):
        left = low_term(left_ref, i, groups, height)
        out_ref[i] = (left + low_term(right_ref, i, groups, height)).astype(BF16)


def head_is_key(heads, h):
    if heads % 2 == 0:
        return h % 2 == 0
    return (lax.axis_index("tensor").astype(jnp.int32) * heads + h) % 2 == 0


def up_kernel(count, n_parts, cap, with_sq, *refs):
    xs = refs[:count]
    parts = refs[count : count + n_parts]
    up_ref = refs[count + n_parts]
    outs = refs[count + n_parts + 1 :]
    per_dev, half, cols = up_ref.shape
    heads = cols // HEAD
    height, rank = outs[0].shape[0], 2 * half
    up = up_ref[...].reshape(per_dev * half, cols)
    sums = []
    for j in range(count):
        terms = [low_term(part, j, count, height) for part in parts]
        sums.append(sum(terms[1:], terms[0]))
    if with_sq:
        outs[count][...] = sums[0][cap : cap + 8]
    low = jnp.concatenate(sums, axis=0) if count > 1 else sums[0]
    slot = [slot_column(x, cap) for x in xs]
    slot = jnp.concatenate(slot, axis=0) if count > 1 else slot[0]
    left = iota((count * height, rank), 1) < half
    turned = pltpu.roll(low, half, 1)
    wide = []
    for source in (jnp.where(left, low, turned), jnp.where(left, turned, low)):
        pieces = []
        for g in range(per_dev // 2):
            mine = slot == jnp.where(left, 2.0 * g, 2.0 * g + 1)
            pieces.append(jnp.where(mine, source, 0.0).astype(BF16))
        wide.append(jnp.concatenate(pieces, axis=1))
    for h in range(heads):
        key = head_is_key(heads, h)
        if isinstance(key, bool):
            lhs = wide[0] if key else wide[1]
        else:
            lhs = jnp.where(key, wide[0].astype(F32), wide[1].astype(F32)).astype(BF16)
        span = slice(h * HEAD, (h + 1) * HEAD)
        y = jnp.dot(lhs, up[:, span], preferred_element_type=F32).astype(BF16)
        for j in range(count):
            outs[j][:, span] = y[j * height : (j + 1) * height]


def placed(sels, deltas):
    height, cols = deltas[0].shape
    blocks = []
    for delta in deltas:
        blocks.append(delta[...])
        if height < HEAD:
            blocks.append(jnp.zeros((HEAD - height, cols), BF16))
    lhs = jnp.concatenate([sel[...] for sel in sels], axis=1) if len(sels) > 1 else sels[0][...]
    return jnp.dot(lhs, jnp.concatenate(blocks, axis=0), preferred_element_type=F32)


def gather_kernel(n_pairs, count, sq_ref, base_ref, *refs):
    tops, bottoms = refs[:n_pairs], refs[n_pairs : 2 * n_pairs]
    deltas = refs[2 * n_pairs : 2 * n_pairs + count]
    sels = refs[2 * n_pairs + count : 2 * n_pairs + 2 * count]
    out_ref, scale_ref = refs[-2:]
    rows, cols = out_ref.shape
    pieces = rows // HEAD
    squares = []
    for i in range(pieces):
        total = sq_ref[i : i + 1]
        for p in range(1, 3):
            total = total + sq_ref[p * pieces + i : p * pieces + i + 1]
        squares.append(total)
    square = to_column(jnp.concatenate(squares, axis=1), rows)
    scale = lax.rsqrt(square * (1.0 / MODEL_WIDTH) + EPSILON)
    scale_ref[...] = jnp.broadcast_to(scale, (rows, HEAD))
    total = base_ref[...] + placed(sels, deltas)
    half = rows // 2
    lower = total[half:]
    for bottom in bottoms:
        lower = lower + bottom[...].astype(F32)
    out_ref[half:] = lower
    for h in range(cols // HEAD):
        span = slice(h * HEAD, (h + 1) * HEAD)
        upper = total[:half, span]
        for top in tops:
            upper = upper + top[h * half : (h + 1) * half].astype(F32)
        out_ref[:half, span] = upper


def finish_kernel(count, sum_ref, scale_ref, cos_ref, sin_ref, *refs):
    deltas, sels, out_ref = refs[:count], refs[count : 2 * count], refs[2 * count]
    rows, cols = out_ref.shape
    total = sum_ref[...] + placed(sels, deltas)
    heads = cols // HEAD
    scale = scale_ref[...]
    for h in range(heads):
        span = slice(h * HEAD, (h + 1) * HEAD)
        x = total[:, span] * scale
        key = head_is_key(heads, h)
        if key is False:
            out_ref[:, span] = x.astype(BF16)
            continue
        y = x * cos_ref[...] + pltpu.roll(x, HEAD // 2, 1) * sin_ref[...]
        if key is not True:
            y = jnp.where(key, y, x)
        out_ref[:, span] = y.astype(BF16)


def local(
    mesh_shape,
    tokens,
    attention_norm_gain,
    key_value_weight,
    adapter_down_weight,
    adapter_up_weight,
    request_adapter,
    adapter_storage_row,
    cached_token_length,
):
    n_wide, n_tensor = mesh_shape["wide"], mesh_shape["tensor"]
    rows, depth = tokens.shape
    per_dev, _, rank = adapter_down_weight.shape
    cols = adapter_up_weight.shape[2]
    cap = 104 if n_wide <= 4 else 64
    height = -(-(cap + 8) // 16) * 16
    req = request_adapter.reshape(1, rows)
    gain = attention_norm_gain.reshape(depth // HEAD, HEAD)

    def over(axis, array, k):
        size = mesh_shape[axis]
        return lax.ppermute(array, axis, [(i, i ^ k) for i in range(size)])

    small = [pltpu.VMEM((1, rows), jnp.int32), pltpu.SMEM(adapter_storage_row.shape, jnp.int32)]
    first, last = [0, 1], list(range(2, n_wide))

    def dispatch(order, after):
        *blocks, wide_gain = call(
            functools.partial(dispatch_kernel, order, n_wide, per_dev, cap),
            "dispatch",
            [shape((height, depth), BF16)] * len(order) + [shape(gain.shape, F32)],
            hbm=(req, adapter_storage_row, tokens, gain),
            hbm_outs=len(order),
            after=after,
            scratch=small
            + [
                pltpu.VMEM((rows, depth), BF16),
                pltpu.VMEM(gain.shape, BF16),
                pltpu.VMEM((len(order), height, depth), BF16),
                pltpu.SemaphoreType.DMA((4,)),
                pltpu.SemaphoreType.DMA((len(order),)),
            ],
            flops=2 * len(order) * height * rows * depth,
            moved=2 * rows * depth * 4,
            limit=63,
        )
        return blocks, wide_gain

    order = list(range(n_wide - 1, -1, -1))
    blocks, wide_gain = dispatch(order, ())
    held = [blocks[n_wide - 1 - k] for k in range(n_wide)]
    held[1:] = [over("wide", held[k], k) for k in range(1, n_wide)]

    twos = list(range(2, n_tensor, 2))
    far = [k ^ 1 for k in twos]
    offsets = far + [1] + twos + [0]
    chunk = math.gcd(depth, 512)
    steps = depth // chunk
    sums = call(
        functools.partial(base_kernel, offsets, cols),
        "base",
        [shape((rows, cols), BF16)] * (len(far) + 1) + [shape((rows, cols), F32)] * (len(twos) + 1),
        hbm=(wide_gain, tokens, key_value_weight),
        scratch=[
            pltpu.VMEM(gain.shape, F32),
            pltpu.VMEM((rows, depth), BF16),
            pltpu.VMEM((steps, chunk, key_value_weight.shape[1]), BF16),
            pltpu.VMEM((len(offsets), rows, cols), F32),
            pltpu.SemaphoreType.DMA((2 + steps,)),
        ],
        flops=2 * rows * depth * cols * n_tensor,
        moved=2 * depth * cols * n_tensor,
        limit=52,
    )
    away, near, own, base = sums[: len(far)], sums[len(far)], sums[len(far) + 1 : -1], sums[-1]
    beside = [over("tensor", p, 1) for p in away]
    (down,) = call(
        scaled_down_kernel,
        "scaled_down",
        [shape((depth, per_dev * rank), BF16)],
        vmem=(wide_gain,),
        hbm=(adapter_down_weight,),
        after=(base,),
        scratch=[
            pltpu.VMEM((per_dev, depth, rank), BF16),
            pltpu.SemaphoreType.DMA((per_dev,)),
        ],
        flops=4 * depth * per_dev * rank,
        moved=4 * depth * per_dev * rank,
    )
    half_size = HEAD // 2
    freq_index = jnp.arange(half_size).astype(F32)
    inverse = jnp.exp(freq_index * (-2.0 / HEAD) * math.log(ROPE_BASE))
    angles = cached_token_length.astype(F32)[:, None] * inverse[None, :]
    cosine, sine = jnp.cos(angles), jnp.sin(angles)
    cosine = jnp.concatenate([cosine, cosine], axis=1)
    sine = jnp.concatenate([-sine, sine], axis=1)

    def down_block(group, extra, after):
        xs = [held[k] for k in group]
        (low,) = call(
            functools.partial(down_kernel, len(xs), cap, bool(extra)),
            "down_block",
            [shape((len(xs), height, rank), BF16)],
            vmem=(*xs, down, *extra),
            after=after,
            flops=2 * len(xs) * height * depth * rank * per_dev,
            moved=2 * per_dev * depth * rank,
        )
        return low

    def up_block(group, parts, with_sq, after):
        xs = [held[k] for k in group]
        outs = [shape((height, cols), BF16)] * len(xs)
        if with_sq:
            outs = outs + [shape((8, HEAD), F32)]
        return call(
            functools.partial(up_kernel, len(xs), len(parts), cap, with_sq),
            "up_block",
            outs,
            vmem=(*xs, *parts, adapter_up_weight),
            after=after,
            flops=2 * len(xs) * height * per_dev * rank * cols,
            moved=2 * per_dev * rank * cols,
        )

    low = down_block(first, (), ())
    sq, *sels, near = call(
        functools.partial(aux_kernel, n_wide, per_dev),
        "aux",
        [shape((8, HEAD), F32)]
        + [shape((rows, HEAD), BF16)] * n_wide
        + [shape((rows, cols), BF16)],
        vmem=(near,),
        hbm=(req, adapter_storage_row, tokens),
        after=(low,),
        scratch=small + [pltpu.VMEM((rows, depth), BF16), pltpu.SemaphoreType.DMA((3,))],
        flops=2 * rows * rows * depth,
        moved=2 * rows * depth,
    )
    half = rows // 2
    upper = cols // HEAD * half
    other = over("tensor", low, 1)
    near = over("tensor", near, 1)
    pairs = call(
        functools.partial(pair_low_kernel, len(twos)),
        "pair_low_sums",
        [shape((upper + len(first) * height, HEAD), BF16)]
        + [shape((upper, HEAD), BF16)] * (len(twos) - 1),
        vmem=(low, other, *own, *beside),
        after=(sq, cosine, sine),
    )
    tops = [over("tensor", p, k) for p, k in zip(pairs, twos)]
    done = pairs[0]
    low, other = pairs[0], tops[0]
    for step in range(2, n_tensor.bit_length() - 1):
        (low,) = call(
            low_sum_kernel,
            "low_sum",
            [shape((len(first), height, rank), BF16)],
            vmem=(low, other),
        )
        other = over("tensor", low, 2**step)
    low_last = down_block(last, (sq,), (done,))
    last_parts = [low_last] + [over("tensor", low_last, k) for k in range(n_tensor - 1, 0, -1)]
    ups = up_block(first, [low, other], False, (low_last,))
    deltas = [u if k == 0 else over("wide", u, k) for k, u in zip(first, ups)]
    *pairs, base = call(
        functools.partial(pair_kernel, len(twos), half),
        "pair_sums",
        [shape((half, cols), BF16)] * len(twos) + [shape((rows, cols), F32)],
        vmem=(base, near, *own, *beside),
        after=(ups[0],),
    )
    bottoms = [over("tensor", p, k) for p, k in zip(pairs, twos)]
    *ups, square = up_block(last, last_parts, True, (pairs[0],))
    last_deltas = [over("wide", u, k) for k, u in zip(last, ups)]
    total, scale = call(
        functools.partial(gather_kernel, len(bottoms), len(first)),
        "gather",
        [shape((rows, cols), F32), shape((rows, HEAD), F32)],
        vmem=(square, base, *tops, *bottoms, *deltas, *[sels[k] for k in first]),
        after=(ups[0],),
        flops=2 * rows * cols * HEAD * len(first),
    )
    return call(
        functools.partial(finish_kernel, len(last)),
        "finish",
        [shape((rows, cols), BF16)],
        vmem=(total, scale, cosine, sine, *last_deltas, *[sels[k] for k in last]),
        flops=2 * rows * cols * HEAD,
    )[0]


def solution(mesh):
    return jax.shard_map(
        functools.partial(local, dict(mesh.shape)),
        mesh=mesh,
        in_specs=(
            P(("parts", "wide"), "tensor"),
            P("tensor"),
            P("tensor", None),
            P(("parts", "wide"), "tensor", None),
            P(("parts", "wide"), None, "tensor"),
            P(("parts", "wide")),
            P("parts"),
            P(("parts", "wide")),
        ),
        out_specs=P(("parts", "wide"), "tensor"),
        check_vma=False,
    )
```

```python
import functools
import math

import jax
import jax.numpy as jnp
from jax import lax
from jax.experimental import pallas as pl
from jax.experimental.pallas import tpu as pltpu
from jax.sharding import PartitionSpec as P

MODEL_WIDTH = 8192
HEAD = 128
EPSILON = 1e-05
ROPE_BASE = 500000.0
F32 = jnp.float32
BF16 = jnp.bfloat16


def iota(shape, axis):
    return lax.broadcasted_iota(jnp.int32, shape, axis)


def call(kernel, name, outs, vmem=(), hbm=(), after=(), scratch=(), flops=0, moved=0, limit=16, hbm_outs=0):
    def body(*refs):
        keep = len(vmem) + len(hbm)
        kernel(*refs[:keep], *refs[keep + len(after) :])

    return pl.pallas_call(
        body,
        out_shape=outs,
        in_specs=[pl.BlockSpec(memory_space=pltpu.VMEM)] * len(vmem)
        + [pl.BlockSpec(memory_space=pltpu.HBM)] * len(hbm)
        + [pl.BlockSpec(memory_space=pl.ANY)] * len(after),
        out_specs=[pl.BlockSpec(memory_space=pltpu.HBM)] * hbm_outs
        + [pl.BlockSpec(memory_space=pltpu.VMEM)] * (len(outs) - hbm_outs),
        scratch_shapes=scratch,
        compiler_params=pltpu.CompilerParams(vmem_limit_bytes=limit * 1024 * 1024),
        cost_estimate=pl.CostEstimate(flops=flops, bytes_accessed=moved, transcendentals=0),
        name=name,
    )(*vmem, *hbm, *after)


def shape(dims, dtype):
    return jax.ShapeDtypeStruct(dims, dtype)


def to_column(row, count):
    spread = iota((count, row.shape[1]), 0) == iota((count, row.shape[1]), 1)
    return jnp.sum(jnp.where(spread, row, 0.0), axis=1, keepdims=True)


def places(req, table, n_wide, per_dev):
    rows = req.shape[1]
    me = lax.axis_index("wide").astype(jnp.int32)
    stored = jnp.zeros_like(req)
    for a in range(table.shape[0]):
        stored = jnp.where(req == a, table[a], stored)
    owner = lax.div(stored, per_dev)
    slot = stored - owner * per_dev
    pad = -(-n_wide // 16) * 16
    hit = owner == (iota((pad, rows), 0) ^ me)
    earlier = (iota((rows, rows), 0) <= iota((rows, rows), 1)).astype(BF16)
    count = jnp.dot(hit.astype(BF16), earlier, preferred_element_type=F32)
    return jnp.where(hit, count.astype(jnp.int32) - 1, -1), slot


def dispatch_kernel(order, n_wide, per_dev, cap, req_hbm, table_hbm, tok_hbm, gain_hbm, *refs):
    xs = refs[: len(order)]
    wide_gain_ref, req_ref, table_ref, tok_ref, gain_ref, x_ref, sems, out_sems = refs[
        len(order) :
    ]
    rows, depth = tok_ref.shape
    height = x_ref.shape[1]
    loads = [
        pltpu.make_async_copy(req_hbm, req_ref, sems.at[0]),
        pltpu.make_async_copy(table_hbm, table_ref, sems.at[1]),
        pltpu.make_async_copy(tok_hbm, tok_ref, sems.at[2]),
        pltpu.make_async_copy(gain_hbm, gain_ref, sems.at[3]),
    ]
    for copy in loads:
        copy.start()
    loads[0].wait()
    loads[1].wait()
    place, slot = places(req_ref[...], table_ref, n_wide, per_dev)
    slots = jnp.broadcast_to(slot.astype(F32), (16, rows)).astype(BF16)
    picks, slot_rows = [], []
    for k in order:
        pick = (iota((HEAD, rows), 0) == place[k : k + 1]).astype(BF16)
        slot_rows.append(
            lax.dot_general(slots, pick, (((1,), (1,)), ((), ())), preferred_element_type=F32)
        )
        picks.append(pick[:height])
    loads[3].wait()
    wide_gain_ref[...] = gain_ref[...].astype(F32)
    loads[2].wait()
    stores = []
    for j, k in enumerate(order):
        y = jnp.dot(picks[j], tok_ref[...], preferred_element_type=F32)
        first = jnp.where(iota((height, HEAD), 0) == cap, slot_rows[j][:1], y[:, :HEAD])
        x_ref[j, :, :HEAD] = first.astype(BF16)
        x_ref[j, :, HEAD:] = y[:, HEAD:].astype(BF16)
        copy = pltpu.make_async_copy(x_ref.at[j], xs[j], out_sems.at[j])
        copy.start()
        stores.append(copy)
    for copy in stores:
        copy.wait()


def base_kernel(offsets, cols, gain_hbm, tok_hbm, weight_hbm, *refs):
    count = len(offsets)
    outs = refs[:count]
    gain_ref, tok_ref, buf, acc_ref, sems = refs[count:]
    steps, chunk, _ = buf.shape
    copies = [
        pltpu.make_async_copy(weight_hbm.at[pl.ds(i * chunk, chunk)], buf.at[i], sems.at[2 + i])
        for i in range(steps)
    ]
    loads = [
        pltpu.make_async_copy(gain_hbm, gain_ref, sems.at[0]),
        pltpu.make_async_copy(tok_hbm, tok_ref, sems.at[1]),
    ]
    for copy in loads + copies:
        copy.start()
    for copy in loads:
        copy.wait()
    spot = lax.axis_index("tensor").astype(jnp.int32)
    for i in range(steps):
        pieces = []
        for b in range(i * chunk // HEAD, (i + 1) * chunk // HEAD):
            piece = tok_ref[:, b * HEAD : (b + 1) * HEAD].astype(F32) * gain_ref[b : b + 1]
            pieces.append(piece.astype(BF16))
        x = jnp.concatenate(pieces, axis=1)
        copies[i].wait()
        for j, k in enumerate(offsets):
            start = pl.multiple_of((spot ^ k) * cols, HEAD)
            y = jnp.dot(x, buf[i, :, pl.ds(start, cols)], preferred_element_type=F32)
            if i > 0:
                y = y + acc_ref[j]
            if i < steps - 1:
                acc_ref[j] = y
            else:
                outs[j][...] = y.astype(outs[j].dtype)


def pair_kernel(count, start, *refs):
    for j in range(count):
        out_ref = refs[2 * count + j]
        rows = slice(start, start + out_ref.shape[0])
        out_ref[...] = (refs[j][rows] + refs[count + j][rows].astype(F32)).astype(BF16)


def pair_low_kernel(count, low_ref, other_ref, *refs):
    outs = refs[2 * count :]
    cols = refs[0].shape[1]
    half = refs[0].shape[0] // 2
    for j in range(count):
        total = (refs[j][:half] + refs[count + j][:half].astype(F32)).astype(BF16)
        for h in range(cols // HEAD):
            outs[j][h * half : (h + 1) * half] = total[:, h * HEAD : (h + 1) * HEAD]
    base = cols // HEAD * half
    groups, height, _ = low_ref.shape
    for i in range(groups):
        total = low_ref[i].astype(F32) + other_ref[i].astype(F32)
        outs[0][base + i * height : base + (i + 1) * height] = total.astype(BF16)


def scaled_down_kernel(gain_ref, down_hbm, out_ref, buf, sems):
    per_dev, depth, rank = down_hbm.shape
    copies = [pltpu.make_async_copy(down_hbm.at[a], buf.at[a], sems.at[a]) for a in range(per_dev)]
    for copy in copies:
        copy.start()
    columns = []
    for b in range(depth // HEAD):
        columns.append(to_column(gain_ref[b : b + 1], HEAD))
    for a in range(per_dev):
        copies[a].wait()
        for b in range(depth // HEAD):
            span = slice(b * HEAD, (b + 1) * HEAD)
            out_ref[span, a * rank : (a + 1) * rank] = (
                buf[a, span].astype(F32) * columns[b]
            ).astype(BF16)


def aux_kernel(n_wide, per_dev, req_hbm, table_hbm, tok_hbm, sq_ref, *refs):
    sels = refs[:n_wide]
    req_ref, table_ref, tok_ref, sems = refs[n_wide:]
    copies = [
        pltpu.make_async_copy(req_hbm, req_ref, sems.at[0]),
        pltpu.make_async_copy(table_hbm, table_ref, sems.at[1]),
        pltpu.make_async_copy(tok_hbm, tok_ref, sems.at[2]),
    ]
    for copy in copies:
        copy.start()
    for copy in copies:
        copy.wait()
    rows = tok_ref.shape[0]
    place, _ = places(req_ref[...], table_ref, n_wide, per_dev)
    place = place.astype(F32)
    for k in range(n_wide):
        column = to_column(place[k : k + 1], rows).astype(jnp.int32)
        sels[k][...] = (iota((rows, HEAD), 1) == column).astype(BF16)
    tok = tok_ref[...]
    gram = lax.dot_general(tok, tok, (((1,), (1,)), ((), ())), preferred_element_type=F32)
    diag = iota((rows, rows), 0) == iota((rows, rows), 1)
    sq = jnp.sum(jnp.where(diag, gram, 0.0), axis=0, keepdims=True)
    block = jnp.zeros((8, HEAD), F32)
    for p in range(3):
        part = sq.astype(BF16).astype(F32)
        sq = sq - part
        for i in range(rows // HEAD):
            term = part[:, i * HEAD : (i + 1) * HEAD]
            block = jnp.where(iota((8, HEAD), 0) == p * (rows // HEAD) + i, term, block)
    sq_ref[...] = block


def slot_column(x_ref, cap):
    height = x_ref.shape[0]
    base = cap // 16 * 16
    row = x_ref[base : base + 16, :HEAD].astype(F32)[cap - base : cap - base + 1]
    column = to_column(row, height)
    return jnp.where(iota((height, 1), 0) < cap, column, -1.0)


def down_kernel(count, cap, with_sq, *refs):
    xs, down_ref = refs[:count], refs[count]
    sq_ref = refs[count + 1] if with_sq else None
    out_ref = refs[-1]
    height, depth = xs[0].shape
    rank = HEAD
    x = jnp.concatenate([x[...] for x in xs], axis=0) if count > 1 else xs[0][...]
    slot = [slot_column(x, cap) for x in xs]
    slot = jnp.concatenate(slot, axis=0) if count > 1 else slot[0]
    low = jnp.zeros((count * height, rank), F32)
    for g in range(down_ref.shape[1] // (2 * rank)):
        y = jnp.dot(
            x, down_ref[:, 2 * g * rank : 2 * (g + 1) * rank], preferred_element_type=F32
        )
        low = jnp.where(slot == 2 * g, y[:, :rank], low)
        low = jnp.where(slot == 2 * g + 1, y[:, rank:], low)
    for j in range(count):
        part = low[j * height : (j + 1) * height]
        if j == 0 and with_sq:
            tail = [jnp.zeros((cap, rank), F32), sq_ref[...]]
            if height > cap + 8:
                tail.append(jnp.zeros((height - cap - 8, rank), F32))
            part = part + jnp.concatenate(tail, axis=0)
        out_ref[j] = part.astype(BF16)


def low_term(ref, i, groups, height):
    if len(ref.shape) == 3:
        return ref[i].astype(F32)
    start = ref.shape[0] - (groups - i) * height
    return ref[start : start + height].astype(F32)


def low_sum_kernel(left_ref, right_ref, out_ref):
    groups, height, _ = out_ref.shape
    for i in range(groups):
        left = low_term(left_ref, i, groups, height)
        out_ref[i] = (left + low_term(right_ref, i, groups, height)).astype(BF16)


def head_is_key(heads, h):
    if heads % 2 == 0:
        return h % 2 == 0
    return (lax.axis_index("tensor").astype(jnp.int32) * heads + h) % 2 == 0


def up_kernel(count, n_parts, cap, with_sq, *refs):
    xs = refs[:count]
    parts = refs[count : count + n_parts]
    up_ref = refs[count + n_parts]
    outs = refs[count + n_parts + (2 if with_sq else 1) :]
    per_dev, half, cols = up_ref.shape
    heads = cols // HEAD
    height, rank = outs[0].shape[0], 2 * half
    up = up_ref[...].reshape(per_dev * half, cols)
    sums = []
    for j in range(count):
        terms = [low_term(part, j, count, height) for part in parts]
        sums.append(sum(terms[1:], terms[0]))
    if with_sq:
        outs[count][...] = sums[0][cap : cap + 8]
        outs[count + 1][...] = refs[count + n_parts + 1][...]
    low = jnp.concatenate(sums, axis=0) if count > 1 else sums[0]
    slot = [slot_column(x, cap) for x in xs]
    slot = jnp.concatenate(slot, axis=0) if count > 1 else slot[0]
    left = iota((count * height, rank), 1) < half
    turned = pltpu.roll(low, half, 1)
    wide = []
    for source in (jnp.where(left, low, turned), jnp.where(left, turned, low)):
        pieces = []
        for g in range(per_dev // 2):
            mine = slot == jnp.where(left, 2.0 * g, 2.0 * g + 1)
            pieces.append(jnp.where(mine, source, 0.0).astype(BF16))
        wide.append(jnp.concatenate(pieces, axis=1))
    for h in range(heads):
        key = head_is_key(heads, h)
        if isinstance(key, bool):
            lhs = wide[0] if key else wide[1]
        else:
            lhs = jnp.where(key, wide[0].astype(F32), wide[1].astype(F32)).astype(BF16)
        span = slice(h * HEAD, (h + 1) * HEAD)
        y = jnp.dot(lhs, up[:, span], preferred_element_type=F32).astype(BF16)
        for j in range(count):
            outs[j][:, span] = y[j * height : (j + 1) * height]


def placed(sels, deltas):
    height, cols = deltas[0].shape
    blocks = []
    for delta in deltas:
        blocks.append(delta[...])
        if height < HEAD:
            blocks.append(jnp.zeros((HEAD - height, cols), BF16))
    lhs = jnp.concatenate([sel[...] for sel in sels], axis=1) if len(sels) > 1 else sels[0][...]
    return jnp.dot(lhs, jnp.concatenate(blocks, axis=0), preferred_element_type=F32)


def gather_kernel(n_pairs, count, sq_ref, base_ref, *refs):
    tops, bottoms = refs[:n_pairs], refs[n_pairs : 2 * n_pairs]
    deltas = refs[2 * n_pairs : 2 * n_pairs + count]
    sels = refs[2 * n_pairs + count : 2 * n_pairs + 2 * count]
    out_ref, scale_ref = refs[-2:]
    rows, cols = out_ref.shape
    pieces = rows // HEAD
    squares = []
    for i in range(pieces):
        total = sq_ref[i : i + 1]
        for p in range(1, 3):
            total = total + sq_ref[p * pieces + i : p * pieces + i + 1]
        squares.append(total)
    square = to_column(jnp.concatenate(squares, axis=1), rows)
    scale = lax.rsqrt(square * (1.0 / MODEL_WIDTH) + EPSILON)
    scale_ref[...] = jnp.broadcast_to(scale, (rows, HEAD))
    total = base_ref[...] + placed(sels, deltas)
    half = rows // 2
    lower = total[half:]
    for bottom in bottoms:
        lower = lower + bottom[...].astype(F32)
    out_ref[half:] = lower
    for h in range(cols // HEAD):
        span = slice(h * HEAD, (h + 1) * HEAD)
        upper = total[:half, span]
        for top in tops:
            upper = upper + top[h * half : (h + 1) * half].astype(F32)
        out_ref[:half, span] = upper


def finish_kernel(count, sum_ref, near_ref, scale_ref, cos_ref, sin_ref, *refs):
    deltas, sels, out_ref = refs[:count], refs[count : 2 * count], refs[2 * count]
    rows, cols = out_ref.shape
    total = sum_ref[...] + near_ref[...].astype(F32) + placed(sels, deltas)
    heads = cols // HEAD
    scale = scale_ref[...]
    for h in range(heads):
        span = slice(h * HEAD, (h + 1) * HEAD)
        x = total[:, span] * scale
        key = head_is_key(heads, h)
        if key is False:
            out_ref[:, span] = x.astype(BF16)
            continue
        y = x * cos_ref[...] + pltpu.roll(x, HEAD // 2, 1) * sin_ref[...]
        if key is not True:
            y = jnp.where(key, y, x)
        out_ref[:, span] = y.astype(BF16)


def local(
    mesh_shape,
    tokens,
    attention_norm_gain,
    key_value_weight,
    adapter_down_weight,
    adapter_up_weight,
    request_adapter,
    adapter_storage_row,
    cached_token_length,
):
    n_wide, n_tensor = mesh_shape["wide"], mesh_shape["tensor"]
    rows, depth = tokens.shape
    per_dev, _, rank = adapter_down_weight.shape
    cols = adapter_up_weight.shape[2]
    cap = 104 if n_wide <= 4 else 64
    height = -(-(cap + 8) // 16) * 16
    req = request_adapter.reshape(1, rows)
    gain = attention_norm_gain.reshape(depth // HEAD, HEAD)

    def over(axis, array, k):
        size = mesh_shape[axis]
        return lax.ppermute(array, axis, [(i, i ^ k) for i in range(size)])

    small = [pltpu.VMEM((1, rows), jnp.int32), pltpu.SMEM(adapter_storage_row.shape, jnp.int32)]
    first, last = [0, 1], list(range(2, n_wide))

    def dispatch(order, after):
        *blocks, wide_gain = call(
            functools.partial(dispatch_kernel, order, n_wide, per_dev, cap),
            "dispatch",
            [shape((height, depth), BF16)] * len(order) + [shape(gain.shape, F32)],
            hbm=(req, adapter_storage_row, tokens, gain),
            hbm_outs=len(order),
            after=after,
            scratch=small
            + [
                pltpu.VMEM((rows, depth), BF16),
                pltpu.VMEM(gain.shape, BF16),
                pltpu.VMEM((len(order), height, depth), BF16),
                pltpu.SemaphoreType.DMA((4,)),
                pltpu.SemaphoreType.DMA((len(order),)),
            ],
            flops=2 * len(order) * height * rows * depth,
            moved=2 * rows * depth * 4,
            limit=63,
        )
        return blocks, wide_gain

    order = list(range(n_wide - 1, -1, -1))
    blocks, wide_gain = dispatch(order, ())
    held = [blocks[n_wide - 1 - k] for k in range(n_wide)]
    held[1:] = [over("wide", held[k], k) for k in range(1, n_wide)]

    twos = list(range(2, n_tensor, 2))
    far = [k ^ 1 for k in twos]
    offsets = far + [1] + twos + [0]
    chunk = math.gcd(depth, 512)
    steps = depth // chunk
    sums = call(
        functools.partial(base_kernel, offsets, cols),
        "base",
        [shape((rows, cols), BF16)] * (len(far) + 1) + [shape((rows, cols), F32)] * (len(twos) + 1),
        hbm=(wide_gain, tokens, key_value_weight),
        scratch=[
            pltpu.VMEM(gain.shape, F32),
            pltpu.VMEM((rows, depth), BF16),
            pltpu.VMEM((steps, chunk, key_value_weight.shape[1]), BF16),
            pltpu.VMEM((len(offsets), rows, cols), F32),
            pltpu.SemaphoreType.DMA((2 + steps,)),
        ],
        flops=2 * rows * depth * cols * n_tensor,
        moved=2 * depth * cols * n_tensor,
        limit=52,
    )
    away, near, own, base = sums[: len(far)], sums[len(far)], sums[len(far) + 1 : -1], sums[-1]
    beside = [over("tensor", p, 1) for p in away]
    (down,) = call(
        scaled_down_kernel,
        "scaled_down",
        [shape((depth, per_dev * rank), BF16)],
        vmem=(wide_gain,),
        hbm=(adapter_down_weight,),
        after=(base,),
        scratch=[
            pltpu.VMEM((per_dev, depth, rank), BF16),
            pltpu.SemaphoreType.DMA((per_dev,)),
        ],
        flops=4 * depth * per_dev * rank,
        moved=4 * depth * per_dev * rank,
    )
    half_size = HEAD // 2
    freq_index = jnp.arange(half_size).astype(F32)
    inverse = jnp.exp(freq_index * (-2.0 / HEAD) * math.log(ROPE_BASE))
    angles = cached_token_length.astype(F32)[:, None] * inverse[None, :]
    cosine, sine = jnp.cos(angles), jnp.sin(angles)
    cosine = jnp.concatenate([cosine, cosine], axis=1)
    sine = jnp.concatenate([-sine, sine], axis=1)

    def down_block(group, extra, after):
        xs = [held[k] for k in group]
        (low,) = call(
            functools.partial(down_kernel, len(xs), cap, bool(extra)),
            "down_block",
            [shape((len(xs), height, rank), BF16)],
            vmem=(*xs, down, *extra),
            after=after,
            flops=2 * len(xs) * height * depth * rank * per_dev,
            moved=2 * per_dev * depth * rank,
        )
        return low

    def up_block(group, parts, extra, after):
        xs = [held[k] for k in group]
        outs = [shape((height, cols), BF16)] * len(xs)
        if extra:
            outs = outs + [shape((8, HEAD), F32), shape((rows, cols), BF16)]
        return call(
            functools.partial(up_kernel, len(xs), len(parts), cap, bool(extra)),
            "up_block",
            outs,
            vmem=(*xs, *parts, adapter_up_weight, *extra),
            after=after,
            flops=2 * len(xs) * height * per_dev * rank * cols,
            moved=2 * per_dev * rank * cols,
        )

    low = down_block(first, (), ())
    sq, *sels = call(
        functools.partial(aux_kernel, n_wide, per_dev),
        "aux",
        [shape((8, HEAD), F32)]
        + [shape((rows, HEAD), BF16)] * n_wide,
        hbm=(req, adapter_storage_row, tokens),
        after=(low,),
        scratch=small + [pltpu.VMEM((rows, depth), BF16), pltpu.SemaphoreType.DMA((3,))],
        flops=2 * rows * rows * depth,
        moved=2 * rows * depth,
    )
    half = rows // 2
    upper = cols // HEAD * half
    other = over("tensor", low, 1)
    pairs = call(
        functools.partial(pair_low_kernel, len(twos)),
        "pair_low_sums",
        [shape((upper + len(first) * height, HEAD), BF16)]
        + [shape((upper, HEAD), BF16)] * (len(twos) - 1),
        vmem=(low, other, *own, *beside),
        after=(sq,),
    )
    tops = [over("tensor", p, k) for p, k in zip(pairs, twos)]
    done = pairs[0]
    low, other = pairs[0], tops[0]
    for step in range(2, n_tensor.bit_length() - 1):
        (low,) = call(
            low_sum_kernel,
            "low_sum",
            [shape((len(first), height, rank), BF16)],
            vmem=(low, other),
        )
        other = over("tensor", low, 2**step)
    low_last = down_block(last, (sq,), (done,))
    last_parts = [low_last] + [over("tensor", low_last, k) for k in range(n_tensor - 1, 0, -1)]
    ups = up_block(first, [low, other], (), (low_last,))
    deltas = [u if k == 0 else over("wide", u, k) for k, u in zip(first, ups)]
    pairs = call(
        functools.partial(pair_kernel, len(twos), half),
        "pair_sums",
        [shape((half, cols), BF16)] * len(twos),
        vmem=(*own, *beside),
        after=(ups[0],),
    )
    bottoms = [over("tensor", p, k) for p, k in zip(pairs, twos)]
    *ups, square, near = up_block(last, last_parts, (near,), (pairs[0],))
    near = over("tensor", near, 1)
    last_deltas = [over("wide", u, k) for k, u in zip(last, ups)]
    total, scale = call(
        functools.partial(gather_kernel, len(bottoms), len(first)),
        "gather",
        [shape((rows, cols), F32), shape((rows, HEAD), F32)],
        vmem=(square, base, *tops, *bottoms, *deltas, *[sels[k] for k in first]),
        after=(ups[0],),
        flops=2 * rows * cols * HEAD * len(first),
    )
    return call(
        functools.partial(finish_kernel, len(last)),
        "finish",
        [shape((rows, cols), BF16)],
        vmem=(total, near, scale, cosine, sine, *last_deltas, *[sels[k] for k in last]),
        flops=2 * rows * cols * HEAD,
    )[0]


def solution(mesh):
    return jax.shard_map(
        functools.partial(local, dict(mesh.shape)),
        mesh=mesh,
        in_specs=(
            P(("parts", "wide"), "tensor"),
            P("tensor"),
            P("tensor", None),
            P(("parts", "wide"), "tensor", None),
            P(("parts", "wide"), None, "tensor"),
            P(("parts", "wide")),
            P("parts"),
            P(("parts", "wide")),
        ),
        out_specs=P(("parts", "wide"), "tensor"),
        check_vma=False,
    )
```

```python
import functools
import math

import jax
import jax.numpy as jnp
from jax import lax
from jax.experimental import pallas as pl
from jax.experimental.pallas import tpu as pltpu
from jax.sharding import PartitionSpec as P

MODEL_WIDTH = 8192
HEAD = 128
EPSILON = 1e-05
ROPE_BASE = 500000.0
F32 = jnp.float32
BF16 = jnp.bfloat16


def iota(shape, axis):
    return lax.broadcasted_iota(jnp.int32, shape, axis)


def call(kernel, name, outs, vmem=(), hbm=(), after=(), scratch=(), flops=0, moved=0, limit=16, hbm_outs=0):
    def body(*refs):
        keep = len(vmem) + len(hbm)
        kernel(*refs[:keep], *refs[keep + len(after) :])

    return pl.pallas_call(
        body,
        out_shape=outs,
        in_specs=[pl.BlockSpec(memory_space=pltpu.VMEM)] * len(vmem)
        + [pl.BlockSpec(memory_space=pltpu.HBM)] * len(hbm)
        + [pl.BlockSpec(memory_space=pl.ANY)] * len(after),
        out_specs=[pl.BlockSpec(memory_space=pltpu.HBM)] * hbm_outs
        + [pl.BlockSpec(memory_space=pltpu.VMEM)] * (len(outs) - hbm_outs),
        scratch_shapes=scratch,
        compiler_params=pltpu.CompilerParams(vmem_limit_bytes=limit * 1024 * 1024),
        cost_estimate=pl.CostEstimate(flops=flops, bytes_accessed=moved, transcendentals=0),
        name=name,
    )(*vmem, *hbm, *after)


def shape(dims, dtype):
    return jax.ShapeDtypeStruct(dims, dtype)


def to_column(row, count):
    spread = iota((count, row.shape[1]), 0) == iota((count, row.shape[1]), 1)
    return jnp.sum(jnp.where(spread, row, 0.0), axis=1, keepdims=True)


def places(req, table, n_wide, per_dev):
    rows = req.shape[1]
    me = lax.axis_index("wide").astype(jnp.int32)
    stored = jnp.zeros_like(req)
    for a in range(table.shape[0]):
        stored = jnp.where(req == a, table[a], stored)
    owner = lax.div(stored, per_dev)
    slot = stored - owner * per_dev
    pad = -(-n_wide // 16) * 16
    hit = owner == (iota((pad, rows), 0) ^ me)
    earlier = (iota((rows, rows), 0) <= iota((rows, rows), 1)).astype(BF16)
    count = jnp.dot(hit.astype(BF16), earlier, preferred_element_type=F32)
    return jnp.where(hit, count.astype(jnp.int32) - 1, -1), slot


def dispatch_kernel(order, n_wide, per_dev, cap, req_hbm, table_hbm, tok_hbm, gain_hbm, *refs):
    xs = refs[: len(order)]
    wide_gain_ref, req_ref, table_ref, tok_ref, gain_ref, x_ref, sems, out_sems = refs[
        len(order) :
    ]
    rows, depth = tok_ref.shape
    height = x_ref.shape[1]
    loads = [
        pltpu.make_async_copy(req_hbm, req_ref, sems.at[0]),
        pltpu.make_async_copy(table_hbm, table_ref, sems.at[1]),
        pltpu.make_async_copy(tok_hbm, tok_ref, sems.at[2]),
        pltpu.make_async_copy(gain_hbm, gain_ref, sems.at[3]),
    ]
    for copy in loads:
        copy.start()
    loads[0].wait()
    loads[1].wait()
    place, slot = places(req_ref[...], table_ref, n_wide, per_dev)
    slots = jnp.broadcast_to(slot.astype(F32), (16, rows)).astype(BF16)
    picks, slot_rows = [], []
    for k in order:
        pick = (iota((HEAD, rows), 0) == place[k : k + 1]).astype(BF16)
        slot_rows.append(
            lax.dot_general(slots, pick, (((1,), (1,)), ((), ())), preferred_element_type=F32)
        )
        picks.append(pick[:height])
    loads[3].wait()
    wide_gain_ref[...] = gain_ref[...].astype(F32)
    loads[2].wait()
    stores = []
    for j, k in enumerate(order):
        y = jnp.dot(picks[j], tok_ref[...], preferred_element_type=F32)
        first = jnp.where(iota((height, HEAD), 0) == cap, slot_rows[j][:1], y[:, :HEAD])
        x_ref[j, :, :HEAD] = first.astype(BF16)
        x_ref[j, :, HEAD:] = y[:, HEAD:].astype(BF16)
        copy = pltpu.make_async_copy(x_ref.at[j], xs[j], out_sems.at[j])
        copy.start()
        stores.append(copy)
    for copy in stores:
        copy.wait()


def base_kernel(offsets, cols, gain_hbm, tok_hbm, weight_hbm, *refs):
    count = len(offsets)
    outs = refs[:count]
    gain_ref, tok_ref, buf, acc_ref, sems = refs[count:]
    steps, chunk, _ = buf.shape
    copies = [
        pltpu.make_async_copy(weight_hbm.at[pl.ds(i * chunk, chunk)], buf.at[i], sems.at[2 + i])
        for i in range(steps)
    ]
    loads = [
        pltpu.make_async_copy(gain_hbm, gain_ref, sems.at[0]),
        pltpu.make_async_copy(tok_hbm, tok_ref, sems.at[1]),
    ]
    for copy in loads + copies:
        copy.start()
    for copy in loads:
        copy.wait()
    spot = lax.axis_index("tensor").astype(jnp.int32)
    for i in range(steps):
        pieces = []
        for b in range(i * chunk // HEAD, (i + 1) * chunk // HEAD):
            piece = tok_ref[:, b * HEAD : (b + 1) * HEAD].astype(F32) * gain_ref[b : b + 1]
            pieces.append(piece.astype(BF16))
        x = jnp.concatenate(pieces, axis=1)
        copies[i].wait()
        for j, k in enumerate(offsets):
            start = pl.multiple_of((spot ^ k) * cols, HEAD)
            y = jnp.dot(x, buf[i, :, pl.ds(start, cols)], preferred_element_type=F32)
            if i > 0:
                y = y + acc_ref[j]
            if i < steps - 1:
                acc_ref[j] = y
            else:
                outs[j][...] = y.astype(outs[j].dtype)


def pair_kernel(count, start, near_ref, *refs):
    refs[-1][...] = near_ref[...]
    for j in range(count):
        out_ref = refs[2 * count + j]
        rows = slice(start, start + out_ref.shape[0])
        out_ref[...] = (refs[j][rows] + refs[count + j][rows].astype(F32)).astype(BF16)


def pair_low_kernel(count, low_ref, other_ref, *refs):
    outs = refs[2 * count :]
    cols = refs[0].shape[1]
    half = refs[0].shape[0] // 2
    for j in range(count):
        total = (refs[j][:half] + refs[count + j][:half].astype(F32)).astype(BF16)
        for h in range(cols // HEAD):
            outs[j][h * half : (h + 1) * half] = total[:, h * HEAD : (h + 1) * HEAD]
    base = cols // HEAD * half
    groups, height, _ = low_ref.shape
    for i in range(groups):
        total = low_ref[i].astype(F32) + other_ref[i].astype(F32)
        outs[0][base + i * height : base + (i + 1) * height] = total.astype(BF16)


def scaled_down_kernel(gain_ref, down_hbm, out_ref, buf, sems):
    per_dev, depth, rank = down_hbm.shape
    copies = [pltpu.make_async_copy(down_hbm.at[a], buf.at[a], sems.at[a]) for a in range(per_dev)]
    for copy in copies:
        copy.start()
    columns = []
    for b in range(depth // HEAD):
        columns.append(to_column(gain_ref[b : b + 1], HEAD))
    for a in range(per_dev):
        copies[a].wait()
        for b in range(depth // HEAD):
            span = slice(b * HEAD, (b + 1) * HEAD)
            out_ref[span, a * rank : (a + 1) * rank] = (
                buf[a, span].astype(F32) * columns[b]
            ).astype(BF16)


def aux_kernel(n_wide, per_dev, req_hbm, table_hbm, tok_hbm, sq_ref, *refs):
    sels = refs[:n_wide]
    req_ref, table_ref, tok_ref, sems = refs[n_wide:]
    copies = [
        pltpu.make_async_copy(req_hbm, req_ref, sems.at[0]),
        pltpu.make_async_copy(table_hbm, table_ref, sems.at[1]),
        pltpu.make_async_copy(tok_hbm, tok_ref, sems.at[2]),
    ]
    for copy in copies:
        copy.start()
    for copy in copies:
        copy.wait()
    rows = tok_ref.shape[0]
    place, _ = places(req_ref[...], table_ref, n_wide, per_dev)
    place = place.astype(F32)
    for k in range(n_wide):
        column = to_column(place[k : k + 1], rows).astype(jnp.int32)
        sels[k][...] = (iota((rows, HEAD), 1) == column).astype(BF16)
    tok = tok_ref[...]
    gram = lax.dot_general(tok, tok, (((1,), (1,)), ((), ())), preferred_element_type=F32)
    diag = iota((rows, rows), 0) == iota((rows, rows), 1)
    sq = jnp.sum(jnp.where(diag, gram, 0.0), axis=0, keepdims=True)
    block = jnp.zeros((8, HEAD), F32)
    for p in range(3):
        part = sq.astype(BF16).astype(F32)
        sq = sq - part
        for i in range(rows // HEAD):
            term = part[:, i * HEAD : (i + 1) * HEAD]
            block = jnp.where(iota((8, HEAD), 0) == p * (rows // HEAD) + i, term, block)
    sq_ref[...] = block


def slot_column(x_ref, cap):
    height = x_ref.shape[0]
    base = cap // 16 * 16
    row = x_ref[base : base + 16, :HEAD].astype(F32)[cap - base : cap - base + 1]
    column = to_column(row, height)
    return jnp.where(iota((height, 1), 0) < cap, column, -1.0)


def down_kernel(count, cap, with_sq, *refs):
    xs, down_ref = refs[:count], refs[count]
    sq_ref = refs[count + 1] if with_sq else None
    out_ref = refs[-1]
    height, depth = xs[0].shape
    rank = HEAD
    x = jnp.concatenate([x[...] for x in xs], axis=0) if count > 1 else xs[0][...]
    slot = [slot_column(x, cap) for x in xs]
    slot = jnp.concatenate(slot, axis=0) if count > 1 else slot[0]
    low = jnp.zeros((count * height, rank), F32)
    for g in range(down_ref.shape[1] // (2 * rank)):
        y = jnp.dot(
            x, down_ref[:, 2 * g * rank : 2 * (g + 1) * rank], preferred_element_type=F32
        )
        low = jnp.where(slot == 2 * g, y[:, :rank], low)
        low = jnp.where(slot == 2 * g + 1, y[:, rank:], low)
    for j in range(count):
        part = low[j * height : (j + 1) * height]
        if j == 0 and with_sq:
            tail = [jnp.zeros((cap, rank), F32), sq_ref[...]]
            if height > cap + 8:
                tail.append(jnp.zeros((height - cap - 8, rank), F32))
            part = part + jnp.concatenate(tail, axis=0)
        out_ref[j] = part.astype(BF16)


def low_term(ref, i, groups, height):
    if len(ref.shape) == 3:
        return ref[i].astype(F32)
    start = ref.shape[0] - (groups - i) * height
    return ref[start : start + height].astype(F32)


def low_sum_kernel(left_ref, right_ref, out_ref):
    groups, height, _ = out_ref.shape
    for i in range(groups):
        left = low_term(left_ref, i, groups, height)
        out_ref[i] = (left + low_term(right_ref, i, groups, height)).astype(BF16)


def head_is_key(heads, h):
    if heads % 2 == 0:
        return h % 2 == 0
    return (lax.axis_index("tensor").astype(jnp.int32) * heads + h) % 2 == 0


def up_kernel(count, n_parts, cap, with_sq, *refs):
    xs = refs[:count]
    parts = refs[count : count + n_parts]
    up_ref = refs[count + n_parts]
    outs = refs[count + n_parts + 1 :]
    per_dev, half, cols = up_ref.shape
    heads = cols // HEAD
    height, rank = outs[0].shape[0], 2 * half
    up = up_ref[...].reshape(per_dev * half, cols)
    sums = []
    for j in range(count):
        terms = [low_term(part, j, count, height) for part in parts]
        sums.append(sum(terms[1:], terms[0]))
    if with_sq:
        outs[count][...] = sums[0][cap : cap + 8]
    low = jnp.concatenate(sums, axis=0) if count > 1 else sums[0]
    slot = [slot_column(x, cap) for x in xs]
    slot = jnp.concatenate(slot, axis=0) if count > 1 else slot[0]
    left = iota((count * height, rank), 1) < half
    turned = pltpu.roll(low, half, 1)
    wide = []
    for source in (jnp.where(left, low, turned), jnp.where(left, turned, low)):
        pieces = []
        for g in range(per_dev // 2):
            mine = slot == jnp.where(left, 2.0 * g, 2.0 * g + 1)
            pieces.append(jnp.where(mine, source, 0.0).astype(BF16))
        wide.append(jnp.concatenate(pieces, axis=1))
    for h in range(heads):
        key = head_is_key(heads, h)
        if isinstance(key, bool):
            lhs = wide[0] if key else wide[1]
        else:
            lhs = jnp.where(key, wide[0].astype(F32), wide[1].astype(F32)).astype(BF16)
        span = slice(h * HEAD, (h + 1) * HEAD)
        y = jnp.dot(lhs, up[:, span], preferred_element_type=F32).astype(BF16)
        for j in range(count):
            outs[j][:, span] = y[j * height : (j + 1) * height]


def placed(sels, deltas):
    height, cols = deltas[0].shape
    blocks = []
    for delta in deltas:
        blocks.append(delta[...])
        if height < HEAD:
            blocks.append(jnp.zeros((HEAD - height, cols), BF16))
    lhs = jnp.concatenate([sel[...] for sel in sels], axis=1) if len(sels) > 1 else sels[0][...]
    return jnp.dot(lhs, jnp.concatenate(blocks, axis=0), preferred_element_type=F32)


def gather_kernel(n_pairs, count, sq_ref, base_ref, *refs):
    tops, bottoms = refs[:n_pairs], refs[n_pairs : 2 * n_pairs]
    deltas = refs[2 * n_pairs : 2 * n_pairs + count]
    sels = refs[2 * n_pairs + count : 2 * n_pairs + 2 * count]
    out_ref, scale_ref = refs[-2:]
    rows, cols = out_ref.shape
    pieces = rows // HEAD
    squares = []
    for i in range(pieces):
        total = sq_ref[i : i + 1]
        for p in range(1, 3):
            total = total + sq_ref[p * pieces + i : p * pieces + i + 1]
        squares.append(total)
    square = to_column(jnp.concatenate(squares, axis=1), rows)
    scale = lax.rsqrt(square * (1.0 / MODEL_WIDTH) + EPSILON)
    scale_ref[...] = jnp.broadcast_to(scale, (rows, HEAD))
    total = base_ref[...] + placed(sels, deltas)
    half = rows // 2
    lower = total[half:]
    for bottom in bottoms:
        lower = lower + bottom[...].astype(F32)
    out_ref[half:] = lower
    for h in range(cols // HEAD):
        span = slice(h * HEAD, (h + 1) * HEAD)
        upper = total[:half, span]
        for top in tops:
            upper = upper + top[h * half : (h + 1) * half].astype(F32)
        out_ref[:half, span] = upper


def finish_kernel(count, sum_ref, near_ref, scale_ref, cos_ref, sin_ref, *refs):
    deltas, sels, out_ref = refs[:count], refs[count : 2 * count], refs[2 * count]
    rows, cols = out_ref.shape
    total = sum_ref[...] + near_ref[...].astype(F32) + placed(sels, deltas)
    heads = cols // HEAD
    scale = scale_ref[...]
    for h in range(heads):
        span = slice(h * HEAD, (h + 1) * HEAD)
        x = total[:, span] * scale
        key = head_is_key(heads, h)
        if key is False:
            out_ref[:, span] = x.astype(BF16)
            continue
        y = x * cos_ref[...] + pltpu.roll(x, HEAD // 2, 1) * sin_ref[...]
        if key is not True:
            y = jnp.where(key, y, x)
        out_ref[:, span] = y.astype(BF16)


def local(
    mesh_shape,
    tokens,
    attention_norm_gain,
    key_value_weight,
    adapter_down_weight,
    adapter_up_weight,
    request_adapter,
    adapter_storage_row,
    cached_token_length,
):
    n_wide, n_tensor = mesh_shape["wide"], mesh_shape["tensor"]
    rows, depth = tokens.shape
    per_dev, _, rank = adapter_down_weight.shape
    cols = adapter_up_weight.shape[2]
    cap = 104 if n_wide <= 4 else 64
    height = -(-(cap + 8) // 16) * 16
    req = request_adapter.reshape(1, rows)
    gain = attention_norm_gain.reshape(depth // HEAD, HEAD)

    def over(axis, array, k):
        size = mesh_shape[axis]
        return lax.ppermute(array, axis, [(i, i ^ k) for i in range(size)])

    small = [pltpu.VMEM((1, rows), jnp.int32), pltpu.SMEM(adapter_storage_row.shape, jnp.int32)]
    first, last = [0, 1], list(range(2, n_wide))

    def dispatch(order, after):
        *blocks, wide_gain = call(
            functools.partial(dispatch_kernel, order, n_wide, per_dev, cap),
            "dispatch",
            [shape((height, depth), BF16)] * len(order) + [shape(gain.shape, F32)],
            hbm=(req, adapter_storage_row, tokens, gain),
            hbm_outs=len(order),
            after=after,
            scratch=small
            + [
                pltpu.VMEM((rows, depth), BF16),
                pltpu.VMEM(gain.shape, BF16),
                pltpu.VMEM((len(order), height, depth), BF16),
                pltpu.SemaphoreType.DMA((4,)),
                pltpu.SemaphoreType.DMA((len(order),)),
            ],
            flops=2 * len(order) * height * rows * depth,
            moved=2 * rows * depth * 4,
            limit=63,
        )
        return blocks, wide_gain

    order = list(range(n_wide - 1, -1, -1))
    blocks, wide_gain = dispatch(order, ())
    held = [blocks[n_wide - 1 - k] for k in range(n_wide)]
    held[1:] = [over("wide", held[k], k) for k in range(1, n_wide)]

    twos = list(range(2, n_tensor, 2))
    far = [k ^ 1 for k in twos]
    offsets = far + [1] + twos + [0]
    chunk = math.gcd(depth, 512)
    steps = depth // chunk
    sums = call(
        functools.partial(base_kernel, offsets, cols),
        "base",
        [shape((rows, cols), BF16)] * (len(far) + 1) + [shape((rows, cols), F32)] * (len(twos) + 1),
        hbm=(wide_gain, tokens, key_value_weight),
        scratch=[
            pltpu.VMEM(gain.shape, F32),
            pltpu.VMEM((rows, depth), BF16),
            pltpu.VMEM((steps, chunk, key_value_weight.shape[1]), BF16),
            pltpu.VMEM((len(offsets), rows, cols), F32),
            pltpu.SemaphoreType.DMA((2 + steps,)),
        ],
        flops=2 * rows * depth * cols * n_tensor,
        moved=2 * depth * cols * n_tensor,
        limit=52,
    )
    away, near, own, base = sums[: len(far)], sums[len(far)], sums[len(far) + 1 : -1], sums[-1]
    beside = [over("tensor", p, 1) for p in away]
    (down,) = call(
        scaled_down_kernel,
        "scaled_down",
        [shape((depth, per_dev * rank), BF16)],
        vmem=(wide_gain,),
        hbm=(adapter_down_weight,),
        after=(base,),
        scratch=[
            pltpu.VMEM((per_dev, depth, rank), BF16),
            pltpu.SemaphoreType.DMA((per_dev,)),
        ],
        flops=4 * depth * per_dev * rank,
        moved=4 * depth * per_dev * rank,
    )
    half_size = HEAD // 2
    freq_index = jnp.arange(half_size).astype(F32)
    inverse = jnp.exp(freq_index * (-2.0 / HEAD) * math.log(ROPE_BASE))
    angles = cached_token_length.astype(F32)[:, None] * inverse[None, :]
    cosine, sine = jnp.cos(angles), jnp.sin(angles)
    cosine = jnp.concatenate([cosine, cosine], axis=1)
    sine = jnp.concatenate([-sine, sine], axis=1)

    def down_block(group, extra, after):
        xs = [held[k] for k in group]
        (low,) = call(
            functools.partial(down_kernel, len(xs), cap, bool(extra)),
            "down_block",
            [shape((len(xs), height, rank), BF16)],
            vmem=(*xs, down, *extra),
            after=after,
            flops=2 * len(xs) * height * depth * rank * per_dev,
            moved=2 * per_dev * depth * rank,
        )
        return low

    def up_block(group, parts, with_sq, after):
        xs = [held[k] for k in group]
        outs = [shape((height, cols), BF16)] * len(xs)
        if with_sq:
            outs = outs + [shape((8, HEAD), F32)]
        return call(
            functools.partial(up_kernel, len(xs), len(parts), cap, with_sq),
            "up_block",
            outs,
            vmem=(*xs, *parts, adapter_up_weight),
            after=after,
            flops=2 * len(xs) * height * per_dev * rank * cols,
            moved=2 * per_dev * rank * cols,
        )

    low = down_block(first, (), ())
    sq, *sels = call(
        functools.partial(aux_kernel, n_wide, per_dev),
        "aux",
        [shape((8, HEAD), F32)]
        + [shape((rows, HEAD), BF16)] * n_wide,
        hbm=(req, adapter_storage_row, tokens),
        after=(low,),
        scratch=small + [pltpu.VMEM((rows, depth), BF16), pltpu.SemaphoreType.DMA((3,))],
        flops=2 * rows * rows * depth,
        moved=2 * rows * depth,
    )
    half = rows // 2
    upper = cols // HEAD * half
    other = over("tensor", low, 1)
    pairs = call(
        functools.partial(pair_low_kernel, len(twos)),
        "pair_low_sums",
        [shape((upper + len(first) * height, HEAD), BF16)]
        + [shape((upper, HEAD), BF16)] * (len(twos) - 1),
        vmem=(low, other, *own, *beside),
        after=(sq,),
    )
    tops = [over("tensor", p, k) for p, k in zip(pairs, twos)]
    done = pairs[0]
    low, other = pairs[0], tops[0]
    for step in range(2, n_tensor.bit_length() - 1):
        (low,) = call(
            low_sum_kernel,
            "low_sum",
            [shape((len(first), height, rank), BF16)],
            vmem=(low, other),
        )
        other = over("tensor", low, 2**step)
    low_last = down_block(last, (sq,), (done,))
    last_parts = [low_last] + [over("tensor", low_last, k) for k in range(n_tensor - 1, 0, -1)]
    ups = up_block(first, [low, other], False, (low_last,))
    deltas = [u if k == 0 else over("wide", u, k) for k, u in zip(first, ups)]
    *pairs, near = call(
        functools.partial(pair_kernel, len(twos), half),
        "pair_sums",
        [shape((half, cols), BF16)] * len(twos) + [shape((rows, cols), BF16)],
        vmem=(near, *own, *beside),
        after=(ups[0],),
    )
    near = over("tensor", near, 1)
    bottoms = [over("tensor", p, k) for p, k in zip(pairs, twos)]
    *ups, square = up_block(last, last_parts, True, (pairs[0],))
    last_deltas = [over("wide", u, k) for k, u in zip(last, ups)]
    total, scale = call(
        functools.partial(gather_kernel, len(bottoms), len(first)),
        "gather",
        [shape((rows, cols), F32), shape((rows, HEAD), F32)],
        vmem=(square, base, *tops, *bottoms, *deltas, *[sels[k] for k in first]),
        after=(ups[0],),
        flops=2 * rows * cols * HEAD * len(first),
    )
    return call(
        functools.partial(finish_kernel, len(last)),
        "finish",
        [shape((rows, cols), BF16)],
        vmem=(total, near, scale, cosine, sine, *last_deltas, *[sels[k] for k in last]),
        flops=2 * rows * cols * HEAD,
    )[0]


def solution(mesh):
    return jax.shard_map(
        functools.partial(local, dict(mesh.shape)),
        mesh=mesh,
        in_specs=(
            P(("parts", "wide"), "tensor"),
            P("tensor"),
            P("tensor", None),
            P(("parts", "wide"), "tensor", None),
            P(("parts", "wide"), None, "tensor"),
            P(("parts", "wide")),
            P("parts"),
            P(("parts", "wide")),
        ),
        out_specs=P(("parts", "wide"), "tensor"),
        check_vma=False,
    )
```

```python
import functools
import math

import jax
import jax.numpy as jnp
from jax import lax
from jax.experimental import pallas as pl
from jax.experimental.pallas import tpu as pltpu
from jax.sharding import PartitionSpec as P

MODEL_WIDTH = 8192
HEAD = 128
EPSILON = 1e-05
ROPE_BASE = 500000.0
F32 = jnp.float32
BF16 = jnp.bfloat16


def iota(shape, axis):
    return lax.broadcasted_iota(jnp.int32, shape, axis)


def call(kernel, name, outs, vmem=(), hbm=(), after=(), scratch=(), flops=0, moved=0, limit=16, hbm_outs=0):
    def body(*refs):
        keep = len(vmem) + len(hbm)
        kernel(*refs[:keep], *refs[keep + len(after) :])

    return pl.pallas_call(
        body,
        out_shape=outs,
        in_specs=[pl.BlockSpec(memory_space=pltpu.VMEM)] * len(vmem)
        + [pl.BlockSpec(memory_space=pltpu.HBM)] * len(hbm)
        + [pl.BlockSpec(memory_space=pl.ANY)] * len(after),
        out_specs=[pl.BlockSpec(memory_space=pltpu.HBM)] * hbm_outs
        + [pl.BlockSpec(memory_space=pltpu.VMEM)] * (len(outs) - hbm_outs),
        scratch_shapes=scratch,
        compiler_params=pltpu.CompilerParams(vmem_limit_bytes=limit * 1024 * 1024),
        cost_estimate=pl.CostEstimate(flops=flops, bytes_accessed=moved, transcendentals=0),
        name=name,
    )(*vmem, *hbm, *after)


def shape(dims, dtype):
    return jax.ShapeDtypeStruct(dims, dtype)


def to_column(row, count):
    spread = iota((count, row.shape[1]), 0) == iota((count, row.shape[1]), 1)
    return jnp.sum(jnp.where(spread, row, 0.0), axis=1, keepdims=True)


def places(req, table, n_wide, per_dev):
    rows = req.shape[1]
    me = lax.axis_index("wide").astype(jnp.int32)
    stored = jnp.zeros_like(req)
    for a in range(table.shape[0]):
        stored = jnp.where(req == a, table[a], stored)
    owner = lax.div(stored, per_dev)
    slot = stored - owner * per_dev
    pad = -(-n_wide // 16) * 16
    hit = owner == (iota((pad, rows), 0) ^ me)
    earlier = (iota((rows, rows), 0) <= iota((rows, rows), 1)).astype(BF16)
    count = jnp.dot(hit.astype(BF16), earlier, preferred_element_type=F32)
    return jnp.where(hit, count.astype(jnp.int32) - 1, -1), slot


def dispatch_kernel(order, n_wide, per_dev, cap, req_hbm, table_hbm, tok_hbm, gain_hbm, *refs):
    xs = refs[: len(order)]
    xg_hbm, req_ref, table_ref, tok_ref, gain_ref, x_ref, xg_ref, sems, out_sems = refs[
        len(order) :
    ]
    rows, depth = tok_ref.shape
    height = x_ref.shape[1]
    loads = [
        pltpu.make_async_copy(req_hbm, req_ref, sems.at[0]),
        pltpu.make_async_copy(table_hbm, table_ref, sems.at[1]),
        pltpu.make_async_copy(tok_hbm, tok_ref, sems.at[2]),
        pltpu.make_async_copy(gain_hbm, gain_ref, sems.at[3]),
    ]
    for copy in loads:
        copy.start()
    loads[0].wait()
    loads[1].wait()
    place, slot = places(req_ref[...], table_ref, n_wide, per_dev)
    slots = jnp.broadcast_to(slot.astype(F32), (16, rows)).astype(BF16)
    picks, slot_rows = [], []
    for k in order:
        pick = (iota((HEAD, rows), 0) == place[k : k + 1]).astype(BF16)
        slot_rows.append(
            lax.dot_general(slots, pick, (((1,), (1,)), ((), ())), preferred_element_type=F32)
        )
        picks.append(pick[:height])
    loads[3].wait()
    loads[2].wait()
    stores = []
    for j, k in enumerate(order):
        if k == 1:
            for b in range(depth // HEAD):
                span = slice(b * HEAD, (b + 1) * HEAD)
                piece = tok_ref[:, span].astype(F32) * gain_ref[b : b + 1].astype(F32)
                xg_ref[:, span] = piece.astype(BF16)
            copy = pltpu.make_async_copy(xg_ref, xg_hbm, out_sems.at[len(order)])
            copy.start()
            stores.append(copy)
        y = jnp.dot(picks[j], tok_ref[...], preferred_element_type=F32)
        first = jnp.where(iota((height, HEAD), 0) == cap, slot_rows[j][:1], y[:, :HEAD])
        x_ref[j, :, :HEAD] = first.astype(BF16)
        x_ref[j, :, HEAD:] = y[:, HEAD:].astype(BF16)
        copy = pltpu.make_async_copy(x_ref.at[j], xs[j], out_sems.at[j])
        copy.start()
        stores.append(copy)
    for copy in stores:
        copy.wait()


def base_kernel(offsets, cols, xg_hbm, weight_hbm, *refs):
    count = len(offsets)
    outs = refs[:count]
    x_ref, buf, acc_ref, sems = refs[count:]
    steps, chunk, _ = buf.shape
    load = pltpu.make_async_copy(xg_hbm, x_ref, sems.at[0])
    copies = [
        pltpu.make_async_copy(weight_hbm.at[pl.ds(i * chunk, chunk)], buf.at[i], sems.at[1 + i])
        for i in range(steps)
    ]
    for copy in [load] + copies:
        copy.start()
    load.wait()
    spot = lax.axis_index("tensor").astype(jnp.int32)
    for i in range(steps):
        x = x_ref[:, i * chunk : (i + 1) * chunk]
        copies[i].wait()
        for j, k in enumerate(offsets):
            start = pl.multiple_of((spot ^ k) * cols, HEAD)
            y = jnp.dot(x, buf[i, :, pl.ds(start, cols)], preferred_element_type=F32)
            if i > 0:
                y = y + acc_ref[j]
            if i < steps - 1:
                acc_ref[j] = y
            else:
                outs[j][...] = y.astype(outs[j].dtype)


def pair_kernel(count, start, near_ref, *refs):
    refs[-1][...] = near_ref[...]
    for j in range(count):
        out_ref = refs[2 * count + j]
        rows = slice(start, start + out_ref.shape[0])
        out_ref[...] = (refs[j][rows] + refs[count + j][rows].astype(F32)).astype(BF16)


def pair_low_kernel(count, low_ref, other_ref, *refs):
    outs = refs[2 * count :]
    cols = refs[0].shape[1]
    half = refs[0].shape[0] // 2
    for j in range(count):
        total = (refs[j][:half] + refs[count + j][:half].astype(F32)).astype(BF16)
        for h in range(cols // HEAD):
            outs[j][h * half : (h + 1) * half] = total[:, h * HEAD : (h + 1) * HEAD]
    base = cols // HEAD * half
    groups, height, _ = low_ref.shape
    for i in range(groups):
        total = low_ref[i].astype(F32) + other_ref[i].astype(F32)
        outs[0][base + i * height : base + (i + 1) * height] = total.astype(BF16)


def scaled_down_kernel(gain_ref, down_hbm, out_ref, buf, sems):
    per_dev, depth, rank = down_hbm.shape
    copies = [pltpu.make_async_copy(down_hbm.at[a], buf.at[a], sems.at[a]) for a in range(per_dev)]
    for copy in copies:
        copy.start()
    columns = []
    for b in range(depth // HEAD):
        columns.append(to_column(gain_ref[b : b + 1].astype(F32), HEAD))
    for a in range(per_dev):
        copies[a].wait()
        for b in range(depth // HEAD):
            span = slice(b * HEAD, (b + 1) * HEAD)
            out_ref[span, a * rank : (a + 1) * rank] = (
                buf[a, span].astype(F32) * columns[b]
            ).astype(BF16)


def aux_kernel(n_wide, per_dev, req_hbm, table_hbm, tok_hbm, sq_ref, *refs):
    sels = refs[:n_wide]
    req_ref, table_ref, tok_ref, sems = refs[n_wide:]
    copies = [
        pltpu.make_async_copy(req_hbm, req_ref, sems.at[0]),
        pltpu.make_async_copy(table_hbm, table_ref, sems.at[1]),
        pltpu.make_async_copy(tok_hbm, tok_ref, sems.at[2]),
    ]
    for copy in copies:
        copy.start()
    for copy in copies:
        copy.wait()
    rows = tok_ref.shape[0]
    place, _ = places(req_ref[...], table_ref, n_wide, per_dev)
    place = place.astype(F32)
    for k in range(n_wide):
        column = to_column(place[k : k + 1], rows).astype(jnp.int32)
        sels[k][...] = (iota((rows, HEAD), 1) == column).astype(BF16)
    tok = tok_ref[...]
    gram = lax.dot_general(tok, tok, (((1,), (1,)), ((), ())), preferred_element_type=F32)
    diag = iota((rows, rows), 0) == iota((rows, rows), 1)
    sq = jnp.sum(jnp.where(diag, gram, 0.0), axis=0, keepdims=True)
    block = jnp.zeros((8, HEAD), F32)
    for p in range(3):
        part = sq.astype(BF16).astype(F32)
        sq = sq - part
        for i in range(rows // HEAD):
            term = part[:, i * HEAD : (i + 1) * HEAD]
            block = jnp.where(iota((8, HEAD), 0) == p * (rows // HEAD) + i, term, block)
    sq_ref[...] = block


def slot_column(x_ref, cap):
    height = x_ref.shape[0]
    base = cap // 16 * 16
    row = x_ref[base : base + 16, :HEAD].astype(F32)[cap - base : cap - base + 1]
    column = to_column(row, height)
    return jnp.where(iota((height, 1), 0) < cap, column, -1.0)


def down_kernel(count, cap, with_sq, *refs):
    xs, down_ref = refs[:count], refs[count]
    sq_ref = refs[count + 1] if with_sq else None
    out_ref = refs[-1]
    height, depth = xs[0].shape
    rank = HEAD
    x = jnp.concatenate([x[...] for x in xs], axis=0) if count > 1 else xs[0][...]
    slot = [slot_column(x, cap) for x in xs]
    slot = jnp.concatenate(slot, axis=0) if count > 1 else slot[0]
    low = jnp.zeros((count * height, rank), F32)
    for g in range(down_ref.shape[1] // (2 * rank)):
        y = jnp.dot(
            x, down_ref[:, 2 * g * rank : 2 * (g + 1) * rank], preferred_element_type=F32
        )
        low = jnp.where(slot == 2 * g, y[:, :rank], low)
        low = jnp.where(slot == 2 * g + 1, y[:, rank:], low)
    for j in range(count):
        part = low[j * height : (j + 1) * height]
        if j == 0 and with_sq:
            tail = [jnp.zeros((cap, rank), F32), sq_ref[...]]
            if height > cap + 8:
                tail.append(jnp.zeros((height - cap - 8, rank), F32))
            part = part + jnp.concatenate(tail, axis=0)
        out_ref[j] = part.astype(BF16)


def low_term(ref, i, groups, height):
    if len(ref.shape) == 3:
        return ref[i].astype(F32)
    start = ref.shape[0] - (groups - i) * height
    return ref[start : start + height].astype(F32)


def low_sum_kernel(left_ref, right_ref, out_ref):
    groups, height, _ = out_ref.shape
    for i in range(groups):
        left = low_term(left_ref, i, groups, height)
        out_ref[i] = (left + low_term(right_ref, i, groups, height)).astype(BF16)


def head_is_key(heads, h):
    if heads % 2 == 0:
        return h % 2 == 0
    return (lax.axis_index("tensor").astype(jnp.int32) * heads + h) % 2 == 0


def up_kernel(count, n_parts, cap, with_sq, *refs):
    xs = refs[:count]
    parts = refs[count : count + n_parts]
    up_ref = refs[count + n_parts]
    outs = refs[count + n_parts + 1 :]
    per_dev, half, cols = up_ref.shape
    heads = cols // HEAD
    height, rank = outs[0].shape[0], 2 * half
    up = up_ref[...].reshape(per_dev * half, cols)
    sums = []
    for j in range(count):
        terms = [low_term(part, j, count, height) for part in parts]
        sums.append(sum(terms[1:], terms[0]))
    if with_sq:
        outs[count][...] = sums[0][cap : cap + 8]
    low = jnp.concatenate(sums, axis=0) if count > 1 else sums[0]
    slot = [slot_column(x, cap) for x in xs]
    slot = jnp.concatenate(slot, axis=0) if count > 1 else slot[0]
    left = iota((count * height, rank), 1) < half
    turned = pltpu.roll(low, half, 1)
    wide = []
    for source in (jnp.where(left, low, turned), jnp.where(left, turned, low)):
        pieces = []
        for g in range(per_dev // 2):
            mine = slot == jnp.where(left, 2.0 * g, 2.0 * g + 1)
            pieces.append(jnp.where(mine, source, 0.0).astype(BF16))
        wide.append(jnp.concatenate(pieces, axis=1))
    for h in range(heads):
        key = head_is_key(heads, h)
        if isinstance(key, bool):
            lhs = wide[0] if key else wide[1]
        else:
            lhs = jnp.where(key, wide[0].astype(F32), wide[1].astype(F32)).astype(BF16)
        span = slice(h * HEAD, (h + 1) * HEAD)
        y = jnp.dot(lhs, up[:, span], preferred_element_type=F32).astype(BF16)
        for j in range(count):
            outs[j][:, span] = y[j * height : (j + 1) * height]


def placed(sels, deltas):
    height, cols = deltas[0].shape
    blocks = []
    for delta in deltas:
        blocks.append(delta[...])
        if height < HEAD:
            blocks.append(jnp.zeros((HEAD - height, cols), BF16))
    lhs = jnp.concatenate([sel[...] for sel in sels], axis=1) if len(sels) > 1 else sels[0][...]
    return jnp.dot(lhs, jnp.concatenate(blocks, axis=0), preferred_element_type=F32)


def gather_kernel(n_pairs, count, sq_ref, base_ref, *refs):
    tops, bottoms = refs[:n_pairs], refs[n_pairs : 2 * n_pairs]
    deltas = refs[2 * n_pairs : 2 * n_pairs + count]
    sels = refs[2 * n_pairs + count : 2 * n_pairs + 2 * count]
    out_ref, scale_ref = refs[-2:]
    rows, cols = out_ref.shape
    pieces = rows // HEAD
    squares = []
    for i in range(pieces):
        total = sq_ref[i : i + 1]
        for p in range(1, 3):
            total = total + sq_ref[p * pieces + i : p * pieces + i + 1]
        squares.append(total)
    square = to_column(jnp.concatenate(squares, axis=1), rows)
    scale = lax.rsqrt(square * (1.0 / MODEL_WIDTH) + EPSILON)
    scale_ref[...] = jnp.broadcast_to(scale, (rows, HEAD))
    total = base_ref[...] + placed(sels, deltas)
    half = rows // 2
    lower = total[half:]
    for bottom in bottoms:
        lower = lower + bottom[...].astype(F32)
    out_ref[half:] = lower
    for h in range(cols // HEAD):
        span = slice(h * HEAD, (h + 1) * HEAD)
        upper = total[:half, span]
        for top in tops:
            upper = upper + top[h * half : (h + 1) * half].astype(F32)
        out_ref[:half, span] = upper


def finish_kernel(count, sum_ref, near_ref, scale_ref, cos_ref, sin_ref, *refs):
    deltas, sels, out_ref = refs[:count], refs[count : 2 * count], refs[2 * count]
    rows, cols = out_ref.shape
    total = sum_ref[...] + near_ref[...].astype(F32) + placed(sels, deltas)
    heads = cols // HEAD
    scale = scale_ref[...]
    for h in range(heads):
        span = slice(h * HEAD, (h + 1) * HEAD)
        x = total[:, span] * scale
        key = head_is_key(heads, h)
        if key is False:
            out_ref[:, span] = x.astype(BF16)
            continue
        y = x * cos_ref[...] + pltpu.roll(x, HEAD // 2, 1) * sin_ref[...]
        if key is not True:
            y = jnp.where(key, y, x)
        out_ref[:, span] = y.astype(BF16)


def local(
    mesh_shape,
    tokens,
    attention_norm_gain,
    key_value_weight,
    adapter_down_weight,
    adapter_up_weight,
    request_adapter,
    adapter_storage_row,
    cached_token_length,
):
    n_wide, n_tensor = mesh_shape["wide"], mesh_shape["tensor"]
    rows, depth = tokens.shape
    per_dev, _, rank = adapter_down_weight.shape
    cols = adapter_up_weight.shape[2]
    cap = 104 if n_wide <= 4 else 64
    height = -(-(cap + 8) // 16) * 16
    req = request_adapter.reshape(1, rows)
    gain = attention_norm_gain.reshape(depth // HEAD, HEAD)

    def over(axis, array, k):
        size = mesh_shape[axis]
        return lax.ppermute(array, axis, [(i, i ^ k) for i in range(size)])

    small = [pltpu.VMEM((1, rows), jnp.int32), pltpu.SMEM(adapter_storage_row.shape, jnp.int32)]
    first, last = [0, 1], list(range(2, n_wide))

    order = list(range(n_wide - 1, -1, -1))
    *blocks, xg = call(
        functools.partial(dispatch_kernel, order, n_wide, per_dev, cap),
        "dispatch",
        [shape((height, depth), BF16)] * n_wide + [shape((rows, depth), BF16)],
        hbm=(req, adapter_storage_row, tokens, gain),
        hbm_outs=n_wide + 1,
        scratch=small
        + [
            pltpu.VMEM((rows, depth), BF16),
            pltpu.VMEM(gain.shape, BF16),
            pltpu.VMEM((n_wide, height, depth), BF16),
            pltpu.VMEM((rows, depth), BF16),
            pltpu.SemaphoreType.DMA((4,)),
            pltpu.SemaphoreType.DMA((n_wide + 1,)),
        ],
        flops=2 * n_wide * height * rows * depth,
        moved=2 * rows * depth * 4,
        limit=63,
    )
    held = [blocks[n_wide - 1 - k] for k in range(n_wide)]
    held[1:] = [over("wide", held[k], k) for k in range(1, n_wide)]

    twos = list(range(2, n_tensor, 2))
    far = [k ^ 1 for k in twos]
    offsets = far + [1] + twos + [0]
    chunk = math.gcd(depth, 512)
    steps = depth // chunk
    sums = call(
        functools.partial(base_kernel, offsets, cols),
        "base",
        [shape((rows, cols), BF16)] * (len(far) + 1) + [shape((rows, cols), F32)] * (len(twos) + 1),
        hbm=(xg, key_value_weight),
        scratch=[
            pltpu.VMEM((rows, depth), BF16),
            pltpu.VMEM((steps, chunk, key_value_weight.shape[1]), BF16),
            pltpu.VMEM((len(offsets), rows, cols), F32),
            pltpu.SemaphoreType.DMA((1 + steps,)),
        ],
        flops=2 * rows * depth * cols * n_tensor,
        moved=2 * depth * cols * n_tensor,
        limit=52,
    )
    away, near, own, base = sums[: len(far)], sums[len(far)], sums[len(far) + 1 : -1], sums[-1]
    beside = [over("tensor", p, 1) for p in away]
    (down,) = call(
        scaled_down_kernel,
        "scaled_down",
        [shape((depth, per_dev * rank), BF16)],
        vmem=(gain,),
        hbm=(adapter_down_weight,),
        after=(base,),
        scratch=[
            pltpu.VMEM((per_dev, depth, rank), BF16),
            pltpu.SemaphoreType.DMA((per_dev,)),
        ],
        flops=4 * depth * per_dev * rank,
        moved=4 * depth * per_dev * rank,
    )
    half_size = HEAD // 2
    freq_index = jnp.arange(half_size).astype(F32)
    inverse = jnp.exp(freq_index * (-2.0 / HEAD) * math.log(ROPE_BASE))
    angles = cached_token_length.astype(F32)[:, None] * inverse[None, :]
    cosine, sine = jnp.cos(angles), jnp.sin(angles)
    cosine = jnp.concatenate([cosine, cosine], axis=1)
    sine = jnp.concatenate([-sine, sine], axis=1)

    def down_block(group, extra, after):
        xs = [held[k] for k in group]
        (low,) = call(
            functools.partial(down_kernel, len(xs), cap, bool(extra)),
            "down_block",
            [shape((len(xs), height, rank), BF16)],
            vmem=(*xs, down, *extra),
            after=after,
            flops=2 * len(xs) * height * depth * rank * per_dev,
            moved=2 * per_dev * depth * rank,
        )
        return low

    def up_block(group, parts, with_sq, after):
        xs = [held[k] for k in group]
        outs = [shape((height, cols), BF16)] * len(xs)
        if with_sq:
            outs = outs + [shape((8, HEAD), F32)]
        return call(
            functools.partial(up_kernel, len(xs), len(parts), cap, with_sq),
            "up_block",
            outs,
            vmem=(*xs, *parts, adapter_up_weight),
            after=after,
            flops=2 * len(xs) * height * per_dev * rank * cols,
            moved=2 * per_dev * rank * cols,
        )

    low = down_block(first, (), ())
    sq, *sels = call(
        functools.partial(aux_kernel, n_wide, per_dev),
        "aux",
        [shape((8, HEAD), F32)]
        + [shape((rows, HEAD), BF16)] * n_wide,
        hbm=(req, adapter_storage_row, tokens),
        after=(low,),
        scratch=small + [pltpu.VMEM((rows, depth), BF16), pltpu.SemaphoreType.DMA((3,))],
        flops=2 * rows * rows * depth,
        moved=2 * rows * depth,
    )
    half = rows // 2
    upper = cols // HEAD * half
    other = over("tensor", low, 1)
    pairs = call(
        functools.partial(pair_low_kernel, len(twos)),
        "pair_low_sums",
        [shape((upper + len(first) * height, HEAD), BF16)]
        + [shape((upper, HEAD), BF16)] * (len(twos) - 1),
        vmem=(low, other, *own, *beside),
        after=(sq,),
    )
    tops = [over("tensor", p, k) for p, k in zip(pairs, twos)]
    done = pairs[0]
    low, other = pairs[0], tops[0]
    for step in range(2, n_tensor.bit_length() - 1):
        (low,) = call(
            low_sum_kernel,
            "low_sum",
            [shape((len(first), height, rank), BF16)],
            vmem=(low, other),
        )
        other = over("tensor", low, 2**step)
    low_last = down_block(last, (sq,), (done,))
    last_parts = [low_last] + [over("tensor", low_last, k) for k in range(n_tensor - 1, 0, -1)]
    ups = up_block(first, [low, other], False, (low_last,))
    deltas = [u if k == 0 else over("wide", u, k) for k, u in zip(first, ups)]
    *pairs, near = call(
        functools.partial(pair_kernel, len(twos), half),
        "pair_sums",
        [shape((half, cols), BF16)] * len(twos) + [shape((rows, cols), BF16)],
        vmem=(near, *own, *beside),
        after=(ups[0],),
    )
    near = over("tensor", near, 1)
    bottoms = [over("tensor", p, k) for p, k in zip(pairs, twos)]
    *ups, square = up_block(last, last_parts, True, (pairs[0],))
    last_deltas = [over("wide", u, k) for k, u in zip(last, ups)]
    total, scale = call(
        functools.partial(gather_kernel, len(bottoms), len(first)),
        "gather",
        [shape((rows, cols), F32), shape((rows, HEAD), F32)],
        vmem=(square, base, *tops, *bottoms, *deltas, *[sels[k] for k in first]),
        after=(ups[0],),
        flops=2 * rows * cols * HEAD * len(first),
    )
    return call(
        functools.partial(finish_kernel, len(last)),
        "finish",
        [shape((rows, cols), BF16)],
        vmem=(total, near, scale, cosine, sine, *last_deltas, *[sels[k] for k in last]),
        flops=2 * rows * cols * HEAD,
    )[0]


def solution(mesh):
    return jax.shard_map(
        functools.partial(local, dict(mesh.shape)),
        mesh=mesh,
        in_specs=(
            P(("parts", "wide"), "tensor"),
            P("tensor"),
            P("tensor", None),
            P(("parts", "wide"), "tensor", None),
            P(("parts", "wide"), None, "tensor"),
            P(("parts", "wide")),
            P("parts"),
            P(("parts", "wide")),
        ),
        out_specs=P(("parts", "wide"), "tensor"),
        check_vma=False,
    )
```

```python
import functools
import math

import jax
import jax.numpy as jnp
from jax import lax
from jax.experimental import pallas as pl
from jax.experimental.pallas import tpu as pltpu
from jax.sharding import PartitionSpec as P

MODEL_WIDTH = 8192
HEAD = 128
EPSILON = 1e-05
ROPE_BASE = 500000.0
F32 = jnp.float32
BF16 = jnp.bfloat16


def iota(shape, axis):
    return lax.broadcasted_iota(jnp.int32, shape, axis)


def call(kernel, name, outs, vmem=(), hbm=(), after=(), scratch=(), flops=0, moved=0, limit=16, hbm_outs=0):
    def body(*refs):
        keep = len(vmem) + len(hbm)
        kernel(*refs[:keep], *refs[keep + len(after) :])

    return pl.pallas_call(
        body,
        out_shape=outs,
        in_specs=[pl.BlockSpec(memory_space=pltpu.VMEM)] * len(vmem)
        + [pl.BlockSpec(memory_space=pltpu.HBM)] * len(hbm)
        + [pl.BlockSpec(memory_space=pl.ANY)] * len(after),
        out_specs=[pl.BlockSpec(memory_space=pltpu.HBM)] * hbm_outs
        + [pl.BlockSpec(memory_space=pltpu.VMEM)] * (len(outs) - hbm_outs),
        scratch_shapes=scratch,
        compiler_params=pltpu.CompilerParams(vmem_limit_bytes=limit * 1024 * 1024),
        cost_estimate=pl.CostEstimate(flops=flops, bytes_accessed=moved, transcendentals=0),
        name=name,
    )(*vmem, *hbm, *after)


def shape(dims, dtype):
    return jax.ShapeDtypeStruct(dims, dtype)


def to_column(row, count):
    spread = iota((count, row.shape[1]), 0) == iota((count, row.shape[1]), 1)
    return jnp.sum(jnp.where(spread, row, 0.0), axis=1, keepdims=True)


def places(req, table, n_wide, per_dev):
    rows = req.shape[1]
    me = lax.axis_index("wide").astype(jnp.int32)
    stored = jnp.zeros_like(req)
    for a in range(table.shape[0]):
        stored = jnp.where(req == a, table[a], stored)
    owner = lax.div(stored, per_dev)
    slot = stored - owner * per_dev
    pad = -(-n_wide // 16) * 16
    hit = owner == (iota((pad, rows), 0) ^ me)
    earlier = (iota((rows, rows), 0) <= iota((rows, rows), 1)).astype(BF16)
    count = jnp.dot(hit.astype(BF16), earlier, preferred_element_type=F32)
    return jnp.where(hit, count.astype(jnp.int32) - 1, -1), slot


def dispatch_kernel(order, n_wide, per_dev, cap, req_hbm, table_hbm, tok_hbm, gain_hbm, *refs):
    xs = refs[: len(order)]
    xg_hbm, req_ref, table_ref, tok_ref, gain_ref, x_ref, xg_ref, sems, out_sems = refs[
        len(order) :
    ]
    rows, depth = tok_ref.shape
    height = x_ref.shape[1]
    loads = [
        pltpu.make_async_copy(req_hbm, req_ref, sems.at[0]),
        pltpu.make_async_copy(table_hbm, table_ref, sems.at[1]),
        pltpu.make_async_copy(tok_hbm, tok_ref, sems.at[2]),
        pltpu.make_async_copy(gain_hbm, gain_ref, sems.at[3]),
    ]
    for copy in loads:
        copy.start()
    loads[0].wait()
    loads[1].wait()
    place, slot = places(req_ref[...], table_ref, n_wide, per_dev)
    slots = jnp.broadcast_to(slot.astype(F32), (16, rows)).astype(BF16)
    picks, slot_rows = [], []
    for k in order:
        pick = (iota((HEAD, rows), 0) == place[k : k + 1]).astype(BF16)
        slot_rows.append(
            lax.dot_general(slots, pick, (((1,), (1,)), ((), ())), preferred_element_type=F32)
        )
        picks.append(pick[:height])
    loads[3].wait()
    loads[2].wait()
    stores = []
    for j, k in enumerate(order):
        if k == 1:
            for b in range(depth // HEAD):
                span = slice(b * HEAD, (b + 1) * HEAD)
                piece = tok_ref[:, span].astype(F32) * gain_ref[b : b + 1].astype(F32)
                xg_ref[:, span] = piece.astype(BF16)
            copy = pltpu.make_async_copy(xg_ref, xg_hbm, out_sems.at[len(order)])
            copy.start()
            stores.append(copy)
        y = jnp.dot(picks[j], tok_ref[...], preferred_element_type=F32)
        first = jnp.where(iota((height, HEAD), 0) == cap, slot_rows[j][:1], y[:, :HEAD])
        x_ref[j, :, :HEAD] = first.astype(BF16)
        x_ref[j, :, HEAD:] = y[:, HEAD:].astype(BF16)
        copy = pltpu.make_async_copy(x_ref.at[j], xs[j], out_sems.at[j])
        copy.start()
        stores.append(copy)
    for copy in stores:
        copy.wait()


def base_kernel(offsets, cols, xg_hbm, weight_hbm, *refs):
    count = len(offsets)
    outs = refs[:count]
    x_ref, buf, acc_ref, sems = refs[count:]
    steps, chunk, _ = buf.shape
    load = pltpu.make_async_copy(xg_hbm, x_ref, sems.at[0])
    copies = [
        pltpu.make_async_copy(weight_hbm.at[pl.ds(i * chunk, chunk)], buf.at[i], sems.at[1 + i])
        for i in range(steps)
    ]
    for copy in [load] + copies:
        copy.start()
    load.wait()
    spot = lax.axis_index("tensor").astype(jnp.int32)
    for i in range(steps):
        x = x_ref[:, i * chunk : (i + 1) * chunk]
        copies[i].wait()
        for j, k in enumerate(offsets):
            start = pl.multiple_of((spot ^ k) * cols, HEAD)
            y = jnp.dot(x, buf[i, :, pl.ds(start, cols)], preferred_element_type=F32)
            if i > 0:
                y = y + acc_ref[j]
            if i < steps - 1:
                acc_ref[j] = y
            else:
                outs[j][...] = y.astype(outs[j].dtype)


def pair_kernel(count, start, near_ref, *refs):
    refs[-1][...] = near_ref[...]
    for j in range(count):
        out_ref = refs[2 * count + j]
        rows = slice(start, start + out_ref.shape[0])
        out_ref[...] = (refs[j][rows] + refs[count + j][rows].astype(F32)).astype(BF16)


def pair_low_kernel(count, half, low_ref, other_ref, *refs):
    outs = refs[2 * count :]
    cols = refs[0].shape[1]
    for j in range(count):
        total = (refs[j][:half] + refs[count + j][:half].astype(F32)).astype(BF16)
        for h in range(cols // HEAD):
            outs[j][h * half : (h + 1) * half] = total[:, h * HEAD : (h + 1) * HEAD]
    base = cols // HEAD * half
    groups, height, _ = low_ref.shape
    for i in range(groups):
        total = low_ref[i].astype(F32) + other_ref[i].astype(F32)
        outs[0][base + i * height : base + (i + 1) * height] = total.astype(BF16)


def scaled_down_kernel(gain_ref, down_hbm, out_ref, buf, sems):
    per_dev, depth, rank = down_hbm.shape
    copies = [pltpu.make_async_copy(down_hbm.at[a], buf.at[a], sems.at[a]) for a in range(per_dev)]
    for copy in copies:
        copy.start()
    columns = []
    for b in range(depth // HEAD):
        columns.append(to_column(gain_ref[b : b + 1].astype(F32), HEAD))
    for a in range(per_dev):
        copies[a].wait()
        for b in range(depth // HEAD):
            span = slice(b * HEAD, (b + 1) * HEAD)
            out_ref[span, a * rank : (a + 1) * rank] = (
                buf[a, span].astype(F32) * columns[b]
            ).astype(BF16)


def aux_kernel(n_wide, per_dev, req_hbm, table_hbm, tok_hbm, sq_ref, *refs):
    sels = refs[:n_wide]
    req_ref, table_ref, tok_ref, sems = refs[n_wide:]
    copies = [
        pltpu.make_async_copy(req_hbm, req_ref, sems.at[0]),
        pltpu.make_async_copy(table_hbm, table_ref, sems.at[1]),
        pltpu.make_async_copy(tok_hbm, tok_ref, sems.at[2]),
    ]
    for copy in copies:
        copy.start()
    for copy in copies:
        copy.wait()
    rows = tok_ref.shape[0]
    place, _ = places(req_ref[...], table_ref, n_wide, per_dev)
    place = place.astype(F32)
    for k in range(n_wide):
        column = to_column(place[k : k + 1], rows).astype(jnp.int32)
        sels[k][...] = (iota((rows, HEAD), 1) == column).astype(BF16)
    tok = tok_ref[...]
    gram = lax.dot_general(tok, tok, (((1,), (1,)), ((), ())), preferred_element_type=F32)
    diag = iota((rows, rows), 0) == iota((rows, rows), 1)
    sq = jnp.sum(jnp.where(diag, gram, 0.0), axis=0, keepdims=True)
    block = jnp.zeros((8, HEAD), F32)
    for p in range(3):
        part = sq.astype(BF16).astype(F32)
        sq = sq - part
        for i in range(rows // HEAD):
            term = part[:, i * HEAD : (i + 1) * HEAD]
            block = jnp.where(iota((8, HEAD), 0) == p * (rows // HEAD) + i, term, block)
    sq_ref[...] = block


def slot_column(x_ref, cap):
    height = x_ref.shape[0]
    base = cap // 16 * 16
    row = x_ref[base : base + 16, :HEAD].astype(F32)[cap - base : cap - base + 1]
    column = to_column(row, height)
    return jnp.where(iota((height, 1), 0) < cap, column, -1.0)


def down_kernel(count, cap, with_sq, *refs):
    xs, down_ref = refs[:count], refs[count]
    sq_ref = refs[count + 1] if with_sq else None
    out_ref = refs[-1]
    height, depth = xs[0].shape
    rank = HEAD
    x = jnp.concatenate([x[...] for x in xs], axis=0) if count > 1 else xs[0][...]
    slot = [slot_column(x, cap) for x in xs]
    slot = jnp.concatenate(slot, axis=0) if count > 1 else slot[0]
    low = jnp.zeros((count * height, rank), F32)
    for g in range(down_ref.shape[1] // (2 * rank)):
        y = jnp.dot(
            x, down_ref[:, 2 * g * rank : 2 * (g + 1) * rank], preferred_element_type=F32
        )
        low = jnp.where(slot == 2 * g, y[:, :rank], low)
        low = jnp.where(slot == 2 * g + 1, y[:, rank:], low)
    for j in range(count):
        part = low[j * height : (j + 1) * height]
        if j == 0 and with_sq:
            tail = [jnp.zeros((cap, rank), F32), sq_ref[...]]
            if height > cap + 8:
                tail.append(jnp.zeros((height - cap - 8, rank), F32))
            part = part + jnp.concatenate(tail, axis=0)
        out_ref[j] = part.astype(BF16)


def low_term(ref, i, groups, height):
    if len(ref.shape) == 3:
        return ref[i].astype(F32)
    start = ref.shape[0] - (groups - i) * height
    return ref[start : start + height].astype(F32)


def low_sum_kernel(left_ref, right_ref, out_ref):
    groups, height, _ = out_ref.shape
    for i in range(groups):
        left = low_term(left_ref, i, groups, height)
        out_ref[i] = (left + low_term(right_ref, i, groups, height)).astype(BF16)


def head_is_key(heads, h):
    if heads % 2 == 0:
        return h % 2 == 0
    return (lax.axis_index("tensor").astype(jnp.int32) * heads + h) % 2 == 0


def up_kernel(count, n_parts, cap, with_sq, *refs):
    xs = refs[:count]
    parts = refs[count : count + n_parts]
    up_ref = refs[count + n_parts]
    outs = refs[count + n_parts + 1 :]
    per_dev, half, cols = up_ref.shape
    heads = cols // HEAD
    height, rank = outs[0].shape[0], 2 * half
    up = up_ref[...].reshape(per_dev * half, cols)
    sums = []
    for j in range(count):
        terms = [low_term(part, j, count, height) for part in parts]
        sums.append(sum(terms[1:], terms[0]))
    if with_sq:
        outs[count][...] = sums[0][cap : cap + 8]
    low = jnp.concatenate(sums, axis=0) if count > 1 else sums[0]
    slot = [slot_column(x, cap) for x in xs]
    slot = jnp.concatenate(slot, axis=0) if count > 1 else slot[0]
    left = iota((count * height, rank), 1) < half
    turned = pltpu.roll(low, half, 1)
    wide = []
    for source in (jnp.where(left, low, turned), jnp.where(left, turned, low)):
        pieces = []
        for g in range(per_dev // 2):
            mine = slot == jnp.where(left, 2.0 * g, 2.0 * g + 1)
            pieces.append(jnp.where(mine, source, 0.0).astype(BF16))
        wide.append(jnp.concatenate(pieces, axis=1))
    for h in range(heads):
        key = head_is_key(heads, h)
        if isinstance(key, bool):
            lhs = wide[0] if key else wide[1]
        else:
            lhs = jnp.where(key, wide[0].astype(F32), wide[1].astype(F32)).astype(BF16)
        span = slice(h * HEAD, (h + 1) * HEAD)
        y = jnp.dot(lhs, up[:, span], preferred_element_type=F32).astype(BF16)
        for j in range(count):
            outs[j][:, span] = y[j * height : (j + 1) * height]


def placed(sels, deltas):
    height, cols = deltas[0].shape
    blocks = []
    for delta in deltas:
        blocks.append(delta[...])
        if height < HEAD:
            blocks.append(jnp.zeros((HEAD - height, cols), BF16))
    lhs = jnp.concatenate([sel[...] for sel in sels], axis=1) if len(sels) > 1 else sels[0][...]
    return jnp.dot(lhs, jnp.concatenate(blocks, axis=0), preferred_element_type=F32)


def gather_kernel(n_pairs, count, half, sq_ref, base_ref, *refs):
    tops, bottoms = refs[:n_pairs], refs[n_pairs : 2 * n_pairs]
    deltas = refs[2 * n_pairs : 2 * n_pairs + count]
    sels = refs[2 * n_pairs + count : 2 * n_pairs + 2 * count]
    out_ref, scale_ref = refs[-2:]
    rows, cols = out_ref.shape
    pieces = rows // HEAD
    squares = []
    for i in range(pieces):
        total = sq_ref[i : i + 1]
        for p in range(1, 3):
            total = total + sq_ref[p * pieces + i : p * pieces + i + 1]
        squares.append(total)
    square = to_column(jnp.concatenate(squares, axis=1), rows)
    scale = lax.rsqrt(square * (1.0 / MODEL_WIDTH) + EPSILON)
    scale_ref[...] = jnp.broadcast_to(scale, (rows, HEAD))
    total = base_ref[...] + placed(sels, deltas)
    lower = total[half:]
    for bottom in bottoms:
        lower = lower + bottom[...].astype(F32)
    out_ref[half:] = lower
    for h in range(cols // HEAD):
        span = slice(h * HEAD, (h + 1) * HEAD)
        upper = total[:half, span]
        for top in tops:
            upper = upper + top[h * half : (h + 1) * half].astype(F32)
        out_ref[:half, span] = upper


def finish_kernel(count, sum_ref, near_ref, scale_ref, cos_ref, sin_ref, *refs):
    deltas, sels, out_ref = refs[:count], refs[count : 2 * count], refs[2 * count]
    rows, cols = out_ref.shape
    total = sum_ref[...] + near_ref[...].astype(F32) + placed(sels, deltas)
    heads = cols // HEAD
    scale = scale_ref[...]
    for h in range(heads):
        span = slice(h * HEAD, (h + 1) * HEAD)
        x = total[:, span] * scale
        key = head_is_key(heads, h)
        if key is False:
            out_ref[:, span] = x.astype(BF16)
            continue
        y = x * cos_ref[...] + pltpu.roll(x, HEAD // 2, 1) * sin_ref[...]
        if key is not True:
            y = jnp.where(key, y, x)
        out_ref[:, span] = y.astype(BF16)


def local(
    mesh_shape,
    tokens,
    attention_norm_gain,
    key_value_weight,
    adapter_down_weight,
    adapter_up_weight,
    request_adapter,
    adapter_storage_row,
    cached_token_length,
):
    n_wide, n_tensor = mesh_shape["wide"], mesh_shape["tensor"]
    rows, depth = tokens.shape
    per_dev, _, rank = adapter_down_weight.shape
    cols = adapter_up_weight.shape[2]
    cap = 104 if n_wide <= 4 else 64
    height = -(-(cap + 8) // 16) * 16
    req = request_adapter.reshape(1, rows)
    gain = attention_norm_gain.reshape(depth // HEAD, HEAD)

    def over(axis, array, k):
        size = mesh_shape[axis]
        return lax.ppermute(array, axis, [(i, i ^ k) for i in range(size)])

    small = [pltpu.VMEM((1, rows), jnp.int32), pltpu.SMEM(adapter_storage_row.shape, jnp.int32)]
    first, last = [0, 1], list(range(2, n_wide))

    order = list(range(n_wide - 1, -1, -1))
    *blocks, xg = call(
        functools.partial(dispatch_kernel, order, n_wide, per_dev, cap),
        "dispatch",
        [shape((height, depth), BF16)] * n_wide + [shape((rows, depth), BF16)],
        hbm=(req, adapter_storage_row, tokens, gain),
        hbm_outs=n_wide + 1,
        scratch=small
        + [
            pltpu.VMEM((rows, depth), BF16),
            pltpu.VMEM(gain.shape, BF16),
            pltpu.VMEM((n_wide, height, depth), BF16),
            pltpu.VMEM((rows, depth), BF16),
            pltpu.SemaphoreType.DMA((4,)),
            pltpu.SemaphoreType.DMA((n_wide + 1,)),
        ],
        flops=2 * n_wide * height * rows * depth,
        moved=2 * rows * depth * 4,
        limit=63,
    )
    held = [blocks[n_wide - 1 - k] for k in range(n_wide)]
    held[1:] = [over("wide", held[k], k) for k in range(1, n_wide)]

    twos = list(range(2, n_tensor, 2))
    far = [k ^ 1 for k in twos]
    offsets = far + [1] + twos + [0]
    chunk = math.gcd(depth, 512)
    steps = depth // chunk
    sums = call(
        functools.partial(base_kernel, offsets, cols),
        "base",
        [shape((rows, cols), BF16)] * (len(far) + 1) + [shape((rows, cols), F32)] * (len(twos) + 1),
        hbm=(xg, key_value_weight),
        scratch=[
            pltpu.VMEM((rows, depth), BF16),
            pltpu.VMEM((steps, chunk, key_value_weight.shape[1]), BF16),
            pltpu.VMEM((len(offsets), rows, cols), F32),
            pltpu.SemaphoreType.DMA((1 + steps,)),
        ],
        flops=2 * rows * depth * cols * n_tensor,
        moved=2 * depth * cols * n_tensor,
        limit=52,
    )
    away, near, own, base = sums[: len(far)], sums[len(far)], sums[len(far) + 1 : -1], sums[-1]
    beside = [over("tensor", p, 1) for p in away]
    (down,) = call(
        scaled_down_kernel,
        "scaled_down",
        [shape((depth, per_dev * rank), BF16)],
        vmem=(gain,),
        hbm=(adapter_down_weight,),
        after=(base,),
        scratch=[
            pltpu.VMEM((per_dev, depth, rank), BF16),
            pltpu.SemaphoreType.DMA((per_dev,)),
        ],
        flops=4 * depth * per_dev * rank,
        moved=4 * depth * per_dev * rank,
    )
    half_size = HEAD // 2
    freq_index = jnp.arange(half_size).astype(F32)
    inverse = jnp.exp(freq_index * (-2.0 / HEAD) * math.log(ROPE_BASE))
    angles = cached_token_length.astype(F32)[:, None] * inverse[None, :]
    cosine, sine = jnp.cos(angles), jnp.sin(angles)
    cosine = jnp.concatenate([cosine, cosine], axis=1)
    sine = jnp.concatenate([-sine, sine], axis=1)

    def down_block(group, extra, after):
        xs = [held[k] for k in group]
        (low,) = call(
            functools.partial(down_kernel, len(xs), cap, bool(extra)),
            "down_block",
            [shape((len(xs), height, rank), BF16)],
            vmem=(*xs, down, *extra),
            after=after,
            flops=2 * len(xs) * height * depth * rank * per_dev,
            moved=2 * per_dev * depth * rank,
        )
        return low

    def up_block(group, parts, with_sq, after):
        xs = [held[k] for k in group]
        outs = [shape((height, cols), BF16)] * len(xs)
        if with_sq:
            outs = outs + [shape((8, HEAD), F32)]
        return call(
            functools.partial(up_kernel, len(xs), len(parts), cap, with_sq),
            "up_block",
            outs,
            vmem=(*xs, *parts, adapter_up_weight),
            after=after,
            flops=2 * len(xs) * height * per_dev * rank * cols,
            moved=2 * per_dev * rank * cols,
        )

    low = down_block(first, (), ())
    sq, *sels = call(
        functools.partial(aux_kernel, n_wide, per_dev),
        "aux",
        [shape((8, HEAD), F32)]
        + [shape((rows, HEAD), BF16)] * n_wide,
        hbm=(req, adapter_storage_row, tokens),
        after=(low,),
        scratch=small + [pltpu.VMEM((rows, depth), BF16), pltpu.SemaphoreType.DMA((3,))],
        flops=2 * rows * rows * depth,
        moved=2 * rows * depth,
    )
    half = rows * 3 // 128 * 16
    upper = cols // HEAD * half
    other = over("tensor", low, 1)
    pairs = call(
        functools.partial(pair_low_kernel, len(twos), half),
        "pair_low_sums",
        [shape((upper + len(first) * height, HEAD), BF16)]
        + [shape((upper, HEAD), BF16)] * (len(twos) - 1),
        vmem=(low, other, *own, *beside),
        after=(sq,),
    )
    tops = [over("tensor", p, k) for p, k in zip(pairs, twos)]
    done = pairs[0]
    low, other = pairs[0], tops[0]
    for step in range(2, n_tensor.bit_length() - 1):
        (low,) = call(
            low_sum_kernel,
            "low_sum",
            [shape((len(first), height, rank), BF16)],
            vmem=(low, other),
        )
        other = over("tensor", low, 2**step)
    low_last = down_block(last, (sq,), (done,))
    last_parts = [low_last] + [over("tensor", low_last, k) for k in range(n_tensor - 1, 0, -1)]
    ups = up_block(first, [low, other], False, (low_last,))
    deltas = [u if k == 0 else over("wide", u, k) for k, u in zip(first, ups)]
    *pairs, near = call(
        functools.partial(pair_kernel, len(twos), half),
        "pair_sums",
        [shape((rows - half, cols), BF16)] * len(twos) + [shape((rows, cols), BF16)],
        vmem=(near, *own, *beside),
        after=(ups[0],),
    )
    near = over("tensor", near, 1)
    bottoms = [over("tensor", p, k) for p, k in zip(pairs, twos)]
    *ups, square = up_block(last, last_parts, True, (pairs[0],))
    last_deltas = [over("wide", u, k) for k, u in zip(last, ups)]
    total, scale = call(
        functools.partial(gather_kernel, len(tops), len(first), half),
        "gather",
        [shape((rows, cols), F32), shape((rows, HEAD), F32)],
        vmem=(square, base, *tops, *bottoms, *deltas, *[sels[k] for k in first]),
        after=(ups[0],),
        flops=2 * rows * cols * HEAD * len(first),
    )
    return call(
        functools.partial(finish_kernel, len(last)),
        "finish",
        [shape((rows, cols), BF16)],
        vmem=(total, near, scale, cosine, sine, *last_deltas, *[sels[k] for k in last]),
        flops=2 * rows * cols * HEAD,
    )[0]


def solution(mesh):
    return jax.shard_map(
        functools.partial(local, dict(mesh.shape)),
        mesh=mesh,
        in_specs=(
            P(("parts", "wide"), "tensor"),
            P("tensor"),
            P("tensor", None),
            P(("parts", "wide"), "tensor", None),
            P(("parts", "wide"), None, "tensor"),
            P(("parts", "wide")),
            P("parts"),
            P(("parts", "wide")),
        ),
        out_specs=P(("parts", "wide"), "tensor"),
        check_vma=False,
    )
```

```python
import functools
import math

import jax
import jax.numpy as jnp
from jax import lax
from jax.experimental import pallas as pl
from jax.experimental.pallas import tpu as pltpu
from jax.sharding import PartitionSpec as P

MODEL_WIDTH = 8192
HEAD = 128
EPSILON = 1e-05
ROPE_BASE = 500000.0
F32 = jnp.float32
BF16 = jnp.bfloat16


def iota(shape, axis):
    return lax.broadcasted_iota(jnp.int32, shape, axis)


def call(kernel, name, outs, vmem=(), hbm=(), after=(), scratch=(), flops=0, moved=0, limit=16, hbm_outs=0):
    def body(*refs):
        keep = len(vmem) + len(hbm)
        kernel(*refs[:keep], *refs[keep + len(after) :])

    return pl.pallas_call(
        body,
        out_shape=outs,
        in_specs=[pl.BlockSpec(memory_space=pltpu.VMEM)] * len(vmem)
        + [pl.BlockSpec(memory_space=pltpu.HBM)] * len(hbm)
        + [pl.BlockSpec(memory_space=pl.ANY)] * len(after),
        out_specs=[pl.BlockSpec(memory_space=pltpu.HBM)] * hbm_outs
        + [pl.BlockSpec(memory_space=pltpu.VMEM)] * (len(outs) - hbm_outs),
        scratch_shapes=scratch,
        compiler_params=pltpu.CompilerParams(vmem_limit_bytes=limit * 1024 * 1024),
        cost_estimate=pl.CostEstimate(flops=flops, bytes_accessed=moved, transcendentals=0),
        name=name,
    )(*vmem, *hbm, *after)


def shape(dims, dtype):
    return jax.ShapeDtypeStruct(dims, dtype)


def to_column(row, count):
    spread = iota((count, row.shape[1]), 0) == iota((count, row.shape[1]), 1)
    return jnp.sum(jnp.where(spread, row, 0.0), axis=1, keepdims=True)


def places(req, table, n_wide, per_dev):
    rows = req.shape[1]
    me = lax.axis_index("wide").astype(jnp.int32)
    stored = jnp.zeros_like(req)
    for a in range(table.shape[0]):
        stored = jnp.where(req == a, table[a], stored)
    owner = lax.div(stored, per_dev)
    slot = stored - owner * per_dev
    pad = -(-n_wide // 16) * 16
    hit = owner == (iota((pad, rows), 0) ^ me)
    earlier = (iota((rows, rows), 0) <= iota((rows, rows), 1)).astype(BF16)
    count = jnp.dot(hit.astype(BF16), earlier, preferred_element_type=F32)
    return jnp.where(hit, count.astype(jnp.int32) - 1, -1), slot


def dispatch_kernel(order, n_wide, per_dev, cap, req_hbm, table_hbm, tok_hbm, gain_hbm, *refs):
    xs = refs[: len(order)]
    xg_hbm, req_ref, table_ref, tok_ref, gain_ref, x_ref, xg_ref, sems, out_sems = refs[
        len(order) :
    ]
    rows, depth = tok_ref.shape
    height = x_ref.shape[1]
    loads = [
        pltpu.make_async_copy(req_hbm, req_ref, sems.at[0]),
        pltpu.make_async_copy(table_hbm, table_ref, sems.at[1]),
        pltpu.make_async_copy(tok_hbm, tok_ref, sems.at[2]),
        pltpu.make_async_copy(gain_hbm, gain_ref, sems.at[3]),
    ]
    for copy in loads:
        copy.start()
    loads[0].wait()
    loads[1].wait()
    place, slot = places(req_ref[...], table_ref, n_wide, per_dev)
    slots = jnp.broadcast_to(slot.astype(F32), (16, rows)).astype(BF16)
    picks, slot_rows = [], []
    for k in order:
        pick = (iota((HEAD, rows), 0) == place[k : k + 1]).astype(BF16)
        slot_rows.append(
            lax.dot_general(slots, pick, (((1,), (1,)), ((), ())), preferred_element_type=F32)
        )
        picks.append(pick[:height])
    loads[3].wait()
    loads[2].wait()
    stores = []
    for j, k in enumerate(order):
        if k == 1:
            for b in range(depth // HEAD):
                span = slice(b * HEAD, (b + 1) * HEAD)
                piece = tok_ref[:, span].astype(F32) * gain_ref[b : b + 1].astype(F32)
                xg_ref[:, span] = piece.astype(BF16)
            copy = pltpu.make_async_copy(xg_ref, xg_hbm, out_sems.at[len(order)])
            copy.start()
            stores.append(copy)
        y = jnp.dot(picks[j], tok_ref[...], preferred_element_type=F32)
        first = jnp.where(iota((height, HEAD), 0) == cap, slot_rows[j][:1], y[:, :HEAD])
        x_ref[j, :, :HEAD] = first.astype(BF16)
        x_ref[j, :, HEAD:] = y[:, HEAD:].astype(BF16)
        copy = pltpu.make_async_copy(x_ref.at[j], xs[j], out_sems.at[j])
        copy.start()
        stores.append(copy)
    for copy in stores:
        copy.wait()


def base_kernel(offsets, cols, xg_hbm, weight_hbm, *refs):
    count = len(offsets)
    outs = refs[:count]
    x_ref, buf, acc_ref, sems = refs[count:]
    steps, chunk, _ = buf.shape
    load = pltpu.make_async_copy(xg_hbm, x_ref, sems.at[0])
    copies = [
        pltpu.make_async_copy(weight_hbm.at[pl.ds(i * chunk, chunk)], buf.at[i], sems.at[1 + i])
        for i in range(steps)
    ]
    for copy in [load] + copies:
        copy.start()
    load.wait()
    spot = lax.axis_index("tensor").astype(jnp.int32)
    for i in range(steps):
        x = x_ref[:, i * chunk : (i + 1) * chunk]
        copies[i].wait()
        for j, k in enumerate(offsets):
            start = pl.multiple_of((spot ^ k) * cols, HEAD)
            y = jnp.dot(x, buf[i, :, pl.ds(start, cols)], preferred_element_type=F32)
            if i > 0:
                y = y + acc_ref[j]
            if i < steps - 1:
                acc_ref[j] = y
            else:
                outs[j][...] = y.astype(outs[j].dtype)


def pair_kernel(count, start, near_ref, *refs):
    refs[-1][...] = near_ref[...]
    for j in range(count):
        out_ref = refs[2 * count + j]
        rows = slice(start, start + out_ref.shape[0])
        out_ref[...] = (refs[j][rows] + refs[count + j][rows].astype(F32)).astype(BF16)


def pair_low_kernel(count, half, low_ref, other_ref, *refs):
    outs = refs[2 * count :]
    cols = refs[0].shape[1]
    for j in range(count):
        total = (refs[j][:half] + refs[count + j][:half].astype(F32)).astype(BF16)
        for h in range(cols // HEAD):
            outs[j][h * half : (h + 1) * half] = total[:, h * HEAD : (h + 1) * HEAD]
    base = cols // HEAD * half
    groups, height, _ = low_ref.shape
    for i in range(groups):
        total = low_ref[i].astype(F32) + other_ref[i].astype(F32)
        outs[0][base + i * height : base + (i + 1) * height] = total.astype(BF16)


def scaled_down_kernel(gain_ref, down_hbm, out_ref, buf, sems):
    per_dev, depth, rank = down_hbm.shape
    copies = [pltpu.make_async_copy(down_hbm.at[a], buf.at[a], sems.at[a]) for a in range(per_dev)]
    for copy in copies:
        copy.start()
    columns = []
    for b in range(depth // HEAD):
        columns.append(to_column(gain_ref[b : b + 1].astype(F32), HEAD))
    for a in range(per_dev):
        copies[a].wait()
        for b in range(depth // HEAD):
            span = slice(b * HEAD, (b + 1) * HEAD)
            out_ref[span, a * rank : (a + 1) * rank] = (
                buf[a, span].astype(F32) * columns[b]
            ).astype(BF16)


def aux_kernel(n_wide, per_dev, req_hbm, table_hbm, tok_hbm, sq_ref, *refs):
    sels = refs[:n_wide]
    req_ref, table_ref, tok_ref, sems = refs[n_wide:]
    copies = [
        pltpu.make_async_copy(req_hbm, req_ref, sems.at[0]),
        pltpu.make_async_copy(table_hbm, table_ref, sems.at[1]),
        pltpu.make_async_copy(tok_hbm, tok_ref, sems.at[2]),
    ]
    for copy in copies:
        copy.start()
    for copy in copies:
        copy.wait()
    rows = tok_ref.shape[0]
    place, _ = places(req_ref[...], table_ref, n_wide, per_dev)
    place = place.astype(F32)
    for k in range(n_wide):
        column = to_column(place[k : k + 1], rows).astype(jnp.int32)
        sels[k][...] = (iota((rows, HEAD), 1) == column).astype(BF16)
    tok = tok_ref[...]
    gram = lax.dot_general(tok, tok, (((1,), (1,)), ((), ())), preferred_element_type=F32)
    diag = iota((rows, rows), 0) == iota((rows, rows), 1)
    sq = jnp.sum(jnp.where(diag, gram, 0.0), axis=0, keepdims=True)
    block = jnp.zeros((8, HEAD), F32)
    for p in range(3):
        part = sq.astype(BF16).astype(F32)
        sq = sq - part
        for i in range(rows // HEAD):
            term = part[:, i * HEAD : (i + 1) * HEAD]
            block = jnp.where(iota((8, HEAD), 0) == p * (rows // HEAD) + i, term, block)
    sq_ref[...] = block


def slot_column(x_ref, cap):
    height = x_ref.shape[0]
    base = cap // 16 * 16
    row = x_ref[base : base + 16, :HEAD].astype(F32)[cap - base : cap - base + 1]
    column = to_column(row, height)
    return jnp.where(iota((height, 1), 0) < cap, column, -1.0)


def down_kernel(count, cap, with_sq, *refs):
    xs, down_ref = refs[:count], refs[count]
    sq_ref = refs[count + 1] if with_sq else None
    out_ref = refs[-1]
    height, depth = xs[0].shape
    rank = HEAD
    x = jnp.concatenate([x[...] for x in xs], axis=0) if count > 1 else xs[0][...]
    slot = [slot_column(x, cap) for x in xs]
    slot = jnp.concatenate(slot, axis=0) if count > 1 else slot[0]
    low = jnp.zeros((count * height, rank), F32)
    for g in range(down_ref.shape[1] // (2 * rank)):
        y = jnp.dot(
            x, down_ref[:, 2 * g * rank : 2 * (g + 1) * rank], preferred_element_type=F32
        )
        low = jnp.where(slot == 2 * g, y[:, :rank], low)
        low = jnp.where(slot == 2 * g + 1, y[:, rank:], low)
    for j in range(count):
        part = low[j * height : (j + 1) * height]
        if j == 0 and with_sq:
            tail = [jnp.zeros((cap, rank), F32), sq_ref[...]]
            if height > cap + 8:
                tail.append(jnp.zeros((height - cap - 8, rank), F32))
            part = part + jnp.concatenate(tail, axis=0)
        out_ref[j] = part.astype(BF16)


def low_term(ref, i, groups, height):
    if len(ref.shape) == 3:
        return ref[i].astype(F32)
    start = ref.shape[0] - (groups - i) * height
    return ref[start : start + height].astype(F32)


def low_sum_kernel(left_ref, right_ref, out_ref):
    groups, height, _ = out_ref.shape
    for i in range(groups):
        left = low_term(left_ref, i, groups, height)
        out_ref[i] = (left + low_term(right_ref, i, groups, height)).astype(BF16)


def head_is_key(heads, h):
    if heads % 2 == 0:
        return h % 2 == 0
    return (lax.axis_index("tensor").astype(jnp.int32) * heads + h) % 2 == 0


def up_kernel(count, n_parts, cap, with_sq, *refs):
    xs = refs[:count]
    parts = refs[count : count + n_parts]
    up_ref = refs[count + n_parts]
    outs = refs[count + n_parts + 1 :]
    per_dev, half, cols = up_ref.shape
    heads = cols // HEAD
    height, rank = outs[0].shape[0], 2 * half
    up = up_ref[...].reshape(per_dev * half, cols)
    sums = []
    for j in range(count):
        terms = [low_term(part, j, count, height) for part in parts]
        sums.append(sum(terms[1:], terms[0]))
    if with_sq:
        outs[count][...] = sums[0][cap : cap + 8]
    low = jnp.concatenate(sums, axis=0) if count > 1 else sums[0]
    slot = [slot_column(x, cap) for x in xs]
    slot = jnp.concatenate(slot, axis=0) if count > 1 else slot[0]
    left = iota((count * height, rank), 1) < half
    turned = pltpu.roll(low, half, 1)
    wide = []
    for source in (jnp.where(left, low, turned), jnp.where(left, turned, low)):
        pieces = []
        for g in range(per_dev // 2):
            mine = slot == jnp.where(left, 2.0 * g, 2.0 * g + 1)
            pieces.append(jnp.where(mine, source, 0.0).astype(BF16))
        wide.append(jnp.concatenate(pieces, axis=1))
    for h in range(heads):
        key = head_is_key(heads, h)
        if isinstance(key, bool):
            lhs = wide[0] if key else wide[1]
        else:
            lhs = jnp.where(key, wide[0].astype(F32), wide[1].astype(F32)).astype(BF16)
        span = slice(h * HEAD, (h + 1) * HEAD)
        y = jnp.dot(lhs, up[:, span], preferred_element_type=F32).astype(BF16)
        for j in range(count):
            outs[j][:, span] = y[j * height : (j + 1) * height]


def placed(sels, deltas):
    height, cols = deltas[0].shape
    blocks = []
    for delta in deltas:
        blocks.append(delta[...])
        if height < HEAD:
            blocks.append(jnp.zeros((HEAD - height, cols), BF16))
    lhs = jnp.concatenate([sel[...] for sel in sels], axis=1) if len(sels) > 1 else sels[0][...]
    return jnp.dot(lhs, jnp.concatenate(blocks, axis=0), preferred_element_type=F32)


def gather_kernel(n_pairs, count, half, sq_ref, base_ref, *refs):
    tops, bottoms = refs[:n_pairs], refs[n_pairs : 2 * n_pairs]
    deltas = refs[2 * n_pairs : 2 * n_pairs + count]
    sels = refs[2 * n_pairs + count : 2 * n_pairs + 2 * count]
    out_ref, scale_ref = refs[-2:]
    rows, cols = out_ref.shape
    pieces = rows // HEAD
    squares = []
    for i in range(pieces):
        total = sq_ref[i : i + 1]
        for p in range(1, 3):
            total = total + sq_ref[p * pieces + i : p * pieces + i + 1]
        squares.append(total)
    square = to_column(jnp.concatenate(squares, axis=1), rows)
    scale = lax.rsqrt(square * (1.0 / MODEL_WIDTH) + EPSILON)
    scale_ref[...] = jnp.broadcast_to(scale, (rows, HEAD))
    total = base_ref[...] + placed(sels, deltas)
    lower = total[half:]
    for bottom in bottoms:
        lower = lower + bottom[...].astype(F32)
    out_ref[half:] = lower
    for h in range(cols // HEAD):
        span = slice(h * HEAD, (h + 1) * HEAD)
        upper = total[:half, span]
        for top in tops:
            upper = upper + top[h * half : (h + 1) * half].astype(F32)
        out_ref[:half, span] = upper


def finish_kernel(count, sum_ref, near_ref, scale_ref, cos_ref, sin_ref, *refs):
    deltas, sels, out_ref = refs[:count], refs[count : 2 * count], refs[2 * count]
    rows, cols = out_ref.shape
    total = sum_ref[...] + near_ref[...].astype(F32) + placed(sels, deltas)
    heads = cols // HEAD
    scale = scale_ref[...]
    for h in range(heads):
        span = slice(h * HEAD, (h + 1) * HEAD)
        x = total[:, span] * scale
        key = head_is_key(heads, h)
        if key is False:
            out_ref[:, span] = x.astype(BF16)
            continue
        y = x * cos_ref[...] + pltpu.roll(x, HEAD // 2, 1) * sin_ref[...]
        if key is not True:
            y = jnp.where(key, y, x)
        out_ref[:, span] = y.astype(BF16)


def local(
    mesh_shape,
    tokens,
    attention_norm_gain,
    key_value_weight,
    adapter_down_weight,
    adapter_up_weight,
    request_adapter,
    adapter_storage_row,
    cached_token_length,
):
    n_wide, n_tensor = mesh_shape["wide"], mesh_shape["tensor"]
    rows, depth = tokens.shape
    per_dev, _, rank = adapter_down_weight.shape
    cols = adapter_up_weight.shape[2]
    cap = 104 if n_wide <= 4 else 64
    height = -(-(cap + 8) // 16) * 16
    req = request_adapter.reshape(1, rows)
    gain = attention_norm_gain.reshape(depth // HEAD, HEAD)

    def over(axis, array, k):
        size = mesh_shape[axis]
        return lax.ppermute(array, axis, [(i, i ^ k) for i in range(size)])

    small = [pltpu.VMEM((1, rows), jnp.int32), pltpu.SMEM(adapter_storage_row.shape, jnp.int32)]
    first, last = [0, 1], list(range(2, n_wide))

    order = list(range(n_wide - 1, -1, -1))
    *blocks, xg = call(
        functools.partial(dispatch_kernel, order, n_wide, per_dev, cap),
        "dispatch",
        [shape((height, depth), BF16)] * n_wide + [shape((rows, depth), BF16)],
        hbm=(req, adapter_storage_row, tokens, gain),
        hbm_outs=n_wide + 1,
        scratch=small
        + [
            pltpu.VMEM((rows, depth), BF16),
            pltpu.VMEM(gain.shape, BF16),
            pltpu.VMEM((n_wide, height, depth), BF16),
            pltpu.VMEM((rows, depth), BF16),
            pltpu.SemaphoreType.DMA((4,)),
            pltpu.SemaphoreType.DMA((n_wide + 1,)),
        ],
        flops=2 * n_wide * height * rows * depth,
        moved=2 * rows * depth * 4,
        limit=63,
    )
    held = [blocks[n_wide - 1 - k] for k in range(n_wide)]
    held[1:] = [over("wide", held[k], k) for k in range(1, n_wide)]

    twos = list(range(2, n_tensor, 2))
    far = [k ^ 1 for k in twos]
    offsets = far + [1] + twos + [0]
    chunk = math.gcd(depth, 512)
    steps = depth // chunk
    sums = call(
        functools.partial(base_kernel, offsets, cols),
        "base",
        [shape((rows, cols), BF16)] * (len(far) + 1) + [shape((rows, cols), F32)] * (len(twos) + 1),
        hbm=(xg, key_value_weight),
        scratch=[
            pltpu.VMEM((rows, depth), BF16),
            pltpu.VMEM((steps, chunk, key_value_weight.shape[1]), BF16),
            pltpu.VMEM((len(offsets), rows, cols), F32),
            pltpu.SemaphoreType.DMA((1 + steps,)),
        ],
        flops=2 * rows * depth * cols * n_tensor,
        moved=2 * depth * cols * n_tensor,
        limit=52,
    )
    away, near, own, base = sums[: len(far)], sums[len(far)], sums[len(far) + 1 : -1], sums[-1]
    beside = [over("tensor", p, 1) for p in away]
    (down,) = call(
        scaled_down_kernel,
        "scaled_down",
        [shape((depth, per_dev * rank), BF16)],
        vmem=(gain,),
        hbm=(adapter_down_weight,),
        after=(base,),
        scratch=[
            pltpu.VMEM((per_dev, depth, rank), BF16),
            pltpu.SemaphoreType.DMA((per_dev,)),
        ],
        flops=4 * depth * per_dev * rank,
        moved=4 * depth * per_dev * rank,
    )
    half_size = HEAD // 2
    freq_index = jnp.arange(half_size).astype(F32)
    inverse = jnp.exp(freq_index * (-2.0 / HEAD) * math.log(ROPE_BASE))
    angles = cached_token_length.astype(F32)[:, None] * inverse[None, :]
    cosine, sine = jnp.cos(angles), jnp.sin(angles)
    cosine = jnp.concatenate([cosine, cosine], axis=1)
    sine = jnp.concatenate([-sine, sine], axis=1)

    def down_block(group, extra, after):
        xs = [held[k] for k in group]
        (low,) = call(
            functools.partial(down_kernel, len(xs), cap, bool(extra)),
            "down_block",
            [shape((len(xs), height, rank), BF16)],
            vmem=(*xs, down, *extra),
            after=after,
            flops=2 * len(xs) * height * depth * rank * per_dev,
            moved=2 * per_dev * depth * rank,
        )
        return low

    def up_block(group, parts, with_sq, after):
        xs = [held[k] for k in group]
        outs = [shape((height, cols), BF16)] * len(xs)
        if with_sq:
            outs = outs + [shape((8, HEAD), F32)]
        return call(
            functools.partial(up_kernel, len(xs), len(parts), cap, with_sq),
            "up_block",
            outs,
            vmem=(*xs, *parts, adapter_up_weight),
            after=after,
            flops=2 * len(xs) * height * per_dev * rank * cols,
            moved=2 * per_dev * rank * cols,
        )

    low = down_block(first, (), ())
    sq, *sels = call(
        functools.partial(aux_kernel, n_wide, per_dev),
        "aux",
        [shape((8, HEAD), F32)]
        + [shape((rows, HEAD), BF16)] * n_wide,
        hbm=(req, adapter_storage_row, tokens),
        after=(low,),
        scratch=small + [pltpu.VMEM((rows, depth), BF16), pltpu.SemaphoreType.DMA((3,))],
        flops=2 * rows * rows * depth,
        moved=2 * rows * depth,
    )
    half = rows // 64 * 16
    upper = cols // HEAD * half
    other = over("tensor", low, 1)
    pairs = call(
        functools.partial(pair_low_kernel, len(twos), half),
        "pair_low_sums",
        [shape((upper + len(first) * height, HEAD), BF16)]
        + [shape((upper, HEAD), BF16)] * (len(twos) - 1),
        vmem=(low, other, *own, *beside),
        after=(sq,),
    )
    tops = [over("tensor", p, k) for p, k in zip(pairs, twos)]
    done = pairs[0]
    low, other = pairs[0], tops[0]
    for step in range(2, n_tensor.bit_length() - 1):
        (low,) = call(
            low_sum_kernel,
            "low_sum",
            [shape((len(first), height, rank), BF16)],
            vmem=(low, other),
        )
        other = over("tensor", low, 2**step)
    low_last = down_block(last, (sq,), (done,))
    last_parts = [low_last] + [over("tensor", low_last, k) for k in range(n_tensor - 1, 0, -1)]
    ups = up_block(first, [low, other], False, (low_last,))
    deltas = [u if k == 0 else over("wide", u, k) for k, u in zip(first, ups)]
    *pairs, near = call(
        functools.partial(pair_kernel, len(twos), half),
        "pair_sums",
        [shape((rows - half, cols), BF16)] * len(twos) + [shape((rows, cols), BF16)],
        vmem=(near, *own, *beside),
        after=(ups[0],),
    )
    near = over("tensor", near, 1)
    bottoms = [over("tensor", p, k) for p, k in zip(pairs, twos)]
    *ups, square = up_block(last, last_parts, True, (pairs[0],))
    last_deltas = [over("wide", u, k) for k, u in zip(last, ups)]
    total, scale = call(
        functools.partial(gather_kernel, len(tops), len(first), half),
        "gather",
        [shape((rows, cols), F32), shape((rows, HEAD), F32)],
        vmem=(square, base, *tops, *bottoms, *deltas, *[sels[k] for k in first]),
        after=(ups[0],),
        flops=2 * rows * cols * HEAD * len(first),
    )
    return call(
        functools.partial(finish_kernel, len(last)),
        "finish",
        [shape((rows, cols), BF16)],
        vmem=(total, near, scale, cosine, sine, *last_deltas, *[sels[k] for k in last]),
        flops=2 * rows * cols * HEAD,
    )[0]


def solution(mesh):
    return jax.shard_map(
        functools.partial(local, dict(mesh.shape)),
        mesh=mesh,
        in_specs=(
            P(("parts", "wide"), "tensor"),
            P("tensor"),
            P("tensor", None),
            P(("parts", "wide"), "tensor", None),
            P(("parts", "wide"), None, "tensor"),
            P(("parts", "wide")),
            P("parts"),
            P(("parts", "wide")),
        ),
        out_specs=P(("parts", "wide"), "tensor"),
        check_vma=False,
    )
```

```python
import functools
import math

import jax
import jax.numpy as jnp
from jax import lax
from jax.experimental import pallas as pl
from jax.experimental.pallas import tpu as pltpu
from jax.sharding import PartitionSpec as P

MODEL_WIDTH = 8192
HEAD = 128
EPSILON = 1e-05
ROPE_BASE = 500000.0
F32 = jnp.float32
BF16 = jnp.bfloat16


def iota(shape, axis):
    return lax.broadcasted_iota(jnp.int32, shape, axis)


def call(kernel, name, outs, vmem=(), hbm=(), after=(), scratch=(), flops=0, moved=0, limit=16, hbm_outs=0):
    def body(*refs):
        keep = len(vmem) + len(hbm)
        kernel(*refs[:keep], *refs[keep + len(after) :])

    return pl.pallas_call(
        body,
        out_shape=outs,
        in_specs=[pl.BlockSpec(memory_space=pltpu.VMEM)] * len(vmem)
        + [pl.BlockSpec(memory_space=pltpu.HBM)] * len(hbm)
        + [pl.BlockSpec(memory_space=pl.ANY)] * len(after),
        out_specs=[pl.BlockSpec(memory_space=pltpu.HBM)] * hbm_outs
        + [pl.BlockSpec(memory_space=pltpu.VMEM)] * (len(outs) - hbm_outs),
        scratch_shapes=scratch,
        compiler_params=pltpu.CompilerParams(vmem_limit_bytes=limit * 1024 * 1024),
        cost_estimate=pl.CostEstimate(flops=flops, bytes_accessed=moved, transcendentals=0),
        name=name,
    )(*vmem, *hbm, *after)


def shape(dims, dtype):
    return jax.ShapeDtypeStruct(dims, dtype)


def to_column(row, count):
    spread = iota((count, row.shape[1]), 0) == iota((count, row.shape[1]), 1)
    return jnp.sum(jnp.where(spread, row, 0.0), axis=1, keepdims=True)


def places(req, table, n_wide, per_dev):
    rows = req.shape[1]
    me = lax.axis_index("wide").astype(jnp.int32)
    stored = jnp.zeros_like(req)
    for a in range(table.shape[0]):
        stored = jnp.where(req == a, table[a], stored)
    owner = lax.div(stored, per_dev)
    slot = stored - owner * per_dev
    pad = -(-n_wide // 16) * 16
    hit = owner == (iota((pad, rows), 0) ^ me)
    earlier = (iota((rows, rows), 0) <= iota((rows, rows), 1)).astype(BF16)
    count = jnp.dot(hit.astype(BF16), earlier, preferred_element_type=F32)
    return jnp.where(hit, count.astype(jnp.int32) - 1, -1), slot


def dispatch_kernel(order, n_wide, per_dev, cap, req_hbm, table_hbm, tok_hbm, gain_hbm, *refs):
    xs = refs[: len(order)]
    xg_hbm, req_ref, table_ref, tok_ref, gain_ref, x_ref, xg_ref, sems, out_sems = refs[
        len(order) :
    ]
    rows, depth = tok_ref.shape
    height = x_ref.shape[1]
    loads = [
        pltpu.make_async_copy(req_hbm, req_ref, sems.at[0]),
        pltpu.make_async_copy(table_hbm, table_ref, sems.at[1]),
        pltpu.make_async_copy(gain_hbm, gain_ref, sems.at[2]),
    ]
    part = rows // 4
    for i in range(4):
        span = pl.ds(i * part, part)
        loads.append(pltpu.make_async_copy(tok_hbm.at[span], tok_ref.at[span], sems.at[3 + i]))
    for copy in loads:
        copy.start()
    loads[0].wait()
    loads[1].wait()
    place, slot = places(req_ref[...], table_ref, n_wide, per_dev)
    slots = jnp.broadcast_to(slot.astype(F32), (16, rows)).astype(BF16)
    picks, slot_rows = [], []
    for k in order:
        pick = (iota((HEAD, rows), 0) == place[k : k + 1]).astype(BF16)
        slot_rows.append(
            lax.dot_general(slots, pick, (((1,), (1,)), ((), ())), preferred_element_type=F32)
        )
        picks.append(pick[:height])
    for copy in loads[2:]:
        copy.wait()
    stores = []
    for j, k in enumerate(order):
        if k == 1:
            for b in range(depth // HEAD):
                span = slice(b * HEAD, (b + 1) * HEAD)
                piece = tok_ref[:, span].astype(F32) * gain_ref[b : b + 1].astype(F32)
                xg_ref[:, span] = piece.astype(BF16)
            copy = pltpu.make_async_copy(xg_ref, xg_hbm, out_sems.at[len(order)])
            copy.start()
            stores.append(copy)
        y = jnp.dot(picks[j], tok_ref[...], preferred_element_type=F32)
        first = jnp.where(iota((height, HEAD), 0) == cap, slot_rows[j][:1], y[:, :HEAD])
        x_ref[j, :, :HEAD] = first.astype(BF16)
        x_ref[j, :, HEAD:] = y[:, HEAD:].astype(BF16)
        copy = pltpu.make_async_copy(x_ref.at[j], xs[j], out_sems.at[j])
        copy.start()
        stores.append(copy)
    for copy in stores:
        copy.wait()


def base_kernel(offsets, cols, xg_hbm, weight_hbm, *refs):
    count = len(offsets)
    outs = refs[:count]
    x_ref, buf, acc_ref, sems = refs[count:]
    steps, chunk, _ = buf.shape
    load = pltpu.make_async_copy(xg_hbm, x_ref, sems.at[0])
    copies = [
        pltpu.make_async_copy(weight_hbm.at[pl.ds(i * chunk, chunk)], buf.at[i], sems.at[1 + i])
        for i in range(steps)
    ]
    for copy in [load] + copies:
        copy.start()
    load.wait()
    spot = lax.axis_index("tensor").astype(jnp.int32)
    for i in range(steps):
        x = x_ref[:, i * chunk : (i + 1) * chunk]
        copies[i].wait()
        for j, k in enumerate(offsets):
            start = pl.multiple_of((spot ^ k) * cols, HEAD)
            y = jnp.dot(x, buf[i, :, pl.ds(start, cols)], preferred_element_type=F32)
            if i > 0:
                y = y + acc_ref[j]
            if i < steps - 1:
                acc_ref[j] = y
            else:
                outs[j][...] = y.astype(outs[j].dtype)


def pair_kernel(count, start, near_ref, *refs):
    refs[-1][...] = near_ref[...]
    for j in range(count):
        out_ref = refs[2 * count + j]
        rows = slice(start, start + out_ref.shape[0])
        out_ref[...] = (refs[j][rows] + refs[count + j][rows].astype(F32)).astype(BF16)


def pair_low_kernel(count, low_ref, other_ref, *refs):
    outs = refs[2 * count :]
    cols = refs[0].shape[1]
    half = refs[0].shape[0] // 2
    for j in range(count):
        total = (refs[j][:half] + refs[count + j][:half].astype(F32)).astype(BF16)
        for h in range(cols // HEAD):
            outs[j][h * half : (h + 1) * half] = total[:, h * HEAD : (h + 1) * HEAD]
    base = cols // HEAD * half
    groups, height, _ = low_ref.shape
    for i in range(groups):
        total = low_ref[i].astype(F32) + other_ref[i].astype(F32)
        outs[0][base + i * height : base + (i + 1) * height] = total.astype(BF16)


def scaled_down_kernel(gain_ref, down_hbm, out_ref, buf, sems):
    per_dev, depth, rank = down_hbm.shape
    copies = [pltpu.make_async_copy(down_hbm.at[a], buf.at[a], sems.at[a]) for a in range(per_dev)]
    for copy in copies:
        copy.start()
    columns = []
    for b in range(depth // HEAD):
        columns.append(to_column(gain_ref[b : b + 1].astype(F32), HEAD))
    for a in range(per_dev):
        copies[a].wait()
        for b in range(depth // HEAD):
            span = slice(b * HEAD, (b + 1) * HEAD)
            out_ref[span, a * rank : (a + 1) * rank] = (
                buf[a, span].astype(F32) * columns[b]
            ).astype(BF16)


def aux_kernel(n_wide, per_dev, req_hbm, table_hbm, tok_hbm, sq_ref, *refs):
    sels = refs[:n_wide]
    req_ref, table_ref, tok_ref, sems = refs[n_wide:]
    copies = [
        pltpu.make_async_copy(req_hbm, req_ref, sems.at[0]),
        pltpu.make_async_copy(table_hbm, table_ref, sems.at[1]),
        pltpu.make_async_copy(tok_hbm, tok_ref, sems.at[2]),
    ]
    for copy in copies:
        copy.start()
    for copy in copies:
        copy.wait()
    rows = tok_ref.shape[0]
    place, _ = places(req_ref[...], table_ref, n_wide, per_dev)
    place = place.astype(F32)
    for k in range(n_wide):
        column = to_column(place[k : k + 1], rows).astype(jnp.int32)
        sels[k][...] = (iota((rows, HEAD), 1) == column).astype(BF16)
    tok = tok_ref[...]
    gram = lax.dot_general(tok, tok, (((1,), (1,)), ((), ())), preferred_element_type=F32)
    diag = iota((rows, rows), 0) == iota((rows, rows), 1)
    sq = jnp.sum(jnp.where(diag, gram, 0.0), axis=0, keepdims=True)
    block = jnp.zeros((8, HEAD), F32)
    for p in range(3):
        part = sq.astype(BF16).astype(F32)
        sq = sq - part
        for i in range(rows // HEAD):
            term = part[:, i * HEAD : (i + 1) * HEAD]
            block = jnp.where(iota((8, HEAD), 0) == p * (rows // HEAD) + i, term, block)
    sq_ref[...] = block


def slot_column(x_ref, cap):
    height = x_ref.shape[0]
    base = cap // 16 * 16
    row = x_ref[base : base + 16, :HEAD].astype(F32)[cap - base : cap - base + 1]
    column = to_column(row, height)
    return jnp.where(iota((height, 1), 0) < cap, column, -1.0)


def down_kernel(count, cap, with_sq, *refs):
    xs, down_ref = refs[:count], refs[count]
    sq_ref = refs[count + 1] if with_sq else None
    out_ref = refs[-1]
    height, depth = xs[0].shape
    rank = HEAD
    x = jnp.concatenate([x[...] for x in xs], axis=0) if count > 1 else xs[0][...]
    slot = [slot_column(x, cap) for x in xs]
    slot = jnp.concatenate(slot, axis=0) if count > 1 else slot[0]
    low = jnp.zeros((count * height, rank), F32)
    for g in range(down_ref.shape[1] // (2 * rank)):
        y = jnp.dot(
            x, down_ref[:, 2 * g * rank : 2 * (g + 1) * rank], preferred_element_type=F32
        )
        low = jnp.where(slot == 2 * g, y[:, :rank], low)
        low = jnp.where(slot == 2 * g + 1, y[:, rank:], low)
    for j in range(count):
        part = low[j * height : (j + 1) * height]
        if j == 0 and with_sq:
            tail = [jnp.zeros((cap, rank), F32), sq_ref[...]]
            if height > cap + 8:
                tail.append(jnp.zeros((height - cap - 8, rank), F32))
            part = part + jnp.concatenate(tail, axis=0)
        out_ref[j] = part.astype(BF16)


def low_term(ref, i, groups, height):
    if len(ref.shape) == 3:
        return ref[i].astype(F32)
    start = ref.shape[0] - (groups - i) * height
    return ref[start : start + height].astype(F32)


def low_sum_kernel(left_ref, right_ref, out_ref):
    groups, height, _ = out_ref.shape
    for i in range(groups):
        left = low_term(left_ref, i, groups, height)
        out_ref[i] = (left + low_term(right_ref, i, groups, height)).astype(BF16)


def head_is_key(heads, h):
    if heads % 2 == 0:
        return h % 2 == 0
    return (lax.axis_index("tensor").astype(jnp.int32) * heads + h) % 2 == 0


def up_kernel(count, n_parts, cap, with_sq, *refs):
    xs = refs[:count]
    parts = refs[count : count + n_parts]
    up_ref = refs[count + n_parts]
    outs = refs[count + n_parts + 1 :]
    per_dev, half, cols = up_ref.shape
    heads = cols // HEAD
    height, rank = outs[0].shape[0], 2 * half
    up = up_ref[...].reshape(per_dev * half, cols)
    sums = []
    for j in range(count):
        terms = [low_term(part, j, count, height) for part in parts]
        sums.append(sum(terms[1:], terms[0]))
    if with_sq:
        outs[count][...] = sums[0][cap : cap + 8]
    low = jnp.concatenate(sums, axis=0) if count > 1 else sums[0]
    slot = [slot_column(x, cap) for x in xs]
    slot = jnp.concatenate(slot, axis=0) if count > 1 else slot[0]
    left = iota((count * height, rank), 1) < half
    turned = pltpu.roll(low, half, 1)
    wide = []
    for source in (jnp.where(left, low, turned), jnp.where(left, turned, low)):
        pieces = []
        for g in range(per_dev // 2):
            mine = slot == jnp.where(left, 2.0 * g, 2.0 * g + 1)
            pieces.append(jnp.where(mine, source, 0.0).astype(BF16))
        wide.append(jnp.concatenate(pieces, axis=1))
    for h in range(heads):
        key = head_is_key(heads, h)
        if isinstance(key, bool):
            lhs = wide[0] if key else wide[1]
        else:
            lhs = jnp.where(key, wide[0].astype(F32), wide[1].astype(F32)).astype(BF16)
        span = slice(h * HEAD, (h + 1) * HEAD)
        y = jnp.dot(lhs, up[:, span], preferred_element_type=F32).astype(BF16)
        for j in range(count):
            outs[j][:, span] = y[j * height : (j + 1) * height]


def placed(sels, deltas):
    height, cols = deltas[0].shape
    blocks = []
    for delta in deltas:
        blocks.append(delta[...])
        if height < HEAD:
            blocks.append(jnp.zeros((HEAD - height, cols), BF16))
    lhs = jnp.concatenate([sel[...] for sel in sels], axis=1) if len(sels) > 1 else sels[0][...]
    return jnp.dot(lhs, jnp.concatenate(blocks, axis=0), preferred_element_type=F32)


def gather_kernel(n_pairs, count, sq_ref, base_ref, *refs):
    tops, bottoms = refs[:n_pairs], refs[n_pairs : 2 * n_pairs]
    deltas = refs[2 * n_pairs : 2 * n_pairs + count]
    sels = refs[2 * n_pairs + count : 2 * n_pairs + 2 * count]
    out_ref, scale_ref = refs[-2:]
    rows, cols = out_ref.shape
    pieces = rows // HEAD
    squares = []
    for i in range(pieces):
        total = sq_ref[i : i + 1]
        for p in range(1, 3):
            total = total + sq_ref[p * pieces + i : p * pieces + i + 1]
        squares.append(total)
    square = to_column(jnp.concatenate(squares, axis=1), rows)
    scale = lax.rsqrt(square * (1.0 / MODEL_WIDTH) + EPSILON)
    scale_ref[...] = jnp.broadcast_to(scale, (rows, HEAD))
    total = base_ref[...] + placed(sels, deltas)
    half = rows // 2
    lower = total[half:]
    for bottom in bottoms:
        lower = lower + bottom[...].astype(F32)
    out_ref[half:] = lower
    for h in range(cols // HEAD):
        span = slice(h * HEAD, (h + 1) * HEAD)
        upper = total[:half, span]
        for top in tops:
            upper = upper + top[h * half : (h + 1) * half].astype(F32)
        out_ref[:half, span] = upper


def finish_kernel(count, sum_ref, near_ref, scale_ref, cos_ref, sin_ref, *refs):
    deltas, sels, out_ref = refs[:count], refs[count : 2 * count], refs[2 * count]
    rows, cols = out_ref.shape
    total = sum_ref[...] + near_ref[...].astype(F32) + placed(sels, deltas)
    heads = cols // HEAD
    scale = scale_ref[...]
    for h in range(heads):
        span = slice(h * HEAD, (h + 1) * HEAD)
        x = total[:, span] * scale
        key = head_is_key(heads, h)
        if key is False:
            out_ref[:, span] = x.astype(BF16)
            continue
        y = x * cos_ref[...] + pltpu.roll(x, HEAD // 2, 1) * sin_ref[...]
        if key is not True:
            y = jnp.where(key, y, x)
        out_ref[:, span] = y.astype(BF16)


def local(
    mesh_shape,
    tokens,
    attention_norm_gain,
    key_value_weight,
    adapter_down_weight,
    adapter_up_weight,
    request_adapter,
    adapter_storage_row,
    cached_token_length,
):
    n_wide, n_tensor = mesh_shape["wide"], mesh_shape["tensor"]
    rows, depth = tokens.shape
    per_dev, _, rank = adapter_down_weight.shape
    cols = adapter_up_weight.shape[2]
    cap = 104 if n_wide <= 4 else 64
    height = -(-(cap + 8) // 16) * 16
    req = request_adapter.reshape(1, rows)
    gain = attention_norm_gain.reshape(depth // HEAD, HEAD)

    def over(axis, array, k):
        size = mesh_shape[axis]
        return lax.ppermute(array, axis, [(i, i ^ k) for i in range(size)])

    small = [pltpu.VMEM((1, rows), jnp.int32), pltpu.SMEM(adapter_storage_row.shape, jnp.int32)]
    first, last = [0, 1], list(range(2, n_wide))

    order = list(range(n_wide - 1, -1, -1))
    *blocks, xg = call(
        functools.partial(dispatch_kernel, order, n_wide, per_dev, cap),
        "dispatch",
        [shape((height, depth), BF16)] * n_wide + [shape((rows, depth), BF16)],
        hbm=(req, adapter_storage_row, tokens, gain),
        hbm_outs=n_wide + 1,
        scratch=small
        + [
            pltpu.VMEM((rows, depth), BF16),
            pltpu.VMEM(gain.shape, BF16),
            pltpu.VMEM((n_wide, height, depth), BF16),
            pltpu.VMEM((rows, depth), BF16),
            pltpu.SemaphoreType.DMA((7,)),
            pltpu.SemaphoreType.DMA((n_wide + 1,)),
        ],
        flops=2 * n_wide * height * rows * depth,
        moved=2 * rows * depth * 4,
        limit=63,
    )
    held = [blocks[n_wide - 1 - k] for k in range(n_wide)]
    held[1:] = [over("wide", held[k], k) for k in range(1, n_wide)]

    twos = list(range(2, n_tensor, 2))
    far = [k ^ 1 for k in twos]
    offsets = far + [1] + twos + [0]
    chunk = math.gcd(depth, 256)
    steps = depth // chunk
    sums = call(
        functools.partial(base_kernel, offsets, cols),
        "base",
        [shape((rows, cols), BF16)] * (len(far) + 1) + [shape((rows, cols), F32)] * (len(twos) + 1),
        hbm=(xg, key_value_weight),
        scratch=[
            pltpu.VMEM((rows, depth), BF16),
            pltpu.VMEM((steps, chunk, key_value_weight.shape[1]), BF16),
            pltpu.VMEM((len(offsets), rows, cols), F32),
            pltpu.SemaphoreType.DMA((1 + steps,)),
        ],
        flops=2 * rows * depth * cols * n_tensor,
        moved=2 * depth * cols * n_tensor,
        limit=52,
    )
    away, near, own, base = sums[: len(far)], sums[len(far)], sums[len(far) + 1 : -1], sums[-1]
    beside = [over("tensor", p, 1) for p in away]
    (down,) = call(
        scaled_down_kernel,
        "scaled_down",
        [shape((depth, per_dev * rank), BF16)],
        vmem=(gain,),
        hbm=(adapter_down_weight,),
        after=(base,),
        scratch=[
            pltpu.VMEM((per_dev, depth, rank), BF16),
            pltpu.SemaphoreType.DMA((per_dev,)),
        ],
        flops=4 * depth * per_dev * rank,
        moved=4 * depth * per_dev * rank,
    )
    half_size = HEAD // 2
    freq_index = jnp.arange(half_size).astype(F32)
    inverse = jnp.exp(freq_index * (-2.0 / HEAD) * math.log(ROPE_BASE))
    angles = cached_token_length.astype(F32)[:, None] * inverse[None, :]
    cosine, sine = jnp.cos(angles), jnp.sin(angles)
    cosine = jnp.concatenate([cosine, cosine], axis=1)
    sine = jnp.concatenate([-sine, sine], axis=1)

    def down_block(group, extra, after):
        xs = [held[k] for k in group]
        (low,) = call(
            functools.partial(down_kernel, len(xs), cap, bool(extra)),
            "down_block",
            [shape((len(xs), height, rank), BF16)],
            vmem=(*xs, down, *extra),
            after=after,
            flops=2 * len(xs) * height * depth * rank * per_dev,
            moved=2 * per_dev * depth * rank,
        )
        return low

    def up_block(group, parts, with_sq, after):
        xs = [held[k] for k in group]
        outs = [shape((height, cols), BF16)] * len(xs)
        if with_sq:
            outs = outs + [shape((8, HEAD), F32)]
        return call(
            functools.partial(up_kernel, len(xs), len(parts), cap, with_sq),
            "up_block",
            outs,
            vmem=(*xs, *parts, adapter_up_weight),
            after=after,
            flops=2 * len(xs) * height * per_dev * rank * cols,
            moved=2 * per_dev * rank * cols,
        )

    low = down_block(first, (), ())
    sq, *sels = call(
        functools.partial(aux_kernel, n_wide, per_dev),
        "aux",
        [shape((8, HEAD), F32)]
        + [shape((rows, HEAD), BF16)] * n_wide,
        hbm=(req, adapter_storage_row, tokens),
        after=(low,),
        scratch=small + [pltpu.VMEM((rows, depth), BF16), pltpu.SemaphoreType.DMA((3,))],
        flops=2 * rows * rows * depth,
        moved=2 * rows * depth,
    )
    half = rows // 2
    upper = cols // HEAD * half
    other = over("tensor", low, 1)
    pairs = call(
        functools.partial(pair_low_kernel, len(twos)),
        "pair_low_sums",
        [shape((upper + len(first) * height, HEAD), BF16)]
        + [shape((upper, HEAD), BF16)] * (len(twos) - 1),
        vmem=(low, other, *own, *beside),
        after=(sq,),
    )
    tops = [over("tensor", p, k) for p, k in zip(pairs, twos)]
    done = pairs[0]
    low, other = pairs[0], tops[0]
    for step in range(2, n_tensor.bit_length() - 1):
        (low,) = call(
            low_sum_kernel,
            "low_sum",
            [shape((len(first), height, rank), BF16)],
            vmem=(low, other),
        )
        other = over("tensor", low, 2**step)
    low_last = down_block(last, (sq,), (done,))
    last_parts = [low_last] + [over("tensor", low_last, k) for k in range(n_tensor - 1, 0, -1)]
    ups = up_block(first, [low, other], False, (low_last,))
    deltas = [u if k == 0 else over("wide", u, k) for k, u in zip(first, ups)]
    *pairs, near = call(
        functools.partial(pair_kernel, len(twos), half),
        "pair_sums",
        [shape((half, cols), BF16)] * len(twos) + [shape((rows, cols), BF16)],
        vmem=(near, *own, *beside),
        after=(ups[0],),
    )
    near = over("tensor", near, 1)
    bottoms = [over("tensor", p, k) for p, k in zip(pairs, twos)]
    *ups, square = up_block(last, last_parts, True, (pairs[0],))
    last_deltas = [over("wide", u, k) for k, u in zip(last, ups)]
    total, scale = call(
        functools.partial(gather_kernel, len(bottoms), len(first)),
        "gather",
        [shape((rows, cols), F32), shape((rows, HEAD), F32)],
        vmem=(square, base, *tops, *bottoms, *deltas, *[sels[k] for k in first]),
        after=(ups[0],),
        flops=2 * rows * cols * HEAD * len(first),
    )
    return call(
        functools.partial(finish_kernel, len(last)),
        "finish",
        [shape((rows, cols), BF16)],
        vmem=(total, near, scale, cosine, sine, *last_deltas, *[sels[k] for k in last]),
        flops=2 * rows * cols * HEAD,
    )[0]


def solution(mesh):
    return jax.shard_map(
        functools.partial(local, dict(mesh.shape)),
        mesh=mesh,
        in_specs=(
            P(("parts", "wide"), "tensor"),
            P("tensor"),
            P("tensor", None),
            P(("parts", "wide"), "tensor", None),
            P(("parts", "wide"), None, "tensor"),
            P(("parts", "wide")),
            P("parts"),
            P(("parts", "wide")),
        ),
        out_specs=P(("parts", "wide"), "tensor"),
        check_vma=False,
    )
```

```python
import functools
import math

import jax
import jax.numpy as jnp
from jax import lax
from jax.experimental import pallas as pl
from jax.experimental.pallas import tpu as pltpu
from jax.sharding import PartitionSpec as P

MODEL_WIDTH = 8192
HEAD = 128
EPSILON = 1e-05
ROPE_BASE = 500000.0
F32 = jnp.float32
BF16 = jnp.bfloat16


def iota(shape, axis):
    return lax.broadcasted_iota(jnp.int32, shape, axis)


def call(kernel, name, outs, vmem=(), hbm=(), after=(), scratch=(), flops=0, moved=0, limit=16, hbm_outs=0):
    def body(*refs):
        keep = len(vmem) + len(hbm)
        kernel(*refs[:keep], *refs[keep + len(after) :])

    return pl.pallas_call(
        body,
        out_shape=outs,
        in_specs=[pl.BlockSpec(memory_space=pltpu.VMEM)] * len(vmem)
        + [pl.BlockSpec(memory_space=pltpu.HBM)] * len(hbm)
        + [pl.BlockSpec(memory_space=pl.ANY)] * len(after),
        out_specs=[pl.BlockSpec(memory_space=pltpu.HBM)] * hbm_outs
        + [pl.BlockSpec(memory_space=pltpu.VMEM)] * (len(outs) - hbm_outs),
        scratch_shapes=scratch,
        compiler_params=pltpu.CompilerParams(vmem_limit_bytes=limit * 1024 * 1024),
        cost_estimate=pl.CostEstimate(flops=flops, bytes_accessed=moved, transcendentals=0),
        name=name,
    )(*vmem, *hbm, *after)


def shape(dims, dtype):
    return jax.ShapeDtypeStruct(dims, dtype)


def to_column(row, count):
    spread = iota((count, row.shape[1]), 0) == iota((count, row.shape[1]), 1)
    return jnp.sum(jnp.where(spread, row, 0.0), axis=1, keepdims=True)


def places(req, table, n_wide, per_dev):
    rows = req.shape[1]
    me = lax.axis_index("wide").astype(jnp.int32)
    stored = jnp.zeros_like(req)
    for a in range(table.shape[0]):
        stored = jnp.where(req == a, table[a], stored)
    owner = lax.div(stored, per_dev)
    slot = stored - owner * per_dev
    pad = -(-n_wide // 16) * 16
    hit = owner == (iota((pad, rows), 0) ^ me)
    earlier = (iota((rows, rows), 0) <= iota((rows, rows), 1)).astype(BF16)
    count = jnp.dot(hit.astype(BF16), earlier, preferred_element_type=F32)
    return jnp.where(hit, count.astype(jnp.int32) - 1, -1), slot


def dispatch_kernel(order, n_wide, per_dev, cap, req_hbm, table_hbm, tok_hbm, gain_hbm, *refs):
    xs = refs[: len(order)]
    xg_hbm, req_ref, table_ref, tok_ref, gain_ref, x_ref, xg_ref, sems, out_sems = refs[
        len(order) :
    ]
    rows, depth = tok_ref.shape
    height = x_ref.shape[1]
    loads = [
        pltpu.make_async_copy(req_hbm, req_ref, sems.at[0]),
        pltpu.make_async_copy(table_hbm, table_ref, sems.at[1]),
        pltpu.make_async_copy(gain_hbm, gain_ref, sems.at[2]),
    ]
    part = rows // 4
    for i in range(4):
        span = pl.ds(i * part, part)
        loads.append(pltpu.make_async_copy(tok_hbm.at[span], tok_ref.at[span], sems.at[3 + i]))
    for copy in loads:
        copy.start()
    loads[0].wait()
    loads[1].wait()
    place, slot = places(req_ref[...], table_ref, n_wide, per_dev)
    slots = jnp.broadcast_to(slot.astype(F32), (16, rows)).astype(BF16)
    picks, slot_rows = [], []
    for k in order:
        pick = (iota((HEAD, rows), 0) == place[k : k + 1]).astype(BF16)
        slot_rows.append(
            lax.dot_general(slots, pick, (((1,), (1,)), ((), ())), preferred_element_type=F32)
        )
        picks.append(pick[:height])
    for copy in loads[2:]:
        copy.wait()
    stores = []
    for j, k in enumerate(order):
        if k == 1:
            for b in range(depth // HEAD):
                span = slice(b * HEAD, (b + 1) * HEAD)
                piece = tok_ref[:, span].astype(F32) * gain_ref[b : b + 1].astype(F32)
                xg_ref[:, span] = piece.astype(BF16)
            copy = pltpu.make_async_copy(xg_ref, xg_hbm, out_sems.at[len(order)])
            copy.start()
            stores.append(copy)
        y = jnp.dot(picks[j], tok_ref[...], preferred_element_type=F32)
        first = jnp.where(iota((height, HEAD), 0) == cap, slot_rows[j][:1], y[:, :HEAD])
        x_ref[j, :, :HEAD] = first.astype(BF16)
        x_ref[j, :, HEAD:] = y[:, HEAD:].astype(BF16)
        copy = pltpu.make_async_copy(x_ref.at[j], xs[j], out_sems.at[j])
        copy.start()
        stores.append(copy)
    for copy in stores:
        copy.wait()


def base_kernel(offsets, cols, xg_hbm, weight_hbm, *refs):
    count = len(offsets)
    outs = refs[:count]
    x_ref, buf, acc_ref, sems = refs[count:]
    steps, chunk, _ = buf.shape
    load = pltpu.make_async_copy(xg_hbm, x_ref, sems.at[0])
    copies = [
        pltpu.make_async_copy(weight_hbm.at[pl.ds(i * chunk, chunk)], buf.at[i], sems.at[1 + i])
        for i in range(steps)
    ]
    for copy in [load] + copies:
        copy.start()
    load.wait()
    spot = lax.axis_index("tensor").astype(jnp.int32)
    for i in range(steps):
        x = x_ref[:, i * chunk : (i + 1) * chunk]
        copies[i].wait()
        for j, k in enumerate(offsets):
            start = pl.multiple_of((spot ^ k) * cols, HEAD)
            y = jnp.dot(x, buf[i, :, pl.ds(start, cols)], preferred_element_type=F32)
            if i > 0:
                y = y + acc_ref[j]
            if i < steps - 1:
                acc_ref[j] = y
            else:
                outs[j][...] = y.astype(outs[j].dtype)


def pair_kernel(count, start, near_ref, *refs):
    refs[-1][...] = near_ref[...]
    for j in range(count):
        out_ref = refs[2 * count + j]
        rows = slice(start, start + out_ref.shape[0])
        out_ref[...] = (refs[j][rows] + refs[count + j][rows].astype(F32)).astype(BF16)


def pair_low_kernel(count, half, low_ref, other_ref, *refs):
    outs = refs[2 * count :]
    cols = refs[0].shape[1]
    for j in range(count):
        total = (refs[j][:half] + refs[count + j][:half].astype(F32)).astype(BF16)
        for h in range(cols // HEAD):
            outs[j][h * half : (h + 1) * half] = total[:, h * HEAD : (h + 1) * HEAD]
    base = cols // HEAD * half
    groups, height, _ = low_ref.shape
    for i in range(groups):
        total = low_ref[i].astype(F32) + other_ref[i].astype(F32)
        outs[0][base + i * height : base + (i + 1) * height] = total.astype(BF16)


def scaled_down_kernel(gain_ref, down_hbm, out_ref, buf, sems):
    per_dev, depth, rank = down_hbm.shape
    copies = [pltpu.make_async_copy(down_hbm.at[a], buf.at[a], sems.at[a]) for a in range(per_dev)]
    for copy in copies:
        copy.start()
    columns = []
    for b in range(depth // HEAD):
        columns.append(to_column(gain_ref[b : b + 1].astype(F32), HEAD))
    for a in range(per_dev):
        copies[a].wait()
        for b in range(depth // HEAD):
            span = slice(b * HEAD, (b + 1) * HEAD)
            out_ref[span, a * rank : (a + 1) * rank] = (
                buf[a, span].astype(F32) * columns[b]
            ).astype(BF16)


def aux_kernel(n_wide, per_dev, req_hbm, table_hbm, tok_hbm, sq_ref, *refs):
    sels = refs[:n_wide]
    req_ref, table_ref, tok_ref, sems = refs[n_wide:]
    copies = [
        pltpu.make_async_copy(req_hbm, req_ref, sems.at[0]),
        pltpu.make_async_copy(table_hbm, table_ref, sems.at[1]),
        pltpu.make_async_copy(tok_hbm, tok_ref, sems.at[2]),
    ]
    for copy in copies:
        copy.start()
    for copy in copies:
        copy.wait()
    rows = tok_ref.shape[0]
    place, _ = places(req_ref[...], table_ref, n_wide, per_dev)
    place = place.astype(F32)
    for k in range(n_wide):
        column = to_column(place[k : k + 1], rows).astype(jnp.int32)
        sels[k][...] = (iota((rows, HEAD), 1) == column).astype(BF16)
    tok = tok_ref[...]
    gram = lax.dot_general(tok, tok, (((1,), (1,)), ((), ())), preferred_element_type=F32)
    diag = iota((rows, rows), 0) == iota((rows, rows), 1)
    sq = jnp.sum(jnp.where(diag, gram, 0.0), axis=0, keepdims=True)
    block = jnp.zeros((8, HEAD), F32)
    for p in range(3):
        part = sq.astype(BF16).astype(F32)
        sq = sq - part
        for i in range(rows // HEAD):
            term = part[:, i * HEAD : (i + 1) * HEAD]
            block = jnp.where(iota((8, HEAD), 0) == p * (rows // HEAD) + i, term, block)
    sq_ref[...] = block


def slot_column(x_ref, cap):
    height = x_ref.shape[0]
    base = cap // 16 * 16
    row = x_ref[base : base + 16, :HEAD].astype(F32)[cap - base : cap - base + 1]
    column = to_column(row, height)
    return jnp.where(iota((height, 1), 0) < cap, column, -1.0)


def down_kernel(count, cap, with_sq, *refs):
    xs, down_ref = refs[:count], refs[count]
    sq_ref = refs[count + 1] if with_sq else None
    out_ref = refs[-1]
    height, depth = xs[0].shape
    rank = HEAD
    x = jnp.concatenate([x[...] for x in xs], axis=0) if count > 1 else xs[0][...]
    slot = [slot_column(x, cap) for x in xs]
    slot = jnp.concatenate(slot, axis=0) if count > 1 else slot[0]
    low = jnp.zeros((count * height, rank), F32)
    for g in range(down_ref.shape[1] // (2 * rank)):
        y = jnp.dot(
            x, down_ref[:, 2 * g * rank : 2 * (g + 1) * rank], preferred_element_type=F32
        )
        low = jnp.where(slot == 2 * g, y[:, :rank], low)
        low = jnp.where(slot == 2 * g + 1, y[:, rank:], low)
    for j in range(count):
        part = low[j * height : (j + 1) * height]
        if j == 0 and with_sq:
            tail = [jnp.zeros((cap, rank), F32), sq_ref[...]]
            if height > cap + 8:
                tail.append(jnp.zeros((height - cap - 8, rank), F32))
            part = part + jnp.concatenate(tail, axis=0)
        out_ref[j] = part.astype(BF16)


def low_term(ref, i, groups, height):
    if len(ref.shape) == 3:
        return ref[i].astype(F32)
    start = ref.shape[0] - (groups - i) * height
    return ref[start : start + height].astype(F32)


def low_sum_kernel(left_ref, right_ref, out_ref):
    groups, height, _ = out_ref.shape
    for i in range(groups):
        left = low_term(left_ref, i, groups, height)
        out_ref[i] = (left + low_term(right_ref, i, groups, height)).astype(BF16)


def head_is_key(heads, h):
    if heads % 2 == 0:
        return h % 2 == 0
    return (lax.axis_index("tensor").astype(jnp.int32) * heads + h) % 2 == 0


def up_kernel(count, n_parts, cap, with_sq, *refs):
    xs = refs[:count]
    parts = refs[count : count + n_parts]
    up_ref = refs[count + n_parts]
    outs = refs[count + n_parts + 1 :]
    per_dev, half, cols = up_ref.shape
    heads = cols // HEAD
    height, rank = outs[0].shape[0], 2 * half
    up = up_ref[...].reshape(per_dev * half, cols)
    sums = []
    for j in range(count):
        terms = [low_term(part, j, count, height) for part in parts]
        sums.append(sum(terms[1:], terms[0]))
    if with_sq:
        outs[count][...] = sums[0][cap : cap + 8]
    low = jnp.concatenate(sums, axis=0) if count > 1 else sums[0]
    slot = [slot_column(x, cap) for x in xs]
    slot = jnp.concatenate(slot, axis=0) if count > 1 else slot[0]
    left = iota((count * height, rank), 1) < half
    turned = pltpu.roll(low, half, 1)
    wide = []
    for source in (jnp.where(left, low, turned), jnp.where(left, turned, low)):
        pieces = []
        for g in range(per_dev // 2):
            mine = slot == jnp.where(left, 2.0 * g, 2.0 * g + 1)
            pieces.append(jnp.where(mine, source, 0.0).astype(BF16))
        wide.append(jnp.concatenate(pieces, axis=1))
    for h in range(heads):
        key = head_is_key(heads, h)
        if isinstance(key, bool):
            lhs = wide[0] if key else wide[1]
        else:
            lhs = jnp.where(key, wide[0].astype(F32), wide[1].astype(F32)).astype(BF16)
        span = slice(h * HEAD, (h + 1) * HEAD)
        y = jnp.dot(lhs, up[:, span], preferred_element_type=F32).astype(BF16)
        for j in range(count):
            outs[j][:, span] = y[j * height : (j + 1) * height]


def placed(sels, deltas):
    height, cols = deltas[0].shape
    blocks = []
    for delta in deltas:
        blocks.append(delta[...])
        if height < HEAD:
            blocks.append(jnp.zeros((HEAD - height, cols), BF16))
    lhs = jnp.concatenate([sel[...] for sel in sels], axis=1) if len(sels) > 1 else sels[0][...]
    return jnp.dot(lhs, jnp.concatenate(blocks, axis=0), preferred_element_type=F32)


def gather_kernel(n_pairs, count, half, sq_ref, base_ref, *refs):
    tops, bottoms = refs[:n_pairs], refs[n_pairs : 2 * n_pairs]
    deltas = refs[2 * n_pairs : 2 * n_pairs + count]
    sels = refs[2 * n_pairs + count : 2 * n_pairs + 2 * count]
    out_ref, scale_ref = refs[-2:]
    rows, cols = out_ref.shape
    pieces = rows // HEAD
    squares = []
    for i in range(pieces):
        total = sq_ref[i : i + 1]
        for p in range(1, 3):
            total = total + sq_ref[p * pieces + i : p * pieces + i + 1]
        squares.append(total)
    square = to_column(jnp.concatenate(squares, axis=1), rows)
    scale = lax.rsqrt(square * (1.0 / MODEL_WIDTH) + EPSILON)
    scale_ref[...] = jnp.broadcast_to(scale, (rows, HEAD))
    total = base_ref[...] + placed(sels, deltas)
    lower = total[half:]
    for bottom in bottoms:
        lower = lower + bottom[...].astype(F32)
    out_ref[half:] = lower
    for h in range(cols // HEAD):
        span = slice(h * HEAD, (h + 1) * HEAD)
        upper = total[:half, span]
        for top in tops:
            upper = upper + top[h * half : (h + 1) * half].astype(F32)
        out_ref[:half, span] = upper


def finish_kernel(count, sum_ref, near_ref, scale_ref, cos_ref, sin_ref, *refs):
    deltas, sels, out_ref = refs[:count], refs[count : 2 * count], refs[2 * count]
    rows, cols = out_ref.shape
    total = sum_ref[...] + near_ref[...].astype(F32) + placed(sels, deltas)
    heads = cols // HEAD
    scale = scale_ref[...]
    for h in range(heads):
        span = slice(h * HEAD, (h + 1) * HEAD)
        x = total[:, span] * scale
        key = head_is_key(heads, h)
        if key is False:
            out_ref[:, span] = x.astype(BF16)
            continue
        y = x * cos_ref[...] + pltpu.roll(x, HEAD // 2, 1) * sin_ref[...]
        if key is not True:
            y = jnp.where(key, y, x)
        out_ref[:, span] = y.astype(BF16)


def local(
    mesh_shape,
    tokens,
    attention_norm_gain,
    key_value_weight,
    adapter_down_weight,
    adapter_up_weight,
    request_adapter,
    adapter_storage_row,
    cached_token_length,
):
    n_wide, n_tensor = mesh_shape["wide"], mesh_shape["tensor"]
    rows, depth = tokens.shape
    per_dev, _, rank = adapter_down_weight.shape
    cols = adapter_up_weight.shape[2]
    cap = 104 if n_wide <= 4 else 64
    height = -(-(cap + 8) // 16) * 16
    req = request_adapter.reshape(1, rows)
    gain = attention_norm_gain.reshape(depth // HEAD, HEAD)

    def over(axis, array, k):
        size = mesh_shape[axis]
        return lax.ppermute(array, axis, [(i, i ^ k) for i in range(size)])

    small = [pltpu.VMEM((1, rows), jnp.int32), pltpu.SMEM(adapter_storage_row.shape, jnp.int32)]
    first, last = [0, 1], list(range(2, n_wide))

    order = list(range(n_wide - 1, -1, -1))
    *blocks, xg = call(
        functools.partial(dispatch_kernel, order, n_wide, per_dev, cap),
        "dispatch",
        [shape((height, depth), BF16)] * n_wide + [shape((rows, depth), BF16)],
        hbm=(req, adapter_storage_row, tokens, gain),
        hbm_outs=n_wide + 1,
        scratch=small
        + [
            pltpu.VMEM((rows, depth), BF16),
            pltpu.VMEM(gain.shape, BF16),
            pltpu.VMEM((n_wide, height, depth), BF16),
            pltpu.VMEM((rows, depth), BF16),
            pltpu.SemaphoreType.DMA((7,)),
            pltpu.SemaphoreType.DMA((n_wide + 1,)),
        ],
        flops=2 * n_wide * height * rows * depth,
        moved=2 * rows * depth * 4,
        limit=63,
    )
    held = [blocks[n_wide - 1 - k] for k in range(n_wide)]
    held[1:] = [over("wide", held[k], k) for k in range(1, n_wide)]

    twos = list(range(2, n_tensor, 2))
    far = [k ^ 1 for k in twos]
    offsets = far + [1] + twos + [0]
    chunk = math.gcd(depth, 256)
    steps = depth // chunk
    sums = call(
        functools.partial(base_kernel, offsets, cols),
        "base",
        [shape((rows, cols), BF16)] * (len(far) + 1) + [shape((rows, cols), F32)] * (len(twos) + 1),
        hbm=(xg, key_value_weight),
        scratch=[
            pltpu.VMEM((rows, depth), BF16),
            pltpu.VMEM((steps, chunk, key_value_weight.shape[1]), BF16),
            pltpu.VMEM((len(offsets), rows, cols), F32),
            pltpu.SemaphoreType.DMA((1 + steps,)),
        ],
        flops=2 * rows * depth * cols * n_tensor,
        moved=2 * depth * cols * n_tensor,
        limit=52,
    )
    away, near, own, base = sums[: len(far)], sums[len(far)], sums[len(far) + 1 : -1], sums[-1]
    beside = [over("tensor", p, 1) for p in away]
    (down,) = call(
        scaled_down_kernel,
        "scaled_down",
        [shape((depth, per_dev * rank), BF16)],
        vmem=(gain,),
        hbm=(adapter_down_weight,),
        after=(base,),
        scratch=[
            pltpu.VMEM((per_dev, depth, rank), BF16),
            pltpu.SemaphoreType.DMA((per_dev,)),
        ],
        flops=4 * depth * per_dev * rank,
        moved=4 * depth * per_dev * rank,
    )
    half_size = HEAD // 2
    freq_index = jnp.arange(half_size).astype(F32)
    inverse = jnp.exp(freq_index * (-2.0 / HEAD) * math.log(ROPE_BASE))
    angles = cached_token_length.astype(F32)[:, None] * inverse[None, :]
    cosine, sine = jnp.cos(angles), jnp.sin(angles)
    cosine = jnp.concatenate([cosine, cosine], axis=1)
    sine = jnp.concatenate([-sine, sine], axis=1)

    def down_block(group, extra, after):
        xs = [held[k] for k in group]
        (low,) = call(
            functools.partial(down_kernel, len(xs), cap, bool(extra)),
            "down_block",
            [shape((len(xs), height, rank), BF16)],
            vmem=(*xs, down, *extra),
            after=after,
            flops=2 * len(xs) * height * depth * rank * per_dev,
            moved=2 * per_dev * depth * rank,
        )
        return low

    def up_block(group, parts, with_sq, after):
        xs = [held[k] for k in group]
        outs = [shape((height, cols), BF16)] * len(xs)
        if with_sq:
            outs = outs + [shape((8, HEAD), F32)]
        return call(
            functools.partial(up_kernel, len(xs), len(parts), cap, with_sq),
            "up_block",
            outs,
            vmem=(*xs, *parts, adapter_up_weight),
            after=after,
            flops=2 * len(xs) * height * per_dev * rank * cols,
            moved=2 * per_dev * rank * cols,
        )

    low = down_block(first, (), ())
    sq, *sels = call(
        functools.partial(aux_kernel, n_wide, per_dev),
        "aux",
        [shape((8, HEAD), F32)]
        + [shape((rows, HEAD), BF16)] * n_wide,
        hbm=(req, adapter_storage_row, tokens),
        after=(low,),
        scratch=small + [pltpu.VMEM((rows, depth), BF16), pltpu.SemaphoreType.DMA((3,))],
        flops=2 * rows * rows * depth,
        moved=2 * rows * depth,
    )
    half = rows * 3 // 128 * 16
    upper = cols // HEAD * half
    other = over("tensor", low, 1)
    pairs = call(
        functools.partial(pair_low_kernel, len(twos), half),
        "pair_low_sums",
        [shape((upper + len(first) * height, HEAD), BF16)]
        + [shape((upper, HEAD), BF16)] * (len(twos) - 1),
        vmem=(low, other, *own, *beside),
        after=(sq,),
    )
    tops = [over("tensor", p, k) for p, k in zip(pairs, twos)]
    done = pairs[0]
    low, other = pairs[0], tops[0]
    for step in range(2, n_tensor.bit_length() - 1):
        (low,) = call(
            low_sum_kernel,
            "low_sum",
            [shape((len(first), height, rank), BF16)],
            vmem=(low, other),
        )
        other = over("tensor", low, 2**step)
    low_last = down_block(last, (sq,), (done,))
    last_parts = [low_last] + [over("tensor", low_last, k) for k in range(n_tensor - 1, 0, -1)]
    ups = up_block(first, [low, other], False, (low_last,))
    deltas = [u if k == 0 else over("wide", u, k) for k, u in zip(first, ups)]
    *pairs, near = call(
        functools.partial(pair_kernel, len(twos), half),
        "pair_sums",
        [shape((rows - half, cols), BF16)] * len(twos) + [shape((rows, cols), BF16)],
        vmem=(near, *own, *beside),
        after=(ups[0],),
    )
    near = over("tensor", near, 1)
    bottoms = [over("tensor", p, k) for p, k in zip(pairs, twos)]
    *ups, square = up_block(last, last_parts, True, (pairs[0],))
    last_deltas = [over("wide", u, k) for k, u in zip(last, ups)]
    total, scale = call(
        functools.partial(gather_kernel, len(tops), len(first), half),
        "gather",
        [shape((rows, cols), F32), shape((rows, HEAD), F32)],
        vmem=(square, base, *tops, *bottoms, *deltas, *[sels[k] for k in first]),
        after=(ups[0],),
        flops=2 * rows * cols * HEAD * len(first),
    )
    return call(
        functools.partial(finish_kernel, len(last)),
        "finish",
        [shape((rows, cols), BF16)],
        vmem=(total, near, scale, cosine, sine, *last_deltas, *[sels[k] for k in last]),
        flops=2 * rows * cols * HEAD,
    )[0]


def solution(mesh):
    return jax.shard_map(
        functools.partial(local, dict(mesh.shape)),
        mesh=mesh,
        in_specs=(
            P(("parts", "wide"), "tensor"),
            P("tensor"),
            P("tensor", None),
            P(("parts", "wide"), "tensor", None),
            P(("parts", "wide"), None, "tensor"),
            P(("parts", "wide")),
            P("parts"),
            P(("parts", "wide")),
        ),
        out_specs=P(("parts", "wide"), "tensor"),
        check_vma=False,
    )
```
